32 devices in a mesh: arc: 8 (over z, x), coef: 4 (over y, core).
Axes of the slice: x: 2, y: 2, z: 4, core: 2. Of those that a mesh axis runs over, the one named last changes fastest.
Arguments:
- local_design: bfloat16 [32, 256, 512], P(('arc', 'coef')), may hold values from -0.25 to 0.25
- global_design: bfloat16 [32, 2304, 512], P(('arc', 'coef')), may hold values from -0.046875 to 0.046875
- local_prior: float32 [32, 256], P(('arc', 'coef')), may hold values from 0.2 to 2
- obs_count: int32 [32], P(('arc', 'coef')), may hold values from 128 to 512, as said below
- band_mask: int32 [32, 4], P(('arc', 'coef')), may hold values 0 or 1
- owner_columns: int32 [2048], replicated, may hold values from 0 to 2047, each once
- kaula_prior: float32 [4, 128], P('coef'), may hold values from 0.05 to 0.5
Outputs:
- normal_rows: float32 [4, 512, 768], P('coef', 'arc')
- panel_factor: float32 [4, 128, 128], P('coef')
The draws below stay inside these ranges and needn't reach their ends.
Inputs may be any that keep to these rules, and one draw needn't show every extreme that they name: Arc a uses its first obs_count[a] rows; some arc uses all 512. `owner_columns`: each coefficient index appears once.
All inputs are finite; a program needn't handle non-finite values. No bound on the sum of `band_mask` on one device may be relied on, other than what follows from the above.
Results may differ from the reference program's by a relative error of at most 0.0006.
Values may be sent and summed in bfloat16 or wider, within the bound.
No kernel may reach another device: no remote copies, remote signals or barrier semaphores. Data moves between devices by JAX's collectives and lax.ppermute only.
A program may use at most 128 MiB of HBM per device.

```python
import math
import jax
import jax.numpy as jnp
from jax import lax

L = 256
OB = 512
KB = 256
P_SIZE = 128
M = 512
ARCS = 32
GO = 2048
G = 2304
N_COEF = 4


def draw_obs_count(key, part):
    counts = jax.random.randint(key, (ARCS,), M // 4, M + 1)
    filled = jax.random.randint(jax.random.fold_in(key, 7), (), 0, ARCS)
    return jnp.where(jnp.arange(ARCS) == filled, M, counts).astype(jnp.int32)


def with_ends(values, rng, low, largest):
    longest = values.shape.index(max(values.shape))
    spots = []
    for shift in (0, 1):
        where = [jax.random.randint(jax.random.fold_in(rng, axis), (), 0, length) for axis, length in enumerate(values.shape)]
        where[longest] = (where[longest] + shift) % values.shape[longest]
        spots.append(tuple(where))
    return values.at[spots[0]].set(low).at[spots[1]].set(largest)


def levels(own_key, extent, pieces, low, high):
    level, own = 1.0, jax.random.fold_in(own_key, 6)
    for axis_at, shards_of in pieces:
        steps = jnp.exp(jax.random.uniform(jax.random.fold_in(own, axis_at), (shards_of,), jnp.float32, low / len(pieces), high / len(pieces)))
        level = level * jnp.repeat(steps, extent[axis_at] // shards_of).reshape([-1 if axis == axis_at else 1 for axis in range(len(extent))])
    return level


def normal_values(rng, shape, spread, bound, split=(), held_as=jnp.bfloat16):
    values = jax.random.normal(rng, shape, jnp.float32) * spread
    if len(split) > 0:
        values = levels(rng, shape, split, -0.22, 0.18) * values
    return jnp.clip(values, min=-bound, max=bound).astype(held_as)


def setup_inputs(seed: int = 0) -> dict:
    keys = jax.random.split(jax.random.key(seed), 8)
    return {
        "local_design": normal_values(keys[0], (ARCS, L, M), M ** -0.5, 0.25, ((0, 32),)),
        "global_design": normal_values(keys[1], (ARCS, G, M), (ARCS * M) ** -0.5, 0.046875, ((0, 32),)),
        "local_prior": jnp.clip(jnp.exp(math.log(2.0) - 2.3025851 * jax.random.uniform(keys[2], (ARCS, L), jnp.float32) ** levels(keys[2], (ARCS, L), ((0, 32),), -0.2, 0.2)), 0.2, 2.0),
        "obs_count": draw_obs_count(jax.random.fold_in(keys[7], 71), 0),
        "band_mask": with_ends((jax.random.randint(keys[4], (ARCS, N_COEF), 0, 4) < 3).astype(jnp.int32), jax.random.fold_in(keys[4], 1), 0, 1),
        "owner_columns": jax.random.permutation(keys[5], GO).astype(jnp.int32),
        "kaula_prior": jnp.clip(jnp.exp(math.log(0.5) - 2.3025851 * jax.random.uniform(keys[6], (N_COEF, P_SIZE), jnp.float32) ** levels(keys[6], (N_COEF, P_SIZE), ((0, 4),), -0.2, 0.2)), 0.05, 0.5),
    }


def reduce_one(local_one, global_one, prior_one, count_one, sense_one):
    row_total = local_one.shape[1]
    row_valid = (lax.iota(jnp.int32, row_total) < count_one).astype(jnp.bfloat16)
    band_cols = jnp.repeat(sense_one, OB)
    column_valid = jnp.concatenate([band_cols, jnp.ones((KB,), jnp.int32)]).astype(jnp.bfloat16)
    local_rows = local_one * row_valid[None, :]
    global_rows = global_one * row_valid[None, :] * column_valid[:, None]
    inner = (((1,), (1,)), ((), ()))
    local_normal = lax.dot_general(local_rows.astype(jnp.float32), local_rows.astype(jnp.float32), inner, preferred_element_type=jnp.float32) + jnp.diag(prior_one)
    coupling = lax.dot_general(local_rows.astype(jnp.float32), global_rows.astype(jnp.float32), inner, preferred_element_type=jnp.float32)
    factor = jnp.linalg.cholesky(local_normal)
    solved = jax.scipy.linalg.cho_solve((factor, True), coupling).astype(jnp.bfloat16)
    removed = lax.dot_general(solved.astype(jnp.float32), local_rows.astype(jnp.float32), (((0,), (0,)), ((), ())), preferred_element_type=jnp.float32)
    return (global_rows.astype(jnp.float32) - removed).astype(jnp.bfloat16)

def reference(local_design, global_design, local_prior, obs_count, band_mask, owner_columns, kaula_prior):
    owner_map = owner_columns.reshape(N_COEF, OB).astype(jnp.int32)

    def add_arc(totals, inputs):
        local_one, global_one, prior_one, count_one, sense_one = inputs
        reduced = reduce_one(local_one, global_one, prior_one, count_one, sense_one)
        owned_rows = jnp.take(reduced, owner_map, axis=0)
        border = reduced[GO:]
        partner = jnp.concatenate([owned_rows, jnp.broadcast_to(border[None], (N_COEF, KB, border.shape[1]))], axis=1)
        product = jnp.einsum('cim,ckm->cik', owned_rows.astype(jnp.float32), partner.astype(jnp.float32), precision=lax.Precision.HIGHEST)
        return (totals + product, None)
    start_sum = jnp.zeros((N_COEF, OB, OB + KB), jnp.float32)
    normal_rows, _ = lax.scan(add_arc, start_sum, (local_design, global_design, local_prior, obs_count, band_mask))
    stride = OB // P_SIZE
    panel = normal_rows[:, ::stride, :OB:stride] + jax.vmap(jnp.diag)(kaula_prior)
    return (normal_rows, jax.vmap(jnp.linalg.cholesky)(panel))
```

```python
import functools

import jax
import jax.numpy as jnp
from jax import lax
from jax.experimental import pallas as pl
from jax.experimental.pallas import tpu as pltpu
from jax.sharding import PartitionSpec as P

OB = 512
KB = 256
P_SIZE = 128
STRIDE = OB // P_SIZE
WIDTH = OB + KB
HALF = WIDTH // 2
PAIR = 2
F16_TOP = 8192.0
INNER = (((1,), (1,)), ((), ()))
AXES = ("arc", "coef")


def reduce_one(local_one, global_one, prior_one, count_one, sense_one):
    row_total = local_one.shape[1]
    row_valid = (lax.iota(jnp.int32, row_total) < count_one).astype(jnp.bfloat16)
    band_cols = jnp.repeat(sense_one, OB)
    column_valid = jnp.concatenate([band_cols, jnp.ones((KB,), jnp.int32)]).astype(jnp.bfloat16)
    local_rows = local_one * row_valid[None, :]
    global_rows = global_one * row_valid[None, :] * column_valid[:, None]
    local_normal = lax.dot_general(
        local_rows, local_rows, INNER, preferred_element_type=jnp.float32
    ) + jnp.diag(prior_one)
    coupling = lax.dot_general(local_rows, global_rows, INNER, preferred_element_type=jnp.float32)
    factor = jnp.linalg.cholesky(local_normal)
    solved = jax.scipy.linalg.cho_solve((factor, True), coupling).astype(jnp.bfloat16)
    removed = lax.dot_general(
        solved, local_rows, (((0,), (0,)), ((), ())), preferred_element_type=jnp.float32
    )
    return (global_rows.astype(jnp.float32) - removed).astype(jnp.bfloat16)


def dot(a, b):
    return lax.dot_general(a, b, INNER, preferred_element_type=jnp.float32)


def product_kernel(n_y, n_z, place_ref, mine_ref, other_ref, prod_ref, panel_ref, left, top):
    z, x = place_ref[0], place_ref[1]
    blocks = n_z * PAIR
    rows = OB // blocks
    border_mine = mine_ref[pl.ds(2 * n_y * OB, KB), :]
    border_other = other_ref[pl.ds(n_y * OB, KB), :]
    pick = lax.broadcasted_iota(jnp.int32, (P_SIZE, OB), 1) == STRIDE * lax.broadcasted_iota(
        jnp.int32, (P_SIZE, OB), 0
    )
    pick = pick.astype(jnp.float32).astype(jnp.bfloat16)
    for y in range(n_y):
        own_mine = mine_ref[pl.ds(y * OB, OB), :]
        own_other = other_ref[pl.ds(y * OB, OB), :]
        for i in range(PAIR):
            for j in range(n_z):
                at = (i * n_z + j) * rows
                source = pl.multiple_of(y * OB + ((z ^ j) * PAIR + (x ^ i)) * rows, rows)
                left[0, pl.ds(at, rows), :] = mine_ref[pl.ds(source, rows), :]
                left[1, pl.ds(at, rows), :] = other_ref[pl.ds(source, rows), :]
        square = dot(left[0], own_mine) + dot(left[1], own_other)
        side = dot(left[0], border_mine) + dot(left[1], border_other)
        prod_ref[y, :, :OB] = square
        prod_ref[y, :, OB:] = side
        largest = jnp.maximum(
            jnp.max(jnp.abs(square), axis=0, keepdims=True).max(axis=1, keepdims=True),
            jnp.max(jnp.abs(side), axis=0, keepdims=True).max(axis=1, keepdims=True),
        )
        largest = jnp.broadcast_to(largest, top.shape)
        top[...] = largest if y == 0 else jnp.maximum(top[...], largest)
        strip_mine = lax.dot_general(
            pick, own_mine, (((1,), (0,)), ((), ())), preferred_element_type=jnp.float32
        ).astype(jnp.bfloat16)
        strip_other = lax.dot_general(
            pick, own_other, (((1,), (0,)), ((), ())), preferred_element_type=jnp.float32
        ).astype(jnp.bfloat16)
        panel_ref[y, :P_SIZE, :] = dot(strip_mine, strip_mine) + dot(strip_other, strip_other)
    for y in range(n_y):
        panel_ref[y, P_SIZE:, :] = top[...]


def products(mine, other, place, n_y, n_z):
    return pl.pallas_call(
        functools.partial(product_kernel, n_y, n_z),
        out_shape=(
            jax.ShapeDtypeStruct((n_y, OB, WIDTH), jnp.float32),
            jax.ShapeDtypeStruct((n_y, P_SIZE + 8, P_SIZE), jnp.float32),
        ),
        in_specs=[
            pl.BlockSpec(memory_space=pltpu.SMEM),
            pl.BlockSpec(memory_space=pltpu.VMEM),
            pl.BlockSpec(memory_space=pltpu.VMEM),
        ],
        out_specs=(
            pl.BlockSpec(memory_space=pltpu.VMEM),
            pl.BlockSpec(memory_space=pltpu.VMEM),
        ),
        scratch_shapes=[
            pltpu.VMEM((2, OB, mine.shape[1]), jnp.bfloat16),
            pltpu.VMEM((8, P_SIZE), jnp.float32),
        ],
        compiler_params=pltpu.CompilerParams(vmem_limit_bytes=48 * 1024 * 1024),
        name="products",
    )(place, mine, other)


def encode(values, bound):
    return (values * (F16_TOP / jnp.maximum(bound, 1e-30))).astype(jnp.float16)


def decode(values, bound):
    return values.astype(jnp.float32) * (bound * (1.0 / F16_TOP))


def per_device(
    local_design, global_design, local_prior, obs_count, band_mask, owner_columns, kaula_prior
):
    n_arc, n_coef = lax.axis_size("arc"), lax.axis_size("coef")
    n_z, n_y = n_arc // PAIR, n_coef // PAIR
    rows = OB // n_arc
    arc, coef = lax.axis_index("arc"), lax.axis_index("coef")
    z, x, y, core = arc // PAIR, arc % PAIR, coef // PAIR, coef % PAIR

    def swap(values, dz=0, dx=0, dy=0, dk=0):
        pairs = []
        for a in range(n_arc):
            for c in range(n_coef):
                to_a = ((a // PAIR) ^ dz) * PAIR + ((a % PAIR) ^ dx)
                to_c = ((c // PAIR) ^ dy) * PAIR + ((c % PAIR) ^ dk)
                pairs.append((a * n_coef + c, to_a * n_coef + to_c))
        return lax.ppermute(values, AXES, pairs)

    reduced = reduce_one(
        local_design[0], global_design[0], local_prior[0], obs_count[0], band_mask[0]
    )
    owners = owner_columns.reshape(n_y, PAIR, OB)
    owners = jnp.take(owners, y ^ jnp.arange(n_y), axis=0, mode="clip")
    owners = jnp.take(owners, core ^ jnp.arange(PAIR), axis=1, mode="clip")
    owners = owners.transpose(1, 0, 2).reshape(-1)
    ordered = reduced.at[owners].get(mode="promise_in_bounds")
    mine = jnp.concatenate([ordered, reduced[n_coef * OB :]], axis=0)
    other = swap(mine[n_y * OB :], dk=1)
    product, panels = products(mine, other, jnp.stack([z, x]), n_y, n_z)

    product = product.reshape(n_y, PAIR, n_z, rows, WIDTH)
    first, second = product[..., :HALF], product[..., HALF:]
    own_top = panels[0, P_SIZE, 0]

    over_y = [None] + [swap(encode(first[j], own_top), dy=j) for j in range(1, n_y)]
    over_x = swap(encode(second[:, 1], own_top), dx=1)
    panel_y = [panels[0]] + [swap(panels[j], dy=j) for j in range(1, n_y)]
    panel_x = [swap(panels[j], dx=1, dy=j) for j in range(n_y)]

    tops_y = [p[P_SIZE, 0] for p in panel_y]
    tops_x = [p[P_SIZE, 0] for p in panel_x]
    first_sum = first[0]
    for j in range(1, n_y):
        first_sum = first_sum + decode(over_y[j], tops_y[j])
    second_sum = second[:, 0] + decode(over_x, tops_x[0])
    panel_sum = functools.reduce(jnp.add, panel_y) + functools.reduce(jnp.add, panel_x)

    first_bound, first_from = sum(tops_y), sum(tops_x)
    over_x = swap(encode(first_sum[1], first_bound), dx=1)
    over_y = [None] + [
        swap(encode(second_sum[j], tops_y[0] + tops_x[0]), dy=j) for j in range(1, n_y)
    ]
    panel_z = [panel_sum] + [swap(panel_sum, dz=j) for j in range(1, n_z)]
    first_sum = first_sum[0] + decode(over_x, first_from)
    second_total = second_sum[0]
    for j in range(1, n_y):
        second_total = second_total + decode(over_y[j], tops_y[j] + tops_x[j])

    total = jnp.concatenate([first_sum, second_total], axis=-1)
    tops_z = [p[P_SIZE, 0] for p in panel_z]
    over_z = [swap(encode(total[j], tops_z[0]), dz=j) for j in range(1, n_z)]
    while len(panel_z) > 1:
        panel_z = [panel_z[2 * i] + panel_z[2 * i + 1] for i in range(len(panel_z) // 2)]
    panel_factor = jnp.linalg.cholesky(panel_z[0][:P_SIZE] + jnp.diag(kaula_prior[0]))
    normal_rows = total[0]
    for j in range(1, n_z):
        normal_rows = normal_rows + decode(over_z[j - 1], tops_z[j])
    return normal_rows[None], panel_factor[None]


def solution(mesh):
    in_specs = (
        P(AXES, None, None),
        P(AXES, None, None),
        P(AXES, None),
        P(AXES),
        P(AXES, None),
        P(),
        P("coef", None),
    )
    out_specs = (P("coef", "arc", None), P("coef", None, None))
    return jax.shard_map(
        per_device, mesh=mesh, in_specs=in_specs, out_specs=out_specs, check_vma=False
    )
```

```python
import functools

import jax
import jax.numpy as jnp
from jax import lax
from jax.experimental import pallas as pl
from jax.experimental.pallas import tpu as pltpu
from jax.sharding import PartitionSpec as P

OB = 512
KB = 256
P_SIZE = 128
STRIDE = OB // P_SIZE
WIDTH = OB + KB
HALF = WIDTH // 2
PAIR = 2
F16_TOP = 8192.0
INNER = (((1,), (1,)), ((), ()))
AXES = ("arc", "coef")

LANES = 128
BLOCK = 8
GROUP = 4
ROWS = (((1,), (0,)), ((), ()))
COLS = (((0,), (0,)), ((), ()))


def mm(a, b, dims=ROWS):
    return lax.dot_general(a, b, dims, preferred_element_type=jnp.float32)


def split3(value):
    high = value.astype(jnp.bfloat16)
    rest = value - high.astype(jnp.float32)
    middle = rest.astype(jnp.bfloat16)
    low = (rest - middle.astype(jnp.float32)).astype(jnp.bfloat16)
    return high, middle, low


def product_six(a, b):
    a0, a1, a2 = split3(a)
    b0, b1, b2 = split3(b)
    return (mm(a0, b2) + mm(a1, b1) + mm(a2, b0)) + (mm(a0, b1) + mm(a1, b0)) + mm(a0, b0)


def product_three(a, b):
    a0, a1, _ = split3(a)
    b0, b1, _ = split3(b)
    return (mm(a0, b1) + mm(a1, b0)) + mm(a0, b0)


def row_of(value, i):
    return jnp.broadcast_to(value[i : i + 1, :], (BLOCK, LANES))


def reciprocal(value):
    guess = pl.reciprocal(value, approx=True)
    guess = guess * (2.0 - value * guess)
    return guess * (2.0 - value * guess)


def eliminate_group(rows, base):
    sub = lax.broadcasted_iota(jnp.int32, (BLOCK, LANES), 0)
    lane = lax.broadcasted_iota(jnp.int32, (BLOCK, LANES), 1)
    count = len(rows)
    for q in range(count):
        half, at = divmod(base + BLOCK * q, LANES)
        factors = [
            [
                jnp.broadcast_to(rows[r][half][:, at + j : at + j + 1], (BLOCK, LANES))
                for j in range(BLOCK)
            ]
            for r in range(count)
        ]
        inside = (lane >= at) & (lane < at + BLOCK)
        unit = (lane - at == sub).astype(jnp.float32)
        for r in range(count):
            rows[r][half] = jnp.where(inside, unit if r == q else 0.0, rows[r][half])
        columns, own = list(factors[q]), rows[q]
        for i in range(BLOCK):
            scale = reciprocal(row_of(columns[i], i))
            pivot = sub == i
            for h in range(len(own)):
                scaled = row_of(own[h], i) * scale
                own[h] = jnp.where(pivot, scaled, own[h] - columns[i] * scaled)
            for j in range(i + 1, BLOCK):
                scaled = row_of(columns[j], i) * scale
                columns[j] = jnp.where(pivot, scaled, columns[j] - columns[i] * scaled)
        for r in range(count):
            if r != q:
                for h in range(len(own)):
                    value = rows[r][h]
                    for j in range(BLOCK):
                        value = value - factors[r][j] * row_of(own[h], j)
                    rows[r][h] = value
    return rows


def sweep_group(a_ref, base):
    n = a_ref.shape[0]
    depth = BLOCK * GROUP
    before = a_ref[base : base + depth, :]
    rows = [
        [
            a_ref[base + BLOCK * r : base + BLOCK * (r + 1), LANES * h : LANES * (h + 1)]
            for h in range(n // LANES)
        ]
        for r in range(GROUP)
    ]
    rows = eliminate_group(rows, base)
    after = jnp.concatenate([jnp.concatenate(row, axis=1) for row in rows], axis=0)
    column = lax.broadcasted_iota(jnp.int32, (depth, n), 1)
    row = lax.broadcasted_iota(jnp.int32, (depth, n), 0)
    inside = (column >= base) & (column < base + depth)
    before = jnp.where(inside, jnp.where(column - base == row, -1.0, 0.0), before)
    after = jnp.where(inside, -after, after)
    u0, u1, u2 = split3(before)
    w0, w1, w2 = split3(after)
    update = mm(
        jnp.concatenate([u0, u0, u0, u1, u1, u2], axis=0),
        jnp.concatenate([w0, w1, w2, w0, w1, w0], axis=0),
        COLS,
    )
    row = lax.broadcasted_iota(jnp.int32, (n, n), 0)
    column = lax.broadcasted_iota(jnp.int32, (n, n), 1)
    outside = ((row < base) | (row >= base + depth)) & ((column < base) | (column >= base + depth))
    a_ref[...] = jnp.where(outside, a_ref[...], 0.0) - update


def local_kernel(
    n_y, place_ref, count_ref, band_ref, owner_ref, local_ref, global_ref, prior_ref,
    out_ref, work_ref, normal_ref, rows_ref,
):
    n, m = local_ref.shape
    owned = n_y * PAIR * OB
    y, core, count = place_ref[2], place_ref[3], count_ref[0]
    used = lax.broadcasted_iota(jnp.int32, (n, m), 1) < count
    rows_ref[...] = jnp.where(used, local_ref[...].astype(jnp.float32), 0.0).astype(jnp.bfloat16)
    local_rows = rows_ref[...]
    row = lax.broadcasted_iota(jnp.int32, (n, n), 0)
    column = lax.broadcasted_iota(jnp.int32, (n, n), 1)
    prior = jnp.broadcast_to(prior_ref[...], (n, n))
    normal = mm(local_rows, local_rows, INNER) + jnp.where(row == column, prior, 0.0)
    work_ref[...] = normal
    normal_ref[...] = normal

    lane = lax.broadcasted_iota(jnp.int32, (LANES, LANES), 1)
    used = lax.broadcasted_iota(jnp.int32, (LANES, m), 1) < count

    def gather_rows(t):
        position, part = divmod(t * LANES, OB)
        core_away, y_away = divmod(position, n_y)
        owner = (y ^ y_away) * PAIR + (core ^ core_away)
        wanted = owner_ref[owner, part // LANES : part // LANES + 1, :]
        wanted = jnp.broadcast_to(wanted.astype(jnp.float32), (LANES, LANES)).T.astype(jnp.int32)
        hot = []
        for k in range(owned // LANES):
            sensed = band_ref[0, k * LANES // OB].astype(jnp.float32)
            hot.append(jnp.where(wanted == lane + k * LANES, sensed, 0.0).astype(jnp.bfloat16))
        got = mm(jnp.concatenate(hot, axis=1), global_ref[0:owned, :])
        out_ref[t * LANES : (t + 1) * LANES, :] = jnp.where(used, got, 0.0).astype(jnp.bfloat16)

    steps = n // (BLOCK * GROUP)
    tiles = owned // LANES
    for p in range(steps):
        sweep_group(work_ref, p * BLOCK * GROUP)
        for t in range(p * tiles // steps, (p + 1) * tiles // steps):
            gather_rows(t)
    used = lax.broadcasted_iota(jnp.int32, (KB, m), 1) < count
    border = global_ref[owned:, :].astype(jnp.float32)
    out_ref[owned:, :] = jnp.where(used, border, 0.0).astype(jnp.bfloat16)

    inverse = -work_ref[...]
    local_rows = rows_ref[...]
    i0, i1, i2 = split3(inverse)
    gain = mm(i2, local_rows) + mm(i1, local_rows) + mm(i0, local_rows)
    left = local_rows.astype(jnp.float32) - product_six(normal_ref[...], gain)
    gain = gain + product_three(inverse, left)
    g0, g1, g2 = split3(gain)
    for t in range((owned + KB) // KB):
        tile = out_ref[t * KB : (t + 1) * KB, :]
        solved = (mm(tile, g2, INNER) + mm(tile, g1, INNER) + mm(tile, g0, INNER)).astype(jnp.bfloat16)
        out_ref[t * KB : (t + 1) * KB, :] = (
            tile.astype(jnp.float32) - mm(solved, local_rows)
        ).astype(jnp.bfloat16)


def reduce_rows(place, count, band, owners, local_rows, global_rows, prior, n_y):
    n, m = local_rows.shape
    scalar = pl.BlockSpec(memory_space=pltpu.SMEM)
    array = pl.BlockSpec(memory_space=pltpu.VMEM)
    return pl.pallas_call(
        functools.partial(local_kernel, n_y),
        out_shape=jax.ShapeDtypeStruct(global_rows.shape, jnp.bfloat16),
        in_specs=[scalar, scalar, scalar, array, array, array, array],
        out_specs=array,
        scratch_shapes=[
            pltpu.VMEM((n, n), jnp.float32),
            pltpu.VMEM((n, n), jnp.float32),
            pltpu.VMEM((n, m), jnp.bfloat16),
        ],
        compiler_params=pltpu.CompilerParams(vmem_limit_bytes=48 * 1024 * 1024),
        name="reduce_rows",
    )(place, count, band, owners, local_rows, global_rows, prior)


def dot(a, b):
    return lax.dot_general(a, b, INNER, preferred_element_type=jnp.float32)


def product_kernel(n_y, n_z, place_ref, mine_ref, other_ref, prod_ref, panel_ref, left, top):
    z, x = place_ref[0], place_ref[1]
    blocks = n_z * PAIR
    rows = OB // blocks
    border_mine = mine_ref[pl.ds(2 * n_y * OB, KB), :]
    border_other = other_ref[pl.ds(n_y * OB, KB), :]
    pick = lax.broadcasted_iota(jnp.int32, (P_SIZE, OB), 1) == STRIDE * lax.broadcasted_iota(
        jnp.int32, (P_SIZE, OB), 0
    )
    pick = pick.astype(jnp.float32).astype(jnp.bfloat16)
    for y in range(n_y):
        own_mine = mine_ref[pl.ds(y * OB, OB), :]
        own_other = other_ref[pl.ds(y * OB, OB), :]
        for i in range(PAIR):
            for j in range(n_z):
                at = (i * n_z + j) * rows
                source = pl.multiple_of(y * OB + ((z ^ j) * PAIR + (x ^ i)) * rows, rows)
                left[0, pl.ds(at, rows), :] = mine_ref[pl.ds(source, rows), :]
                left[1, pl.ds(at, rows), :] = other_ref[pl.ds(source, rows), :]
        square = dot(left[0], own_mine) + dot(left[1], own_other)
        side = dot(left[0], border_mine) + dot(left[1], border_other)
        prod_ref[y, :, :OB] = square
        prod_ref[y, :, OB:] = side
        largest = jnp.maximum(
            jnp.max(jnp.abs(square), axis=0, keepdims=True).max(axis=1, keepdims=True),
            jnp.max(jnp.abs(side), axis=0, keepdims=True).max(axis=1, keepdims=True),
        )
        largest = jnp.broadcast_to(largest, top.shape)
        top[...] = largest if y == 0 else jnp.maximum(top[...], largest)
        strip_mine = lax.dot_general(
            pick, own_mine, (((1,), (0,)), ((), ())), preferred_element_type=jnp.float32
        ).astype(jnp.bfloat16)
        strip_other = lax.dot_general(
            pick, own_other, (((1,), (0,)), ((), ())), preferred_element_type=jnp.float32
        ).astype(jnp.bfloat16)
        panel_ref[y, :P_SIZE, :] = dot(strip_mine, strip_mine) + dot(strip_other, strip_other)
    for y in range(n_y):
        panel_ref[y, P_SIZE:, :] = top[...]


def products(mine, other, place, n_y, n_z):
    return pl.pallas_call(
        functools.partial(product_kernel, n_y, n_z),
        out_shape=(
            jax.ShapeDtypeStruct((n_y, OB, WIDTH), jnp.float32),
            jax.ShapeDtypeStruct((n_y, P_SIZE + 8, P_SIZE), jnp.float32),
        ),
        in_specs=[
            pl.BlockSpec(memory_space=pltpu.SMEM),
            pl.BlockSpec(memory_space=pltpu.VMEM),
            pl.BlockSpec(memory_space=pltpu.VMEM),
        ],
        out_specs=(
            pl.BlockSpec(memory_space=pltpu.VMEM),
            pl.BlockSpec(memory_space=pltpu.VMEM),
        ),
        scratch_shapes=[
            pltpu.VMEM((2, OB, mine.shape[1]), jnp.bfloat16),
            pltpu.VMEM((8, P_SIZE), jnp.float32),
        ],
        compiler_params=pltpu.CompilerParams(vmem_limit_bytes=48 * 1024 * 1024),
        name="products",
    )(place, mine, other)


def encode(values, bound):
    return (values * (F16_TOP / jnp.maximum(bound, 1e-30))).astype(jnp.float16)


def decode(values, bound):
    return values.astype(jnp.float32) * (bound * (1.0 / F16_TOP))


def per_device(
    local_design, global_design, local_prior, obs_count, band_mask, owner_columns, kaula_prior
):
    n_arc, n_coef = lax.axis_size("arc"), lax.axis_size("coef")
    n_z, n_y = n_arc // PAIR, n_coef // PAIR
    rows = OB // n_arc
    arc, coef = lax.axis_index("arc"), lax.axis_index("coef")
    z, x, y, core = arc // PAIR, arc % PAIR, coef // PAIR, coef % PAIR

    def swap(values, dz=0, dx=0, dy=0, dk=0):
        pairs = []
        for a in range(n_arc):
            for c in range(n_coef):
                to_a = ((a // PAIR) ^ dz) * PAIR + ((a % PAIR) ^ dx)
                to_c = ((c // PAIR) ^ dy) * PAIR + ((c % PAIR) ^ dk)
                pairs.append((a * n_coef + c, to_a * n_coef + to_c))
        return lax.ppermute(values, AXES, pairs)

    place = jnp.stack([z, x, y, core])
    mine = reduce_rows(
        place,
        obs_count,
        band_mask,
        owner_columns.reshape(n_coef, OB // LANES, LANES),
        local_design[0],
        global_design[0],
        local_prior,
        n_y,
    )
    other = swap(mine[n_y * OB :], dk=1)
    product, panels = products(mine, other, place, n_y, n_z)

    product = product.reshape(n_y, PAIR, n_z, rows, WIDTH)
    first, second = product[..., :HALF], product[..., HALF:]
    own_top = panels[0, P_SIZE, 0]

    over_y = [None] + [swap(encode(first[j], own_top), dy=j) for j in range(1, n_y)]
    over_x = swap(encode(second[:, 1], own_top), dx=1)
    panel_y = [panels[0]] + [swap(panels[j], dy=j) for j in range(1, n_y)]
    panel_x = [swap(panels[j], dx=1, dy=j) for j in range(n_y)]

    tops_y = [p[P_SIZE, 0] for p in panel_y]
    tops_x = [p[P_SIZE, 0] for p in panel_x]
    first_sum = first[0]
    for j in range(1, n_y):
        first_sum = first_sum + decode(over_y[j], tops_y[j])
    second_sum = second[:, 0] + decode(over_x, tops_x[0])
    panel_sum = functools.reduce(jnp.add, panel_y) + functools.reduce(jnp.add, panel_x)

    first_bound, first_from = sum(tops_y), sum(tops_x)
    over_x = swap(encode(first_sum[1], first_bound), dx=1)
    over_y = [None] + [
        swap(encode(second_sum[j], tops_y[0] + tops_x[0]), dy=j) for j in range(1, n_y)
    ]
    panel_z = [panel_sum] + [swap(panel_sum, dz=j) for j in range(1, n_z)]
    first_sum = first_sum[0] + decode(over_x, first_from)
    second_total = second_sum[0]
    for j in range(1, n_y):
        second_total = second_total + decode(over_y[j], tops_y[j] + tops_x[j])

    total = jnp.concatenate([first_sum, second_total], axis=-1)
    tops_z = [p[P_SIZE, 0] for p in panel_z]
    over_z = [swap(encode(total[j], tops_z[0]), dz=j) for j in range(1, n_z)]
    while len(panel_z) > 1:
        panel_z = [panel_z[2 * i] + panel_z[2 * i + 1] for i in range(len(panel_z) // 2)]
    panel_factor = jnp.linalg.cholesky(panel_z[0][:P_SIZE] + jnp.diag(kaula_prior[0]))
    normal_rows = total[0]
    for j in range(1, n_z):
        normal_rows = normal_rows + decode(over_z[j - 1], tops_z[j])
    return normal_rows[None], panel_factor[None]


def solution(mesh):
    in_specs = (
        P(AXES, None, None),
        P(AXES, None, None),
        P(AXES, None),
        P(AXES),
        P(AXES, None),
        P(),
        P("coef", None),
    )
    out_specs = (P("coef", "arc", None), P("coef", None, None))
    return jax.shard_map(
        per_device, mesh=mesh, in_specs=in_specs, out_specs=out_specs, check_vma=False
    )
```

```python
import functools

import jax
import jax.numpy as jnp
from jax import lax
from jax.experimental import pallas as pl
from jax.experimental.pallas import tpu as pltpu
from jax.sharding import PartitionSpec as P

OB = 512
KB = 256
P_SIZE = 128
STRIDE = OB // P_SIZE
WIDTH = OB + KB
HALF = WIDTH // 2
PAIR = 2
TOP_LEVEL = 12.0
HEAD = 16
INNER = (((1,), (1,)), ((), ()))
AXES = ("arc", "coef")

LANES = 128
BLOCK = 8
GROUP = 2
FACTOR_GROUP = 4
FIRST = 4
ROWS = (((1,), (0,)), ((), ()))
COLS = (((0,), (0,)), ((), ()))


def mm(a, b, dims=ROWS):
    return lax.dot_general(a, b, dims, preferred_element_type=jnp.float32)


def split3(value):
    high = value.astype(jnp.bfloat16)
    rest = value - high.astype(jnp.float32)
    middle = rest.astype(jnp.bfloat16)
    low = (rest - middle.astype(jnp.float32)).astype(jnp.bfloat16)
    return high, middle, low


def product_six(a, b):
    a0, a1, a2 = split3(a)
    b0, b1, b2 = split3(b)
    return (mm(a0, b2) + mm(a1, b1) + mm(a2, b0)) + (mm(a0, b1) + mm(a1, b0)) + mm(a0, b0)


def product_three(a, b):
    a0, a1, _ = split3(a)
    b0, b1, _ = split3(b)
    return (mm(a0, b1) + mm(a1, b0)) + mm(a0, b0)


def row_of(value, i):
    return jnp.broadcast_to(value[i : i + 1, :], (BLOCK, LANES))


def eliminate_group(rows, base):
    sub = lax.broadcasted_iota(jnp.int32, (BLOCK, LANES), 0)
    lane = lax.broadcasted_iota(jnp.int32, (BLOCK, LANES), 1)
    count = len(rows)
    for q in range(count):
        half, at = divmod(base + BLOCK * q, LANES)
        factors = [
            [
                jnp.broadcast_to(rows[r][half][:, at + j : at + j + 1], (BLOCK, LANES))
                for j in range(BLOCK)
            ]
            for r in range(count)
        ]
        inside = (lane >= at) & (lane < at + BLOCK)
        unit = (lane - at == sub).astype(jnp.float32)
        for r in range(count):
            rows[r][half] = jnp.where(inside, unit if r == q else 0.0, rows[r][half])
        columns, own = list(factors[q]), rows[q]
        a, b, d = row_of(columns[0], 0), row_of(columns[1], 0), row_of(columns[1], 1)
        for i in range(0, BLOCK, 2):
            scale = pl.reciprocal(a * d - b * b, approx=True)

            def step(value, i=i, a=a, b=b, d=d, scale=scale):
                first, second = row_of(value, i), row_of(value, i + 1)
                upper, lower = d * first - b * second, a * second - b * first
                new = value - (columns[i] * upper + columns[i + 1] * lower) * scale
                kept = jnp.where(sub == i + 1, lower * scale, new)
                return new, jnp.where(sub == i, upper * scale, kept)

            pairs = {j: step(columns[j]) for j in range(i + 2, BLOCK)}
            for h in range(len(own)):
                own[h] = step(own[h])[1]
            if i + 2 < BLOCK:
                one, two = pairs[i + 2][0], pairs[i + 3][0]
                a, b, d = row_of(one, i + 2), row_of(two, i + 2), row_of(two, i + 3)
            for j, pair in pairs.items():
                columns[j] = pair[1]
        for r in range(count):
            if r != q:
                for h in range(len(own)):
                    t = [factors[r][j] * row_of(own[h], j) for j in range(BLOCK)]
                    rows[r][h] = rows[r][h] - (
                        ((t[0] + t[1]) + (t[2] + t[3])) + ((t[4] + t[5]) + (t[6] + t[7]))
                    )
    return rows


def sweep_group(a_ref, base):
    n = a_ref.shape[0]
    depth = BLOCK * GROUP
    before = a_ref[base : base + depth, :]
    rows = [
        [
            a_ref[base + BLOCK * r : base + BLOCK * (r + 1), LANES * h : LANES * (h + 1)]
            for h in range(n // LANES)
        ]
        for r in range(GROUP)
    ]
    rows = eliminate_group(rows, base)
    after = jnp.concatenate([jnp.concatenate(row, axis=1) for row in rows], axis=0)
    column = lax.broadcasted_iota(jnp.int32, (depth, n), 1)
    row = lax.broadcasted_iota(jnp.int32, (depth, n), 0)
    inside = (column >= base) & (column < base + depth)
    before = jnp.where(inside, jnp.where(column - base == row, -1.0, 0.0), before)
    after = jnp.where(inside, -after, after)
    u0, u1, u2 = split3(before)
    w0, w1, w2 = split3(after)
    left = jnp.concatenate([u0, u0, u0, u1, u1, u2], axis=0).T
    right = jnp.concatenate([w0, w1, w2, w0, w1, w0], axis=0)

    def update(low, high):
        row = lax.broadcasted_iota(jnp.int32, (high - low, n), 0) + low
        column = lax.broadcasted_iota(jnp.int32, (high - low, n), 1)
        outside = ((row < base) | (row >= base + depth)) & (
            (column < base) | (column >= base + depth)
        )
        a_ref[low:high, :] = jnp.where(outside, a_ref[low:high, :], 0.0) - mm(left[low:high], right)

    after = base + depth
    for low, high in ((after, after + depth), (0, after), (after + depth, n)):
        if low < min(high, n):
            update(low, min(high, n))


def place_of():
    arc, coef = lax.axis_index("arc"), lax.axis_index("coef")
    return lax.div(arc, PAIR), lax.rem(arc, PAIR), lax.div(coef, PAIR), lax.rem(coef, PAIR)


def solve_rows(tile, gain_ref, local_rows):
    solved = mm(tile, gain_ref[2], INNER) + mm(tile, gain_ref[1], INNER)
    solved = (solved + mm(tile, gain_ref[0], INNER)).astype(jnp.bfloat16)
    return (tile.astype(jnp.float32) - mm(solved, local_rows)).astype(jnp.bfloat16)


def normal_kernel(count_ref, prior_ref, local_ref, rows_ref, normal_ref, work_ref):
    n, m = local_ref.shape
    used = lax.broadcasted_iota(jnp.int32, (n, m), 1) < count_ref[0]
    rows_ref[...] = jnp.where(used, local_ref[...].astype(jnp.float32), 0.0).astype(jnp.bfloat16)
    local_rows = rows_ref[...]
    row = lax.broadcasted_iota(jnp.int32, (n, n), 0)
    column = lax.broadcasted_iota(jnp.int32, (n, n), 1)
    prior = jnp.broadcast_to(prior_ref[...], (n, n))
    normal = mm(local_rows, local_rows, INNER) + jnp.where(row == column, prior, 0.0)
    work_ref[...] = normal
    normal_ref[...] = normal
    for p in range(FIRST):
        sweep_group(work_ref, p * BLOCK * GROUP)


def local_kernel(
    n_y, count_ref, band_ref, owner_ref, rows_ref, normal_ref, begun_ref, global_ref,
    send_ref, own_ref, gain_ref, work_ref,
):
    n, m = rows_ref.shape
    owned = n_y * PAIR * OB
    mine = n_y * OB
    count = count_ref[0]
    _, _, y, core = place_of()
    work_ref[...] = begun_ref[...]
    lane = lax.broadcasted_iota(jnp.int32, (LANES, LANES), 1)
    used = lax.broadcasted_iota(jnp.int32, (LANES, m), 1) < count

    def gather_rows(t):
        position, part = divmod(t * LANES, OB)
        core_away, y_away = divmod(position, n_y)
        owner = (y ^ y_away) * PAIR + (core ^ core_away)
        wanted = owner_ref[owner, part // LANES : part // LANES + 1, :]
        wanted = jnp.broadcast_to(wanted.astype(jnp.float32), (LANES, LANES)).T.astype(jnp.int32)
        hot = []
        for k in range(owned // LANES):
            sensed = band_ref[0, k * LANES // OB].astype(jnp.float32)
            hot.append(jnp.where(wanted == lane + k * LANES, sensed, 0.0).astype(jnp.bfloat16))
        got = mm(jnp.concatenate(hot, axis=1), global_ref[0:owned, :])
        got = jnp.where(used, got, 0.0).astype(jnp.bfloat16)
        if t * LANES < mine:
            own_ref[t * LANES : (t + 1) * LANES, :] = got
        else:
            send_ref[t * LANES - mine : (t + 1) * LANES - mine, :] = got

    steps = n // (BLOCK * GROUP) - FIRST
    tiles = owned // LANES
    for p in range(steps):
        sweep_group(work_ref, (FIRST + p) * BLOCK * GROUP)
        for t in range(p * tiles // steps, (p + 1) * tiles // steps):
            gather_rows(t)
    used = lax.broadcasted_iota(jnp.int32, (KB, m), 1) < count
    border = global_ref[owned:, :].astype(jnp.float32)
    send_ref[mine:, :] = jnp.where(used, border, 0.0).astype(jnp.bfloat16)

    inverse = -work_ref[...]
    local_rows = rows_ref[...]
    i0, i1, i2 = split3(inverse)
    gain = mm(i2, local_rows) + mm(i1, local_rows) + mm(i0, local_rows)
    left = local_rows.astype(jnp.float32) - product_six(normal_ref[...], gain)
    gain = gain + product_three(inverse, left)
    for i, part in enumerate(split3(gain)):
        gain_ref[i] = part
    for t in range((mine + KB) // KB):
        tile = send_ref[t * KB : (t + 1) * KB, :]
        send_ref[t * KB : (t + 1) * KB, :] = solve_rows(tile, gain_ref, local_rows)


def begin_normal(count, prior, local_rows):
    n, m = local_rows.shape
    array = pl.BlockSpec(memory_space=pltpu.VMEM)
    return pl.pallas_call(
        normal_kernel,
        out_shape=(
            jax.ShapeDtypeStruct((n, m), jnp.bfloat16),
            jax.ShapeDtypeStruct((n, n), jnp.float32),
            jax.ShapeDtypeStruct((n, n), jnp.float32),
        ),
        in_specs=[pl.BlockSpec(memory_space=pltpu.SMEM), array, array],
        out_specs=(array, array, array),
        compiler_params=pltpu.CompilerParams(vmem_limit_bytes=16 * 1024 * 1024),
        cost_estimate=pl.CostEstimate(flops=4 * 10**9, bytes_accessed=0, transcendentals=0),
        name="begin_normal",
    )(count, prior, local_rows)


def reduce_rows(count, band, owners, rows, normal, begun, global_rows, n_y):
    n, m = rows.shape
    scalar = pl.BlockSpec(memory_space=pltpu.SMEM)
    array = pl.BlockSpec(memory_space=pltpu.VMEM)
    shapes = ((n_y * OB + KB, m), (n_y * OB, m), (3, n, m))
    return pl.pallas_call(
        functools.partial(local_kernel, n_y),
        out_shape=tuple(jax.ShapeDtypeStruct(shape, jnp.bfloat16) for shape in shapes),
        in_specs=[scalar, scalar, array, array, array, array, array],
        out_specs=tuple(array for _ in shapes),
        scratch_shapes=[pltpu.VMEM((n, n), jnp.float32)],
        compiler_params=pltpu.CompilerParams(vmem_limit_bytes=24 * 1024 * 1024),
        name="reduce_rows",
    )(count, band, owners, rows, normal, begun, global_rows)


def own_product_kernel(
    n_y, n_z, own_ref, send_ref, gain_ref, rows_ref, mine_ref, prod_ref, left
):
    z, x, _, _ = place_of()
    border = send_ref[n_y * OB :, :]
    local_rows = rows_ref[...]
    for t in range(n_y * OB // KB):
        tile = own_ref[t * KB : (t + 1) * KB, :]
        mine_ref[t * KB : (t + 1) * KB, :] = solve_rows(tile, gain_ref, local_rows)
    for y in range(n_y):
        order_rows(n_z, z, x, mine_ref, y, left)
        prod_ref[y, :, :OB] = mm(left[...], mine_ref[y * OB : (y + 1) * OB, :], INNER)
        prod_ref[y, :, OB:] = mm(left[...], border, INNER)


def order_rows(n_z, z, x, rows_ref, y, left):
    rows = OB // (n_z * PAIR)
    for i in range(PAIR):
        for j in range(n_z):
            at = (i * n_z + j) * rows
            source = pl.multiple_of(y * OB + ((z ^ j) * PAIR + (x ^ i)) * rows, rows)
            left[at : at + rows, :] = rows_ref[pl.ds(source, rows), :]


def product_kernel(
    n_y, n_z, other_ref, prod_ref,
    keep_y_ref, send_y_ref, keep_x_ref, send_x_ref, level_ref, left, total,
):
    z, x, _, _ = place_of()
    half = OB // PAIR
    border = other_ref[n_y * OB :, :]
    top = jnp.zeros((BLOCK, LANES), jnp.float32)
    for y in range(n_y):
        order_rows(n_z, z, x, other_ref, y, left)
        own = other_ref[y * OB : (y + 1) * OB, :]
        total[y, :, :OB] = prod_ref[y, :, :OB] + mm(left[...], own, INNER)
        total[y, :, OB:] = prod_ref[y, :, OB:] + mm(left[...], border, INNER)
        for h in range(WIDTH // LANES):
            part = jnp.abs(total[y, :, h * LANES : (h + 1) * LANES])
            top = jnp.maximum(top, jnp.max(part.reshape(OB // BLOCK, BLOCK, LANES), axis=0))
    top = jnp.max(jnp.max(top, axis=0, keepdims=True), axis=1, keepdims=True)
    level = jnp.floor(jnp.log2(jnp.maximum(jnp.broadcast_to(top, (BLOCK, HALF)), 1e-30)))
    level_ref[...] = level
    scale = jnp.exp2(TOP_LEVEL - level[:1])
    keep_y_ref[...] = total[0, :, :HALF]
    for j in range(1, n_y):
        send_y_ref[j - 1, :HEAD, :] = jnp.broadcast_to(level[:1], (HEAD, HALF))
        send_y_ref[j - 1, HEAD:, :] = total[j, :, :HALF] * scale
    send_x_ref[:HEAD, :] = jnp.broadcast_to(level[:1], (HEAD, HALF))
    for y in range(n_y):
        keep_x_ref[y] = total[y, :half, HALF:]
        at = HEAD + y * half
        send_x_ref[at : at + half, :] = total[y, half:, HALF:] * scale


def panel_kernel(n_y, mine_ref, other_ref, level_ref, out_ref):
    pick = lax.broadcasted_iota(jnp.int32, (P_SIZE, OB), 1) == STRIDE * lax.broadcasted_iota(
        jnp.int32, (P_SIZE, OB), 0
    )
    pick = pick.astype(jnp.float32).astype(jnp.bfloat16)
    level = level_ref[:1, :P_SIZE]
    scale = jnp.exp2(TOP_LEVEL - level)
    for y in range(n_y):
        panel = jnp.zeros((P_SIZE, P_SIZE), jnp.float32)
        for ref in (mine_ref, other_ref):
            strip = mm(pick, ref[y * OB : (y + 1) * OB, :]).astype(jnp.bfloat16)
            panel = panel + mm(strip, strip, INNER)
        out_ref[y, :HEAD, :] = jnp.broadcast_to(level, (HEAD, P_SIZE))
        out_ref[y, HEAD:, :] = panel * scale


def own_products(own, send, gain, rows, n_y, n_z):
    array = pl.BlockSpec(memory_space=pltpu.VMEM)
    m = own.shape[1]
    return pl.pallas_call(
        functools.partial(own_product_kernel, n_y, n_z),
        out_shape=(
            jax.ShapeDtypeStruct(own.shape, jnp.bfloat16),
            jax.ShapeDtypeStruct((n_y, OB, WIDTH), jnp.float32),
        ),
        in_specs=[array, array, array, array],
        out_specs=(array, array),
        scratch_shapes=[pltpu.VMEM((OB, m), jnp.bfloat16)],
        compiler_params=pltpu.CompilerParams(vmem_limit_bytes=24 * 1024 * 1024),
        cost_estimate=pl.CostEstimate(
            flops=4 * n_y * OB * WIDTH * m, bytes_accessed=0, transcendentals=0
        ),
        name="own_products",
    )(own, send, gain, rows)


def products(other, own, n_y, n_z):
    array = pl.BlockSpec(memory_space=pltpu.VMEM)
    m = other.shape[1]
    half = OB // PAIR
    shapes = (
        (OB, HALF),
        (n_y - 1, HEAD + OB, HALF),
        (n_y, half, HALF),
        (HEAD + n_y * half, HALF),
        (BLOCK, HALF),
    )
    return pl.pallas_call(
        functools.partial(product_kernel, n_y, n_z),
        out_shape=tuple(jax.ShapeDtypeStruct(shape, jnp.float32) for shape in shapes),
        in_specs=[array, array],
        out_specs=tuple(array for _ in shapes),
        scratch_shapes=[
            pltpu.VMEM((OB, m), jnp.bfloat16),
            pltpu.VMEM((n_y, OB, WIDTH), jnp.float32),
        ],
        compiler_params=pltpu.CompilerParams(vmem_limit_bytes=24 * 1024 * 1024),
        name="products",
    )(other, own)


def panel_products(mine, other, level, n_y):
    array = pl.BlockSpec(memory_space=pltpu.VMEM)
    return pl.pallas_call(
        functools.partial(panel_kernel, n_y),
        out_shape=jax.ShapeDtypeStruct((n_y, HEAD + P_SIZE, P_SIZE), jnp.float32),
        in_specs=[array, array, array],
        out_specs=array,
        cost_estimate=pl.CostEstimate(
            flops=4 * n_y * P_SIZE * OB * mine.shape[1], bytes_accessed=0, transcendentals=0
        ),
        compiler_params=pltpu.CompilerParams(vmem_limit_bytes=8 * 1024 * 1024),
        name="panel_products",
    )(mine, other, level)


def factor_group(rows, base):
    sub = lax.broadcasted_iota(jnp.int32, (BLOCK, LANES), 0)
    count = len(rows)
    for q in range(count):
        at = base + BLOCK * q
        factors = [
            [
                jnp.broadcast_to(rows[r][:, at + j : at + j + 1], (BLOCK, LANES))
                for j in range(BLOCK)
            ]
            for r in range(q, count)
        ]
        columns, own = factors[0], rows[q]
        scales, entries = [], []
        for i in range(BLOCK):
            pivot = row_of(columns[i], i)
            scale = lax.rsqrt(pivot)
            scale = scale * (1.5 - 0.5 * pivot * scale * scale)
            scales.append(scale)
            scaled = row_of(own, i) * scale
            step = columns[i] * scale
            own = jnp.where(sub == i, scaled, jnp.where(sub > i, own - step * scaled, own))
            entries.append([row_of(columns[j], i) * scale for j in range(BLOCK)])
            for j in range(i + 1, BLOCK):
                columns[j] = columns[j] - step * entries[i][j]
        rows[q] = own
        for r in range(q + 1, count):
            value = rows[r]
            below = list(factors[r - q])
            for i in range(BLOCK):
                step = below[i] * scales[i]
                value = value - step * row_of(own, i)
                for j in range(i + 1, BLOCK):
                    below[j] = below[j] - step * entries[i][j]
            rows[r] = value
    return rows


def factor_kernel(panel_ref, prior_ref, out_ref, work_ref):
    n = work_ref.shape[0]
    depth = BLOCK * FACTOR_GROUP
    row = lax.broadcasted_iota(jnp.int32, (n, n), 0)
    column = lax.broadcasted_iota(jnp.int32, (n, n), 1)
    prior = jnp.broadcast_to(prior_ref[...], (n, n))
    work_ref[...] = panel_ref[...] + jnp.where(row == column, prior, 0.0)
    for p in range(n // depth):
        base = p * depth
        rows = [
            work_ref[base + BLOCK * r : base + BLOCK * (r + 1), :] for r in range(FACTOR_GROUP)
        ]
        done = jnp.concatenate(factor_group(rows, base), axis=0)
        work_ref[base : base + depth, :] = done
        if base + depth < n:
            d0, d1, d2 = split3(done)
            update = mm(
                jnp.concatenate([d0, d0, d0, d1, d1, d2], axis=0),
                jnp.concatenate([d0, d1, d2, d0, d1, d0], axis=0),
                COLS,
            )
            work_ref[base + depth :, :] = work_ref[base + depth :, :] - update[base + depth :, :]
    out_ref[...] = jnp.where(row <= column, work_ref[...], 0.0).T


def factor_panel(panel, prior):
    n = panel.shape[0]
    return pl.pallas_call(
        factor_kernel,
        out_shape=jax.ShapeDtypeStruct((n, n), jnp.float32),
        scratch_shapes=[pltpu.VMEM((n, n), jnp.float32)],
        cost_estimate=pl.CostEstimate(flops=n**3, bytes_accessed=12 * n * n, transcendentals=n),
        compiler_params=pltpu.CompilerParams(vmem_limit_bytes=8 * 1024 * 1024),
        name="factor_panel",
    )(panel, prior)


def level_of(message):
    return message[:1].astype(jnp.float32)


def values_of(message):
    return message[HEAD:].astype(jnp.float32) * jnp.exp2(level_of(message) - TOP_LEVEL)


def message_of(values, level):
    head = jnp.broadcast_to(level, (HEAD, values.shape[1]))
    return jnp.concatenate([head, values * jnp.exp2(TOP_LEVEL - level)]).astype(jnp.float16)


def fold(message):
    parts = HALF // P_SIZE
    step = message.shape[0] // parts
    return jnp.concatenate([message[i * step : (i + 1) * step] for i in range(parts)], axis=1)


def unfold(rows):
    parts = HALF // P_SIZE
    return jnp.concatenate([rows[:, i * P_SIZE : (i + 1) * P_SIZE] for i in range(parts)], axis=0)


def pairwise(terms):
    while len(terms) > 1:
        terms = [terms[2 * i] + terms[2 * i + 1] for i in range(len(terms) // 2)]
    return terms[0]


def per_device(
    local_design, global_design, local_prior, obs_count, band_mask, owner_columns, kaula_prior
):
    n_arc, n_coef = lax.axis_size("arc"), lax.axis_size("coef")
    n_z, n_y = n_arc // PAIR, n_coef // PAIR
    rows = OB // n_arc
    def swap(values, dz=0, dx=0, dy=0, dk=0):
        pairs = []
        for a in range(n_arc):
            for c in range(n_coef):
                to_a = ((a // PAIR) ^ dz) * PAIR + ((a % PAIR) ^ dx)
                to_c = ((c // PAIR) ^ dy) * PAIR + ((c % PAIR) ^ dk)
                pairs.append((a * n_coef + c, to_a * n_coef + to_c))
        return lax.ppermute(values, AXES, pairs)

    local_rows, normal, begun = begin_normal(obs_count, local_prior, local_design[0])
    send, own, gain = reduce_rows(
        obs_count,
        band_mask,
        owner_columns.reshape(n_coef, OB // LANES, LANES),
        local_rows,
        normal,
        begun,
        global_design[0],
        n_y,
    )
    other = swap(send, dk=1)
    mine, own = own_products(own, send, gain, local_rows, n_y, n_z)
    keep_y, send_y, keep_x, send_x, level = products(other, own, n_y, n_z)
    half = OB // PAIR
    grown = float(n_y.bit_length() - 1)

    from_y = [swap(send_y[j - 1].astype(jnp.float16), dy=j) for j in range(1, n_y)]
    from_x = swap(send_x.astype(jnp.float16), dx=1)
    panels = panel_products(mine, other, level, n_y).astype(jnp.float16)
    panel_z = [panels] + [swap(panels, dz=j) for j in range(1, n_z)]
    from_y, from_x, panel_z = lax.optimization_barrier((from_y, from_x, panel_z))

    left = functools.reduce(jnp.add, [values_of(message) for message in from_y], keep_y)
    left_level = functools.reduce(
        jnp.maximum, [level_of(message) for message in from_y], level[:1]
    ) + grown
    right = keep_x + values_of(from_x).reshape(n_y, half, HALF)
    right_level = jnp.maximum(level[:1], level_of(from_x)) + 1.0
    panel_level = functools.reduce(jnp.maximum, [level_of(p[0]) for p in panel_z])
    panel_level = panel_level + float(n_z.bit_length() - 1)
    panels = [
        message_of(pairwise([values_of(message[j]) for message in panel_z]), panel_level)
        for j in range(n_y)
    ]

    over_x = jnp.concatenate([message_of(left[half:], left_level), fold(panels[0])])
    over_y = [
        jnp.concatenate([message_of(right[j], right_level), fold(panels[j])])
        for j in range(1, n_y)
    ]
    over_x, over_y, panels = lax.optimization_barrier((over_x, over_y, panels))
    from_x = swap(over_x, dx=1)
    from_y = [swap(over_y[j - 1], dy=j) for j in range(1, n_y)]
    panel_xy = [swap(panels[j], dx=1, dy=j) for j in range(1, n_y)]
    tail = (HEAD + P_SIZE) * P_SIZE // HALF
    panel_y = [panels[0]] + [unfold(message[-tail:]) for message in from_y]
    panel_x = [unfold(from_x[-tail:])] + panel_xy
    from_x, from_y = from_x[:-tail], [message[:-tail] for message in from_y]
    left = left[:half] + values_of(from_x)
    left_level = jnp.maximum(left_level, level_of(from_x)) + 1.0
    right = functools.reduce(jnp.add, [values_of(message) for message in from_y], right[0])
    right_level = functools.reduce(
        jnp.maximum, [level_of(message) for message in from_y], right_level
    ) + grown

    total = jnp.concatenate([left, right], axis=1)
    level = jnp.concatenate([left_level, right_level], axis=1)
    over_z = [message_of(total[j * rows : (j + 1) * rows], level) for j in range(1, n_z)]
    over_z, panel_x, panel_y = lax.optimization_barrier((over_z, panel_x, panel_y))
    from_z = [swap(over_z[j - 1], dz=j) for j in range(1, n_z)]
    from_z[0], panel_x, panel_y = lax.optimization_barrier((from_z[0], panel_x, panel_y))
    panel = functools.reduce(jnp.add, [values_of(message) for message in panel_y])
    panel = panel + functools.reduce(jnp.add, [values_of(message) for message in panel_x])
    panel_factor = factor_panel(panel, kaula_prior)
    normal_rows = functools.reduce(
        jnp.add, [values_of(message) for message in from_z], total[:rows]
    )
    return normal_rows[None], panel_factor[None]


def solution(mesh):
    in_specs = (
        P(AXES, None, None),
        P(AXES, None, None),
        P(AXES, None),
        P(AXES),
        P(AXES, None),
        P(),
        P("coef", None),
    )
    out_specs = (P("coef", "arc", None), P("coef", None, None))
    return jax.shard_map(
        per_device, mesh=mesh, in_specs=in_specs, out_specs=out_specs, check_vma=False
    )
```

```python
import functools

import jax
import jax.numpy as jnp
from jax import lax
from jax.experimental import pallas as pl
from jax.experimental.pallas import tpu as pltpu
from jax.sharding import PartitionSpec as P

OB = 512
KB = 256
P_SIZE = 128
STRIDE = OB // P_SIZE
WIDTH = OB + KB
HALF = WIDTH // 2
PAIR = 2
TOP_LEVEL = 12.0
HEAD = 8
INNER = (((1,), (1,)), ((), ()))
AXES = ("arc", "coef")

LANES = 128
BLOCK = 8
GROUP = 2
FACTOR_GROUP = 4
FIRST = 4
TILE = 128
ROWS = (((1,), (0,)), ((), ()))
COLS = (((0,), (0,)), ((), ()))


def mm(a, b, dims=ROWS):
    return lax.dot_general(a, b, dims, preferred_element_type=jnp.float32)


def split3(value):
    high = value.astype(jnp.bfloat16)
    rest = value - high.astype(jnp.float32)
    middle = rest.astype(jnp.bfloat16)
    low = (rest - middle.astype(jnp.float32)).astype(jnp.bfloat16)
    return high, middle, low


def row_of(value, i):
    return jnp.broadcast_to(value[i : i + 1, :], (BLOCK, LANES))


def eliminate_group(rows, base):
    sub = lax.broadcasted_iota(jnp.int32, (BLOCK, LANES), 0)
    lane = lax.broadcasted_iota(jnp.int32, (BLOCK, LANES), 1)
    count = len(rows)
    for q in range(count):
        half, at = divmod(base + BLOCK * q, LANES)
        factors = [
            [
                jnp.broadcast_to(rows[r][half][:, at + j : at + j + 1], (BLOCK, LANES))
                for j in range(BLOCK)
            ]
            for r in range(count)
        ]
        inside = (lane >= at) & (lane < at + BLOCK)
        unit = (lane - at == sub).astype(jnp.float32)
        for r in range(count):
            rows[r][half] = jnp.where(inside, unit if r == q else 0.0, rows[r][half])
        columns, own = list(factors[q]), rows[q]
        a, b, d = row_of(columns[0], 0), row_of(columns[1], 0), row_of(columns[1], 1)
        for i in range(0, BLOCK, 2):
            scale = pl.reciprocal(a * d - b * b, approx=True)

            def step(value, i=i, a=a, b=b, d=d, scale=scale):
                first, second = row_of(value, i), row_of(value, i + 1)
                upper, lower = d * first - b * second, a * second - b * first
                new = value - (columns[i] * upper + columns[i + 1] * lower) * scale
                kept = jnp.where(sub == i + 1, lower * scale, new)
                return new, jnp.where(sub == i, upper * scale, kept)

            pairs = {j: step(columns[j]) for j in range(i + 2, BLOCK)}
            for h in range(len(own)):
                own[h] = step(own[h])[1]
            if i + 2 < BLOCK:
                one, two = pairs[i + 2][0], pairs[i + 3][0]
                a, b, d = row_of(one, i + 2), row_of(two, i + 2), row_of(two, i + 3)
            for j, pair in pairs.items():
                columns[j] = pair[1]
        for r in range(count):
            if r != q:
                for h in range(len(own)):
                    t = [factors[r][j] * row_of(own[h], j) for j in range(BLOCK)]
                    rows[r][h] = rows[r][h] - (
                        ((t[0] + t[1]) + (t[2] + t[3])) + ((t[4] + t[5]) + (t[6] + t[7]))
                    )
    return rows


def sweep_group(a_ref, base):
    n = a_ref.shape[0]
    depth = BLOCK * GROUP
    before = a_ref[base : base + depth, :]
    rows = [
        [
            a_ref[base + BLOCK * r : base + BLOCK * (r + 1), LANES * h : LANES * (h + 1)]
            for h in range(n // LANES)
        ]
        for r in range(GROUP)
    ]
    rows = eliminate_group(rows, base)
    after = jnp.concatenate([jnp.concatenate(row, axis=1) for row in rows], axis=0)
    column = lax.broadcasted_iota(jnp.int32, (depth, n), 1)
    row = lax.broadcasted_iota(jnp.int32, (depth, n), 0)
    inside = (column >= base) & (column < base + depth)
    before = jnp.where(inside, jnp.where(column - base == row, -1.0, 0.0), before)
    after = jnp.where(inside, -after, after)
    u0, u1, u2 = split3(before)
    w0, w1, w2 = split3(after)
    left = jnp.concatenate([u0, u0, u0, u1, u1, u2], axis=0).T
    right = jnp.concatenate([w0, w1, w2, w0, w1, w0], axis=0)

    def update(low, high):
        row = lax.broadcasted_iota(jnp.int32, (high - low, n), 0) + low
        column = lax.broadcasted_iota(jnp.int32, (high - low, n), 1)
        outside = ((row < base) | (row >= base + depth)) & (
            (column < base) | (column >= base + depth)
        )
        a_ref[low:high, :] = jnp.where(outside, a_ref[low:high, :], 0.0) - mm(left[low:high], right)

    after = base + depth
    for low, high in ((after, after + depth), (0, after), (after + depth, n)):
        if low < min(high, n):
            update(low, min(high, n))


def place_of():
    arc, coef = lax.axis_index("arc"), lax.axis_index("coef")
    return lax.div(arc, PAIR), lax.rem(arc, PAIR), lax.div(coef, PAIR), lax.rem(coef, PAIR)


def solve_rows(tile, gain_ref, local_rows):
    solved = (mm(tile, gain_ref[1], INNER) + mm(tile, gain_ref[0], INNER)).astype(jnp.bfloat16)
    return (tile.astype(jnp.float32) - mm(solved, local_rows)).astype(jnp.bfloat16)


def normal_kernel(count_ref, prior_ref, local_ref, rows_ref, work_ref):
    n, m = local_ref.shape
    used = lax.broadcasted_iota(jnp.int32, (n, m), 1) < count_ref[0]
    rows_ref[...] = jnp.where(used, local_ref[...].astype(jnp.float32), 0.0).astype(jnp.bfloat16)
    local_rows = rows_ref[...]
    row = lax.broadcasted_iota(jnp.int32, (n, n), 0)
    column = lax.broadcasted_iota(jnp.int32, (n, n), 1)
    prior = jnp.broadcast_to(prior_ref[...], (n, n))
    work_ref[...] = mm(local_rows, local_rows, INNER) + jnp.where(row == column, prior, 0.0)
    for p in range(FIRST):
        sweep_group(work_ref, p * BLOCK * GROUP)


def local_kernel(
    n_y, count_ref, band_ref, owner_ref, rows_ref, begun_ref, global_ref,
    send_ref, own_ref, gain_ref, work_ref,
):
    n, m = rows_ref.shape
    owned = n_y * PAIR * OB
    mine = n_y * OB
    count = count_ref[0]
    _, _, y, core = place_of()
    work_ref[...] = begun_ref[...]
    lane = lax.broadcasted_iota(jnp.int32, (TILE, LANES), 1)
    used = lax.broadcasted_iota(jnp.int32, (TILE, m), 1) < count

    def gather_rows(t):
        position, part = divmod(t * TILE, OB)
        core_away, y_away = divmod(position, n_y)
        owner = (y ^ y_away) * PAIR + (core ^ core_away)
        wanted = []
        for r in range(TILE // LANES):
            at = part // LANES + r
            ids = owner_ref[owner, at : at + 1, :].astype(jnp.float32)
            wanted.append(jnp.broadcast_to(ids, (LANES, LANES)).T.astype(jnp.int32))
        wanted = jnp.concatenate(wanted, axis=0)
        hot = []
        for k in range(owned // LANES):
            sensed = band_ref[0, k * LANES // OB].astype(jnp.float32)
            hot.append(jnp.where(wanted == lane + k * LANES, sensed, 0.0).astype(jnp.bfloat16))
        got = mm(jnp.concatenate(hot, axis=1), global_ref[0:owned, :])
        got = jnp.where(used, got, 0.0).astype(jnp.bfloat16)
        if t * TILE < mine:
            own_ref[t * TILE : (t + 1) * TILE, :] = got
        else:
            send_ref[t * TILE - mine : (t + 1) * TILE - mine, :] = got

    steps = n // (BLOCK * GROUP) - FIRST
    tiles = owned // TILE
    for p in range(steps):
        sweep_group(work_ref, (FIRST + p) * BLOCK * GROUP)
        for t in range(p * tiles // steps, (p + 1) * tiles // steps):
            gather_rows(t)
    used = lax.broadcasted_iota(jnp.int32, (KB, m), 1) < count
    border = global_ref[owned:, :].astype(jnp.float32)
    send_ref[mine:, :] = jnp.where(used, border, 0.0).astype(jnp.bfloat16)

    local_rows = rows_ref[...]
    i0, i1, i2 = split3(-work_ref[...])
    gain = mm(i2, local_rows) + mm(i1, local_rows) + mm(i0, local_rows)
    for i, part in enumerate(split3(gain)[:2]):
        gain_ref[i] = part
    send_ref[...] = solve_rows(send_ref[...], gain_ref, local_rows)


def begin_normal(count, prior, local_rows):
    n, m = local_rows.shape
    array = pl.BlockSpec(memory_space=pltpu.VMEM)
    return pl.pallas_call(
        normal_kernel,
        out_shape=(
            jax.ShapeDtypeStruct((n, m), jnp.bfloat16),
            jax.ShapeDtypeStruct((n, n), jnp.float32),
        ),
        in_specs=[pl.BlockSpec(memory_space=pltpu.SMEM), array, array],
        out_specs=(array, array),
        compiler_params=pltpu.CompilerParams(vmem_limit_bytes=16 * 1024 * 1024),
        cost_estimate=pl.CostEstimate(flops=4 * 10**9, bytes_accessed=0, transcendentals=0),
        name="begin_normal",
    )(count, prior, local_rows)


def reduce_rows(count, band, owners, rows, begun, global_rows, n_y):
    n, m = rows.shape
    scalar = pl.BlockSpec(memory_space=pltpu.SMEM)
    array = pl.BlockSpec(memory_space=pltpu.VMEM)
    shapes = ((n_y * OB + KB, m), (n_y * OB, m), (2, n, m))
    return pl.pallas_call(
        functools.partial(local_kernel, n_y),
        out_shape=tuple(jax.ShapeDtypeStruct(shape, jnp.bfloat16) for shape in shapes),
        in_specs=[scalar, scalar, array, array, array, array],
        out_specs=tuple(array for _ in shapes),
        scratch_shapes=[pltpu.VMEM((n, n), jnp.float32)],
        compiler_params=pltpu.CompilerParams(vmem_limit_bytes=24 * 1024 * 1024),
        name="reduce_rows",
    )(count, band, owners, rows, begun, global_rows)


def own_product_kernel(
    n_y, n_z, own_ref, send_ref, gain_ref, rows_ref, mine_ref, prod_ref, left
):
    z, x, _, _ = place_of()
    border = send_ref[n_y * OB :, :]
    local_rows = rows_ref[...]
    for t in range(n_y):
        tile = own_ref[t * OB : (t + 1) * OB, :]
        mine_ref[t * OB : (t + 1) * OB, :] = solve_rows(tile, gain_ref, local_rows)
    for y in range(n_y):
        order_rows(n_z, z, x, mine_ref, y, left)
        prod_ref[y, :, :OB] = mm(left[...], mine_ref[y * OB : (y + 1) * OB, :], INNER)
        prod_ref[y, :, OB:] = mm(left[...], border, INNER)


def order_rows(n_z, z, x, rows_ref, y, left):
    rows = OB // (n_z * PAIR)
    for i in range(PAIR):
        for j in range(n_z):
            at = (i * n_z + j) * rows
            source = pl.multiple_of(y * OB + ((z ^ j) * PAIR + (x ^ i)) * rows, rows)
            left[at : at + rows, :] = rows_ref[pl.ds(source, rows), :]


def product_kernel(
    n_y, n_z, other_ref, prod_ref,
    keep_y_ref, send_y_ref, keep_x_ref, send_x_ref, level_ref, left, total,
):
    z, x, _, _ = place_of()
    half = OB // PAIR
    border = other_ref[n_y * OB :, :]
    top = jnp.zeros((BLOCK, LANES), jnp.float32)
    for y in range(n_y):
        order_rows(n_z, z, x, other_ref, y, left)
        own = other_ref[y * OB : (y + 1) * OB, :]
        total[y, :, :OB] = prod_ref[y, :, :OB] + mm(left[...], own, INNER)
        total[y, :, OB:] = prod_ref[y, :, OB:] + mm(left[...], border, INNER)
        for h in range(WIDTH // LANES):
            part = jnp.abs(total[y, :, h * LANES : (h + 1) * LANES])
            top = jnp.maximum(top, jnp.max(part.reshape(OB // BLOCK, BLOCK, LANES), axis=0))
    top = jnp.max(jnp.max(top, axis=0, keepdims=True), axis=1, keepdims=True)
    level = jnp.floor(jnp.log2(jnp.maximum(jnp.broadcast_to(top, (BLOCK, HALF)), 1e-30)))
    level_ref[...] = level
    scale = jnp.exp2(TOP_LEVEL - level[:1])
    keep_y_ref[...] = total[0, :, :HALF]
    for j in range(1, n_y):
        send_y_ref[j - 1, :HEAD, :] = jnp.broadcast_to(level[:1], (HEAD, HALF))
        send_y_ref[j - 1, HEAD:, :] = total[j, :, :HALF] * scale
    send_x_ref[:HEAD, :] = jnp.broadcast_to(level[:1], (HEAD, HALF))
    for y in range(n_y):
        keep_x_ref[y] = total[y, :half, HALF:]
        at = HEAD + y * half
        send_x_ref[at : at + half, :] = total[y, half:, HALF:] * scale


def panel_kernel(n_y, mine_ref, other_ref, level_ref, out_ref):
    pick = lax.broadcasted_iota(jnp.int32, (P_SIZE, OB), 1) == STRIDE * lax.broadcasted_iota(
        jnp.int32, (P_SIZE, OB), 0
    )
    pick = pick.astype(jnp.float32).astype(jnp.bfloat16)
    level = level_ref[:1, :P_SIZE]
    scale = jnp.exp2(TOP_LEVEL - level)
    for y in range(n_y):
        panel = jnp.zeros((P_SIZE, P_SIZE), jnp.float32)
        for ref in (mine_ref, other_ref):
            strip = mm(pick, ref[y * OB : (y + 1) * OB, :]).astype(jnp.bfloat16)
            panel = panel + mm(strip, strip, INNER)
        out_ref[y, :HEAD, :] = jnp.broadcast_to(level, (HEAD, P_SIZE))
        out_ref[y, HEAD:, :] = panel * scale


def own_products(own, send, gain, rows, n_y, n_z):
    array = pl.BlockSpec(memory_space=pltpu.VMEM)
    m = own.shape[1]
    return pl.pallas_call(
        functools.partial(own_product_kernel, n_y, n_z),
        out_shape=(
            jax.ShapeDtypeStruct(own.shape, jnp.bfloat16),
            jax.ShapeDtypeStruct((n_y, OB, WIDTH), jnp.float32),
        ),
        in_specs=[array, array, array, array],
        out_specs=(array, array),
        scratch_shapes=[pltpu.VMEM((OB, m), jnp.bfloat16)],
        compiler_params=pltpu.CompilerParams(vmem_limit_bytes=24 * 1024 * 1024),
        cost_estimate=pl.CostEstimate(
            flops=4 * n_y * OB * WIDTH * m, bytes_accessed=0, transcendentals=0
        ),
        name="own_products",
    )(own, send, gain, rows)


def products(other, own, n_y, n_z):
    array = pl.BlockSpec(memory_space=pltpu.VMEM)
    m = other.shape[1]
    half = OB // PAIR
    shapes = (
        (OB, HALF),
        (n_y - 1, HEAD + OB, HALF),
        (n_y, half, HALF),
        (HEAD + n_y * half, HALF),
        (BLOCK, HALF),
    )
    return pl.pallas_call(
        functools.partial(product_kernel, n_y, n_z),
        out_shape=tuple(jax.ShapeDtypeStruct(shape, jnp.float32) for shape in shapes),
        in_specs=[array, array],
        out_specs=tuple(array for _ in shapes),
        scratch_shapes=[
            pltpu.VMEM((OB, m), jnp.bfloat16),
            pltpu.VMEM((n_y, OB, WIDTH), jnp.float32),
        ],
        compiler_params=pltpu.CompilerParams(vmem_limit_bytes=24 * 1024 * 1024),
        name="products",
    )(other, own)


def panel_products(mine, other, level, n_y):
    array = pl.BlockSpec(memory_space=pltpu.VMEM)
    return pl.pallas_call(
        functools.partial(panel_kernel, n_y),
        out_shape=jax.ShapeDtypeStruct((n_y, HEAD + P_SIZE, P_SIZE), jnp.float32),
        in_specs=[array, array, array],
        out_specs=array,
        cost_estimate=pl.CostEstimate(
            flops=4 * n_y * P_SIZE * OB * mine.shape[1], bytes_accessed=0, transcendentals=0
        ),
        compiler_params=pltpu.CompilerParams(vmem_limit_bytes=8 * 1024 * 1024),
        name="panel_products",
    )(mine, other, level)


def factor_group(rows, base):
    sub = lax.broadcasted_iota(jnp.int32, (BLOCK, LANES), 0)
    count = len(rows)
    for q in range(count):
        at = base + BLOCK * q
        factors = [
            [
                jnp.broadcast_to(rows[r][:, at + j : at + j + 1], (BLOCK, LANES))
                for j in range(BLOCK)
            ]
            for r in range(q, count)
        ]
        columns, own = factors[0], rows[q]
        scales, entries = [], []
        for i in range(BLOCK):
            pivot = row_of(columns[i], i)
            scale = lax.rsqrt(pivot)
            scale = scale * (1.5 - 0.5 * pivot * scale * scale)
            scales.append(scale)
            scaled = row_of(own, i) * scale
            step = columns[i] * scale
            own = jnp.where(sub == i, scaled, jnp.where(sub > i, own - step * scaled, own))
            entries.append([row_of(columns[j], i) * scale for j in range(BLOCK)])
            for j in range(i + 1, BLOCK):
                columns[j] = columns[j] - step * entries[i][j]
        rows[q] = own
        for r in range(q + 1, count):
            value = rows[r]
            below = list(factors[r - q])
            for i in range(BLOCK):
                step = below[i] * scales[i]
                value = value - step * row_of(own, i)
                for j in range(i + 1, BLOCK):
                    below[j] = below[j] - step * entries[i][j]
            rows[r] = value
    return rows


def factor_kernel(panel_ref, prior_ref, out_ref, work_ref):
    n = work_ref.shape[0]
    depth = BLOCK * FACTOR_GROUP
    row = lax.broadcasted_iota(jnp.int32, (n, n), 0)
    column = lax.broadcasted_iota(jnp.int32, (n, n), 1)
    prior = jnp.broadcast_to(prior_ref[...], (n, n))
    work_ref[...] = panel_ref[...] + jnp.where(row == column, prior, 0.0)
    for p in range(n // depth):
        base = p * depth
        rows = [
            work_ref[base + BLOCK * r : base + BLOCK * (r + 1), :] for r in range(FACTOR_GROUP)
        ]
        done = jnp.concatenate(factor_group(rows, base), axis=0)
        work_ref[base : base + depth, :] = done
        if base + depth < n:
            d0, d1, d2 = split3(done)
            update = mm(
                jnp.concatenate([d0, d0, d0, d1, d1, d2], axis=0),
                jnp.concatenate([d0, d1, d2, d0, d1, d0], axis=0),
                COLS,
            )
            work_ref[base + depth :, :] = work_ref[base + depth :, :] - update[base + depth :, :]
    out_ref[...] = jnp.where(row <= column, work_ref[...], 0.0).T


def factor_panel(panel, prior):
    n = panel.shape[0]
    return pl.pallas_call(
        factor_kernel,
        out_shape=jax.ShapeDtypeStruct((n, n), jnp.float32),
        scratch_shapes=[pltpu.VMEM((n, n), jnp.float32)],
        cost_estimate=pl.CostEstimate(flops=n**3, bytes_accessed=12 * n * n, transcendentals=n),
        compiler_params=pltpu.CompilerParams(vmem_limit_bytes=8 * 1024 * 1024),
        name="factor_panel",
    )(panel, prior)


def level_of(message):
    return message[:1].astype(jnp.float32)


def values_of(message):
    return message[HEAD:].astype(jnp.float32) * jnp.exp2(level_of(message) - TOP_LEVEL)


def message_of(values, level):
    head = jnp.broadcast_to(level, (HEAD, values.shape[1]))
    return jnp.concatenate([head, values * jnp.exp2(TOP_LEVEL - level)]).astype(jnp.float16)


def pairwise(terms):
    while len(terms) > 1:
        terms = [terms[2 * i] + terms[2 * i + 1] for i in range(len(terms) // 2)]
    return terms[0]


def per_device(
    local_design, global_design, local_prior, obs_count, band_mask, owner_columns, kaula_prior
):
    n_arc, n_coef = lax.axis_size("arc"), lax.axis_size("coef")
    n_z, n_y = n_arc // PAIR, n_coef // PAIR
    rows = OB // n_arc
    def swap(values, dz=0, dx=0, dy=0, dk=0):
        pairs = []
        for a in range(n_arc):
            for c in range(n_coef):
                to_a = ((a // PAIR) ^ dz) * PAIR + ((a % PAIR) ^ dx)
                to_c = ((c // PAIR) ^ dy) * PAIR + ((c % PAIR) ^ dk)
                pairs.append((a * n_coef + c, to_a * n_coef + to_c))
        return lax.ppermute(values, AXES, pairs)

    local_rows, begun = begin_normal(obs_count, local_prior, local_design[0])
    send, own, gain = reduce_rows(
        obs_count,
        band_mask,
        owner_columns.reshape(n_coef, OB // LANES, LANES),
        local_rows,
        begun,
        global_design[0],
        n_y,
    )
    other = swap(send, dk=1)
    mine, own = own_products(own, send, gain, local_rows, n_y, n_z)
    keep_y, send_y, keep_x, send_x, level = products(other, own, n_y, n_z)
    half = OB // PAIR
    grown = float(n_y.bit_length() - 1)

    from_y = [swap(send_y[j - 1].astype(jnp.float16), dy=j) for j in range(1, n_y)]
    from_x = swap(send_x.astype(jnp.float16), dx=1)
    panels = panel_products(mine, other, level, n_y).astype(jnp.float16)
    panel_z = [panels] + [swap(panels, dz=j) for j in range(1, n_z)]

    left = functools.reduce(jnp.add, [values_of(message) for message in from_y], keep_y)
    left_level = functools.reduce(
        jnp.maximum, [level_of(message) for message in from_y], level[:1]
    ) + grown
    right = keep_x + values_of(from_x).reshape(n_y, half, HALF)
    right_level = jnp.maximum(level[:1], level_of(from_x)) + 1.0

    over_x = message_of(left[half:], left_level)
    over_y = [message_of(right[j], right_level) for j in range(1, n_y)]
    over_x, over_y = lax.optimization_barrier((over_x, over_y))
    panel_z, _ = lax.optimization_barrier((panel_z, (over_x, over_y)))
    from_x = swap(over_x, dx=1)
    from_y = [swap(over_y[j - 1], dy=j) for j in range(1, n_y)]
    from_x, from_y = lax.optimization_barrier((from_x, from_y))
    panel_level = functools.reduce(jnp.maximum, [level_of(p[0]) for p in panel_z])
    panel_level = panel_level + float(n_z.bit_length() - 1)
    panels = [
        message_of(pairwise([values_of(message[j]) for message in panel_z]), panel_level)
        for j in range(n_y)
    ]
    panel_y = [panels[0]] + [swap(panels[j], dy=j) for j in range(1, n_y)]
    panel_x = [swap(panels[j], dx=1, dy=j) for j in range(n_y)]
    left = left[:half] + values_of(from_x)
    left_level = jnp.maximum(left_level, level_of(from_x)) + 1.0
    right = functools.reduce(jnp.add, [values_of(message) for message in from_y], right[0])
    right_level = functools.reduce(
        jnp.maximum, [level_of(message) for message in from_y], right_level
    ) + grown

    total = jnp.concatenate([left, right], axis=1)
    level = jnp.concatenate([left_level, right_level], axis=1)
    over_z = [message_of(total[j * rows : (j + 1) * rows], level) for j in range(1, n_z)]
    from_z = [swap(over_z[j - 1], dz=j) for j in range(1, n_z)]
    panel_x, panel_y, _ = lax.optimization_barrier((panel_x, panel_y, over_z))
    panel = functools.reduce(jnp.add, [values_of(message) for message in panel_y])
    panel = panel + functools.reduce(jnp.add, [values_of(message) for message in panel_x])
    panel_factor = factor_panel(panel, kaula_prior)
    from_z, panel_factor = lax.optimization_barrier((from_z, panel_factor))
    normal_rows = functools.reduce(
        jnp.add, [values_of(message) for message in from_z], total[:rows]
    )
    return normal_rows[None], panel_factor[None]


def solution(mesh):
    in_specs = (
        P(AXES, None, None),
        P(AXES, None, None),
        P(AXES, None),
        P(AXES),
        P(AXES, None),
        P(),
        P("coef", None),
    )
    out_specs = (P("coef", "arc", None), P("coef", None, None))
    return jax.shard_map(
        per_device, mesh=mesh, in_specs=in_specs, out_specs=out_specs, check_vma=False
    )
```

```python
import functools

import jax
import jax.numpy as jnp
from jax import lax
from jax.experimental import pallas as pl
from jax.experimental.pallas import tpu as pltpu
from jax.sharding import PartitionSpec as P

OB = 512
KB = 256
P_SIZE = 128
STRIDE = OB // P_SIZE
WIDTH = OB + KB
PAIR = 2
TOP_LEVEL = 12.0
HEAD = 8
INNER = (((1,), (1,)), ((), ()))
AXES = ("arc", "coef")

LANES = 128
BLOCK = 8
GROUP = 2
FACTOR_GROUP = 4
FIRST = 4
TILE = 128
ROWS = (((1,), (0,)), ((), ()))
COLS = (((0,), (0,)), ((), ()))


def mm(a, b, dims=ROWS):
    return lax.dot_general(a, b, dims, preferred_element_type=jnp.float32)


def split3(value):
    high = value.astype(jnp.bfloat16)
    rest = value - high.astype(jnp.float32)
    middle = rest.astype(jnp.bfloat16)
    low = (rest - middle.astype(jnp.float32)).astype(jnp.bfloat16)
    return high, middle, low


def row_of(value, i):
    return jnp.broadcast_to(value[i : i + 1, :], (BLOCK, LANES))


def eliminate_group(rows, base):
    sub = lax.broadcasted_iota(jnp.int32, (BLOCK, LANES), 0)
    lane = lax.broadcasted_iota(jnp.int32, (BLOCK, LANES), 1)
    count = len(rows)
    for q in range(count):
        half, at = divmod(base + BLOCK * q, LANES)
        factors = [
            [
                jnp.broadcast_to(rows[r][half][:, at + j : at + j + 1], (BLOCK, LANES))
                for j in range(BLOCK)
            ]
            for r in range(count)
        ]
        inside = (lane >= at) & (lane < at + BLOCK)
        unit = (lane - at == sub).astype(jnp.float32)
        for r in range(count):
            rows[r][half] = jnp.where(inside, unit if r == q else 0.0, rows[r][half])
        columns, own = list(factors[q]), rows[q]
        a, b, d = row_of(columns[0], 0), row_of(columns[1], 0), row_of(columns[1], 1)
        for i in range(0, BLOCK, 2):
            scale = pl.reciprocal(a * d - b * b, approx=True)

            def step(value, i=i, a=a, b=b, d=d, scale=scale):
                first, second = row_of(value, i), row_of(value, i + 1)
                upper, lower = d * first - b * second, a * second - b * first
                new = value - (columns[i] * upper + columns[i + 1] * lower) * scale
                kept = jnp.where(sub == i + 1, lower * scale, new)
                return new, jnp.where(sub == i, upper * scale, kept)

            pairs = {j: step(columns[j]) for j in range(i + 2, BLOCK)}
            for h in range(len(own)):
                own[h] = step(own[h])[1]
            if i + 2 < BLOCK:
                one, two = pairs[i + 2][0], pairs[i + 3][0]
                a, b, d = row_of(one, i + 2), row_of(two, i + 2), row_of(two, i + 3)
            for j, pair in pairs.items():
                columns[j] = pair[1]
        for r in range(count):
            if r != q:
                for h in range(len(own)):
                    t = [factors[r][j] * row_of(own[h], j) for j in range(BLOCK)]
                    rows[r][h] = rows[r][h] - (
                        ((t[0] + t[1]) + (t[2] + t[3])) + ((t[4] + t[5]) + (t[6] + t[7]))
                    )
    return rows


def sweep_group(a_ref, base):
    n = a_ref.shape[0]
    depth = BLOCK * GROUP
    before = a_ref[base : base + depth, :]
    rows = [
        [
            a_ref[base + BLOCK * r : base + BLOCK * (r + 1), LANES * h : LANES * (h + 1)]
            for h in range(n // LANES)
        ]
        for r in range(GROUP)
    ]
    rows = eliminate_group(rows, base)
    after = jnp.concatenate([jnp.concatenate(row, axis=1) for row in rows], axis=0)
    column = lax.broadcasted_iota(jnp.int32, (depth, n), 1)
    row = lax.broadcasted_iota(jnp.int32, (depth, n), 0)
    inside = (column >= base) & (column < base + depth)
    before = jnp.where(inside, jnp.where(column - base == row, -1.0, 0.0), before)
    after = jnp.where(inside, -after, after)
    u0, u1, u2 = split3(before)
    w0, w1, w2 = split3(after)
    left = jnp.concatenate([u0, u0, u0, u1, u1, u2], axis=0).T
    right = jnp.concatenate([w0, w1, w2, w0, w1, w0], axis=0)

    def update(low, high):
        row = lax.broadcasted_iota(jnp.int32, (high - low, n), 0) + low
        column = lax.broadcasted_iota(jnp.int32, (high - low, n), 1)
        outside = ((row < base) | (row >= base + depth)) & (
            (column < base) | (column >= base + depth)
        )
        a_ref[low:high, :] = jnp.where(outside, a_ref[low:high, :], 0.0) - mm(left[low:high], right)

    after = base + depth
    for low, high in ((after, after + depth), (0, after), (after + depth, n)):
        if low < min(high, n):
            update(low, min(high, n))


def place_of():
    arc, coef = lax.axis_index("arc"), lax.axis_index("coef")
    return lax.div(arc, PAIR), lax.rem(arc, PAIR), lax.div(coef, PAIR), lax.rem(coef, PAIR)


def solve_rows(tile, gain_ref, local_rows):
    solved = (mm(tile, gain_ref[1], INNER) + mm(tile, gain_ref[0], INNER)).astype(jnp.bfloat16)
    return (tile.astype(jnp.float32) - mm(solved, local_rows)).astype(jnp.bfloat16)


def normal_kernel(count_ref, prior_ref, local_ref, rows_ref, work_ref):
    n, m = local_ref.shape
    used = lax.broadcasted_iota(jnp.int32, (n, m), 1) < count_ref[0]
    rows_ref[...] = jnp.where(used, local_ref[...].astype(jnp.float32), 0.0).astype(jnp.bfloat16)
    local_rows = rows_ref[...]
    row = lax.broadcasted_iota(jnp.int32, (n, n), 0)
    column = lax.broadcasted_iota(jnp.int32, (n, n), 1)
    prior = jnp.broadcast_to(prior_ref[...], (n, n))
    work_ref[...] = mm(local_rows, local_rows, INNER) + jnp.where(row == column, prior, 0.0)
    for p in range(FIRST):
        sweep_group(work_ref, p * BLOCK * GROUP)


def local_kernel(
    n_y, count_ref, band_ref, owner_ref, rows_ref, begun_ref, global_ref,
    send_ref, own_ref, gain_ref, work_ref,
):
    n, m = rows_ref.shape
    owned = n_y * PAIR * OB
    mine = n_y * OB
    count = count_ref[0]
    _, _, y, core = place_of()
    work_ref[...] = begun_ref[...]
    lane = lax.broadcasted_iota(jnp.int32, (TILE, LANES), 1).astype(jnp.int16)
    used = lax.broadcasted_iota(jnp.int32, (TILE, m), 1) < count

    def gather_rows(t):
        position, part = divmod(t * TILE, OB)
        core_away, y_away = divmod(position, n_y)
        owner = (y ^ y_away) * PAIR + (core ^ core_away)
        wanted = []
        for r in range(TILE // LANES):
            at = part // LANES + r
            ids = owner_ref[owner, at : at + 1, :].astype(jnp.float32)
            ids = jnp.broadcast_to(ids, (LANES, LANES)).T
            wanted.append(ids.astype(jnp.int32).astype(jnp.int16))
        wanted = jnp.concatenate(wanted, axis=0)
        hot, nothing = [], jnp.zeros((TILE, LANES), jnp.bfloat16)
        for k in range(owned // LANES):
            sensed = band_ref[0, k * LANES // OB].astype(jnp.float32).astype(jnp.bfloat16)
            sensed = jnp.full((TILE, LANES), sensed)
            hot.append(jnp.where(wanted == lane + jnp.int16(k * LANES), sensed, nothing))
        got = mm(jnp.concatenate(hot, axis=1), global_ref[0:owned, :])
        got = jnp.where(used, got, 0.0).astype(jnp.bfloat16)
        if t * TILE < mine:
            own_ref[t * TILE : (t + 1) * TILE, :] = got
        else:
            send_ref[t * TILE - mine : (t + 1) * TILE - mine, :] = got

    steps = n // (BLOCK * GROUP) - FIRST
    tiles = owned // TILE
    for p in range(steps):
        sweep_group(work_ref, (FIRST + p) * BLOCK * GROUP)
        for t in range(p * tiles // steps, (p + 1) * tiles // steps):
            gather_rows(t)
    used = lax.broadcasted_iota(jnp.int32, (KB, m), 1) < count
    border = global_ref[owned:, :].astype(jnp.float32)
    send_ref[mine:, :] = jnp.where(used, border, 0.0).astype(jnp.bfloat16)

    local_rows = rows_ref[...]
    i0, i1, i2 = split3(-work_ref[...])
    gain = mm(i2, local_rows) + mm(i1, local_rows) + mm(i0, local_rows)
    for i, part in enumerate(split3(gain)[:2]):
        gain_ref[i] = part
    send_ref[...] = solve_rows(send_ref[...], gain_ref, local_rows)


def begin_normal(count, prior, local_rows):
    n, m = local_rows.shape
    array = pl.BlockSpec(memory_space=pltpu.VMEM)
    return pl.pallas_call(
        normal_kernel,
        out_shape=(
            jax.ShapeDtypeStruct((n, m), jnp.bfloat16),
            jax.ShapeDtypeStruct((n, n), jnp.float32),
        ),
        in_specs=[pl.BlockSpec(memory_space=pltpu.SMEM), array, array],
        out_specs=(array, array),
        compiler_params=pltpu.CompilerParams(vmem_limit_bytes=16 * 1024 * 1024),
        cost_estimate=pl.CostEstimate(flops=4 * 10**9, bytes_accessed=0, transcendentals=0),
        name="begin_normal",
    )(count, prior, local_rows)


def reduce_rows(count, band, owners, rows, begun, global_rows, n_y):
    n, m = rows.shape
    scalar = pl.BlockSpec(memory_space=pltpu.SMEM)
    array = pl.BlockSpec(memory_space=pltpu.VMEM)
    shapes = ((n_y * OB + KB, m), (n_y * OB, m), (2, n, m))
    return pl.pallas_call(
        functools.partial(local_kernel, n_y),
        out_shape=tuple(jax.ShapeDtypeStruct(shape, jnp.bfloat16) for shape in shapes),
        in_specs=[scalar, scalar, array, array, array, array],
        out_specs=tuple(array for _ in shapes),
        scratch_shapes=[pltpu.VMEM((n, n), jnp.float32)],
        compiler_params=pltpu.CompilerParams(vmem_limit_bytes=24 * 1024 * 1024),
        name="reduce_rows",
    )(count, band, owners, rows, begun, global_rows)


def own_product_kernel(
    n_y, n_z, own_ref, send_ref, gain_ref, rows_ref, mine_ref, square_ref, side_ref, left
):
    z, x, _, _ = place_of()
    border = send_ref[n_y * OB :, :]
    local_rows = rows_ref[...]
    for t in range(n_y):
        tile = own_ref[t * OB : (t + 1) * OB, :]
        mine_ref[t * OB : (t + 1) * OB, :] = solve_rows(tile, gain_ref, local_rows)
    for y in range(n_y):
        for g in range(OB // LANES):
            low, high = g * LANES, (g + 1) * LANES
            rows = mine_ref[y * OB + low : y * OB + high, :]
            square_ref[y, low:high, :high] = mm(rows, mine_ref[y * OB : y * OB + high, :], INNER)
        order_rows(n_z, z, x, mine_ref, y, left)
        side_ref[y] = mm(left[...], border, INNER)


def order_rows(n_z, z, x, rows_ref, y, left):
    rows = OB // (n_z * PAIR)
    for i in range(PAIR):
        for j in range(n_z):
            at = (i * n_z + j) * rows
            source = pl.multiple_of(y * OB + ((z ^ j) * PAIR + (x ^ i)) * rows, rows)
            left[at : at + rows, :] = rows_ref[pl.ds(source, rows), :]


def lower_blocks():
    return [(g, t) for g in range(OB // LANES) for t in range(g + 1)]


def product_kernel(
    n_y, n_z, other_ref, square_ref, side_ref,
    keep_y_ref, send_y_ref, keep_x_ref, send_x_ref, level_ref, left, square, side,
):
    z, x, _, _ = place_of()
    half = OB // PAIR
    border = other_ref[n_y * OB :, :]
    top = jnp.zeros((BLOCK, LANES), jnp.float32)

    def raised(top, value):
        count = value.shape[0]
        value = jnp.abs(value).reshape(count // BLOCK, BLOCK, LANES)
        return jnp.maximum(top, jnp.max(value, axis=0))

    for y in range(n_y):
        for g in range(OB // LANES):
            low, high = g * LANES, (g + 1) * LANES
            rows = other_ref[y * OB + low : y * OB + high, :]
            square[y, low:high, :high] = square_ref[y, low:high, :high] + mm(
                rows, other_ref[y * OB : y * OB + high, :], INNER
            )
            for t in range(g + 1):
                top = raised(top, square[y, low:high, t * LANES : (t + 1) * LANES])
        order_rows(n_z, z, x, other_ref, y, left)
        side[y] = side_ref[y] + mm(left[...], border, INNER)
        for h in range(KB // LANES):
            top = raised(top, side[y, :, h * LANES : (h + 1) * LANES])
    top = jnp.max(jnp.max(top, axis=0, keepdims=True), axis=1, keepdims=True)
    level = jnp.floor(jnp.log2(jnp.maximum(jnp.broadcast_to(top, (BLOCK, OB)), 1e-30)))
    level_ref[...] = level
    scale = jnp.exp2(TOP_LEVEL - level[:1, :KB])
    for j in range(1, n_y):
        send_y_ref[j - 1, :HEAD, :] = jnp.broadcast_to(level[:1, :LANES], (HEAD, LANES))
    for i, (g, t) in enumerate(lower_blocks()):
        rows, columns = slice(g * LANES, (g + 1) * LANES), slice(t * LANES, (t + 1) * LANES)
        keep_y_ref[i * LANES : (i + 1) * LANES, :] = square[0, rows, columns]
        for j in range(1, n_y):
            at = HEAD + i * LANES
            send_y_ref[j - 1, at : at + LANES, :] = square[j, rows, columns] * scale[:, :LANES]
    send_x_ref[:HEAD, :] = jnp.broadcast_to(level[:1, :KB], (HEAD, KB))
    for y in range(n_y):
        keep_x_ref[y] = side[y, :half, :]
        at = HEAD + y * half
        send_x_ref[at : at + half, :] = side[y, half:, :] * scale


def expand_kernel(n_z, packed_ref, out_ref):
    z, x, _, _ = place_of()
    rows = OB // (n_z * PAIR)
    place = {pair: i for i, pair in enumerate(lower_blocks())}
    for g in range(OB // LANES):
        for t in range(OB // LANES):
            at = place[max(g, t), min(g, t)] * LANES
            block = packed_ref[at : at + LANES, :]
            block = block if t <= g else block.T
            for b in range(LANES // rows):
                arc = g * (LANES // rows) + b
                to = (((arc % PAIR) ^ x) * n_z + ((arc // PAIR) ^ z)) * rows
                to = pl.multiple_of(to, rows)
                out_ref[pl.ds(to, rows), t * LANES : (t + 1) * LANES] = block[
                    b * rows : (b + 1) * rows, :
                ]


def panel_kernel(n_y, mine_ref, other_ref, level_ref, out_ref):
    pick = lax.broadcasted_iota(jnp.int32, (P_SIZE, OB), 1) == STRIDE * lax.broadcasted_iota(
        jnp.int32, (P_SIZE, OB), 0
    )
    pick = pick.astype(jnp.float32).astype(jnp.bfloat16)
    level = level_ref[:1, :P_SIZE]
    scale = jnp.exp2(TOP_LEVEL - level)
    half = P_SIZE // 2
    row = lax.broadcasted_iota(jnp.int32, (half, P_SIZE), 0)
    column = lax.broadcasted_iota(jnp.int32, (half, P_SIZE), 1) - half
    for y in range(n_y):
        panel = jnp.zeros((P_SIZE, P_SIZE), jnp.float32)
        for ref in (mine_ref, other_ref):
            strip = mm(pick, ref[y * OB : (y + 1) * OB, :]).astype(jnp.bfloat16)
            panel = panel + mm(strip, strip, INNER)
        upper, lower = panel[:half], panel[half:]
        corner = jnp.where(row >= column, pltpu.roll(upper, half, 1), lower)
        spare = jnp.sum(jnp.where(row == column, lower, 0.0), axis=0, keepdims=True)
        out_ref[y, :HEAD, :] = jnp.broadcast_to(level, (HEAD, P_SIZE))
        out_ref[y, HEAD : HEAD + half, :] = jnp.where(column < 0, lower, corner) * scale
        out_ref[y, HEAD + half :, :] = jnp.broadcast_to(spare * scale, (BLOCK, P_SIZE))


def own_products(own, send, gain, rows, n_y, n_z):
    array = pl.BlockSpec(memory_space=pltpu.VMEM)
    m = own.shape[1]
    return pl.pallas_call(
        functools.partial(own_product_kernel, n_y, n_z),
        out_shape=(
            jax.ShapeDtypeStruct(own.shape, jnp.bfloat16),
            jax.ShapeDtypeStruct((n_y, OB, OB), jnp.float32),
            jax.ShapeDtypeStruct((n_y, OB, KB), jnp.float32),
        ),
        in_specs=[array, array, array, array],
        out_specs=(array, array, array),
        scratch_shapes=[pltpu.VMEM((OB, m), jnp.bfloat16)],
        compiler_params=pltpu.CompilerParams(vmem_limit_bytes=24 * 1024 * 1024),
        cost_estimate=pl.CostEstimate(
            flops=4 * n_y * OB * WIDTH * m, bytes_accessed=0, transcendentals=0
        ),
        name="own_products",
    )(own, send, gain, rows)


def products(other, square, side, n_y, n_z):
    array = pl.BlockSpec(memory_space=pltpu.VMEM)
    m = other.shape[1]
    half, packed = OB // PAIR, len(lower_blocks()) * LANES
    shapes = (
        (packed, LANES),
        (n_y - 1, HEAD + packed, LANES),
        (n_y, half, KB),
        (HEAD + n_y * half, KB),
        (BLOCK, OB),
    )
    return pl.pallas_call(
        functools.partial(product_kernel, n_y, n_z),
        out_shape=tuple(jax.ShapeDtypeStruct(shape, jnp.float32) for shape in shapes),
        in_specs=[array, array, array],
        out_specs=tuple(array for _ in shapes),
        scratch_shapes=[
            pltpu.VMEM((OB, m), jnp.bfloat16),
            pltpu.VMEM((n_y, OB, OB), jnp.float32),
            pltpu.VMEM((n_y, OB, KB), jnp.float32),
        ],
        compiler_params=pltpu.CompilerParams(vmem_limit_bytes=24 * 1024 * 1024),
        name="products",
    )(other, square, side)


def expand(packed, n_z):
    array = pl.BlockSpec(memory_space=pltpu.VMEM)
    return pl.pallas_call(
        functools.partial(expand_kernel, n_z),
        out_shape=jax.ShapeDtypeStruct((OB, OB), jnp.float32),
        in_specs=[array],
        out_specs=array,
        compiler_params=pltpu.CompilerParams(vmem_limit_bytes=8 * 1024 * 1024),
        name="expand",
    )(packed)


def panel_products(mine, other, level, n_y):
    array = pl.BlockSpec(memory_space=pltpu.VMEM)
    return pl.pallas_call(
        functools.partial(panel_kernel, n_y),
        out_shape=jax.ShapeDtypeStruct((n_y, HEAD + P_SIZE // 2 + BLOCK, P_SIZE), jnp.float32),
        in_specs=[array, array, array],
        out_specs=array,
        cost_estimate=pl.CostEstimate(
            flops=4 * n_y * P_SIZE * OB * mine.shape[1], bytes_accessed=0, transcendentals=0
        ),
        compiler_params=pltpu.CompilerParams(vmem_limit_bytes=8 * 1024 * 1024),
        name="panel_products",
    )(mine, other, level)


def factor_group(rows, base):
    sub = lax.broadcasted_iota(jnp.int32, (BLOCK, LANES), 0)
    count = len(rows)
    for q in range(count):
        at = base + BLOCK * q
        factors = [
            [
                jnp.broadcast_to(rows[r][:, at + j : at + j + 1], (BLOCK, LANES))
                for j in range(BLOCK)
            ]
            for r in range(q, count)
        ]
        columns, own = factors[0], rows[q]
        scales, entries = [], []
        for i in range(BLOCK):
            pivot = row_of(columns[i], i)
            scale = lax.rsqrt(pivot)
            scale = scale * (1.5 - 0.5 * pivot * scale * scale)
            scales.append(scale)
            scaled = row_of(own, i) * scale
            step = columns[i] * scale
            own = jnp.where(sub == i, scaled, jnp.where(sub > i, own - step * scaled, own))
            entries.append([row_of(columns[j], i) * scale for j in range(BLOCK)])
            for j in range(i + 1, BLOCK):
                columns[j] = columns[j] - step * entries[i][j]
        rows[q] = own
        for r in range(q + 1, count):
            value = rows[r]
            below = list(factors[r - q])
            for i in range(BLOCK):
                step = below[i] * scales[i]
                value = value - step * row_of(own, i)
                for j in range(i + 1, BLOCK):
                    below[j] = below[j] - step * entries[i][j]
            rows[r] = value
    return rows


def factor_kernel(panel_ref, prior_ref, out_ref, work_ref):
    n = work_ref.shape[0]
    depth = BLOCK * FACTOR_GROUP
    row = lax.broadcasted_iota(jnp.int32, (n, n), 0)
    column = lax.broadcasted_iota(jnp.int32, (n, n), 1)
    prior = jnp.broadcast_to(prior_ref[...], (n, n))
    half = n // 2
    packed, spare = panel_ref[:half, :], panel_ref[half : half + 1, :]
    diagonal = column[:half] - half == row[:half]
    whole = jnp.concatenate(
        [pltpu.roll(packed, half, 1), jnp.where(diagonal, spare, packed)], axis=0
    )
    known = ((row < half) & (column < half) & (row >= column)) | (
        (row >= half) & ((column < half) | (row <= column))
    )
    whole = jnp.where(known, whole, whole.T)
    work_ref[...] = whole + jnp.where(row == column, prior, 0.0)
    for p in range(n // depth):
        base = p * depth
        rows = [
            work_ref[base + BLOCK * r : base + BLOCK * (r + 1), :] for r in range(FACTOR_GROUP)
        ]
        done = jnp.concatenate(factor_group(rows, base), axis=0)
        work_ref[base : base + depth, :] = done
        if base + depth < n:
            d0, d1, d2 = split3(done)
            update = mm(
                jnp.concatenate([d0, d0, d0, d1, d1, d2], axis=0),
                jnp.concatenate([d0, d1, d2, d0, d1, d0], axis=0),
                COLS,
            )
            work_ref[base + depth :, :] = work_ref[base + depth :, :] - update[base + depth :, :]
    out_ref[...] = jnp.where(row <= column, work_ref[...], 0.0).T


def factor_panel(panel, prior):
    n = panel.shape[1]
    return pl.pallas_call(
        factor_kernel,
        out_shape=jax.ShapeDtypeStruct((n, n), jnp.float32),
        scratch_shapes=[pltpu.VMEM((n, n), jnp.float32)],
        cost_estimate=pl.CostEstimate(flops=n**3, bytes_accessed=12 * n * n, transcendentals=n),
        compiler_params=pltpu.CompilerParams(vmem_limit_bytes=8 * 1024 * 1024),
        name="factor_panel",
    )(panel, prior)


def level_of(message):
    return message[:1].astype(jnp.float32)


def values_of(message):
    return message[HEAD:].astype(jnp.float32) * jnp.exp2(level_of(message) - TOP_LEVEL)


def message_of(values, level):
    head = jnp.broadcast_to(level, (HEAD, values.shape[1]))
    return jnp.concatenate([head, values * jnp.exp2(TOP_LEVEL - level)]).astype(jnp.float16)


def pairwise(terms):
    while len(terms) > 1:
        terms = [terms[2 * i] + terms[2 * i + 1] for i in range(len(terms) // 2)]
    return terms[0]


def per_device(
    local_design, global_design, local_prior, obs_count, band_mask, owner_columns, kaula_prior
):
    n_arc, n_coef = lax.axis_size("arc"), lax.axis_size("coef")
    n_z, n_y = n_arc // PAIR, n_coef // PAIR
    rows = OB // n_arc
    def swap(values, dz=0, dx=0, dy=0, dk=0):
        pairs = []
        for a in range(n_arc):
            for c in range(n_coef):
                to_a = ((a // PAIR) ^ dz) * PAIR + ((a % PAIR) ^ dx)
                to_c = ((c // PAIR) ^ dy) * PAIR + ((c % PAIR) ^ dk)
                pairs.append((a * n_coef + c, to_a * n_coef + to_c))
        return lax.ppermute(values, AXES, pairs)

    local_rows, begun = begin_normal(obs_count, local_prior, local_design[0])
    send, own, gain = reduce_rows(
        obs_count,
        band_mask,
        owner_columns.reshape(n_coef, OB // LANES, LANES),
        local_rows,
        begun,
        global_design[0],
        n_y,
    )
    other = swap(send, dk=1)
    mine, square, side = own_products(own, send, gain, local_rows, n_y, n_z)
    keep_y, send_y, keep_x, send_x, level = products(other, square, side, n_y, n_z)
    half = OB // PAIR
    grown = float(n_y.bit_length() - 1)

    from_y = [swap(send_y[j - 1].astype(jnp.float16), dy=j) for j in range(1, n_y)]
    from_x = swap(send_x.astype(jnp.float16), dx=1)
    panels = panel_products(mine, other, level, n_y).astype(jnp.float16)
    panel_z = [panels] + [swap(panels, dz=j) for j in range(1, n_z)]

    from_y, from_x = lax.optimization_barrier((from_y, from_x))
    packed = functools.reduce(jnp.add, [values_of(message) for message in from_y], keep_y)
    left_level = functools.reduce(
        jnp.maximum, [level_of(message) for message in from_y], level[:1, :LANES]
    ) + grown
    left_level = jnp.concatenate([left_level] * (OB // LANES), axis=1)
    left = expand(packed, n_z)
    right = keep_x + values_of(from_x).reshape(n_y, half, KB)
    right_level = jnp.maximum(level[:1, :KB], level_of(from_x)) + 1.0

    over_x = message_of(left[half:], left_level)
    over_y = [message_of(right[j], right_level) for j in range(1, n_y)]
    over_x, over_y = lax.optimization_barrier((over_x, over_y))
    panel_z, _ = lax.optimization_barrier((panel_z, (over_x, over_y)))
    from_x = swap(over_x, dx=1)
    from_y = [swap(over_y[j - 1], dy=j) for j in range(1, n_y)]
    from_x, from_y = lax.optimization_barrier((from_x, from_y))
    panel_level = functools.reduce(jnp.maximum, [level_of(p[0]) for p in panel_z])
    panel_level = panel_level + float(n_z.bit_length() - 1)
    panels = [
        message_of(pairwise([values_of(message[j]) for message in panel_z]), panel_level)
        for j in range(n_y)
    ]
    panel_y = [panels[0]] + [swap(panels[j], dy=j) for j in range(1, n_y)]
    panel_x = [swap(panels[j], dx=1, dy=j) for j in range(n_y)]
    left = left[:half] + values_of(from_x)
    left_level = jnp.maximum(left_level, level_of(from_x)) + 1.0
    right = functools.reduce(jnp.add, [values_of(message) for message in from_y], right[0])
    right_level = functools.reduce(
        jnp.maximum, [level_of(message) for message in from_y], right_level
    ) + grown

    total = jnp.concatenate([left, right], axis=1)
    level = jnp.concatenate([left_level, right_level], axis=1)
    over_z = [message_of(total[j * rows : (j + 1) * rows], level) for j in range(1, n_z)]
    from_z = [swap(over_z[j - 1], dz=j) for j in range(1, n_z)]
    panel_x, panel_y, _ = lax.optimization_barrier((panel_x, panel_y, over_z))
    panel = functools.reduce(jnp.add, [values_of(message) for message in panel_y])
    panel = panel + functools.reduce(jnp.add, [values_of(message) for message in panel_x])
    panel_factor = factor_panel(panel, kaula_prior)
    from_z, panel_factor = lax.optimization_barrier((from_z, panel_factor))
    normal_rows = functools.reduce(
        jnp.add, [values_of(message) for message in from_z], total[:rows]
    )
    return normal_rows[None], panel_factor[None]


def solution(mesh):
    in_specs = (
        P(AXES, None, None),
        P(AXES, None, None),
        P(AXES, None),
        P(AXES),
        P(AXES, None),
        P(),
        P("coef", None),
    )
    out_specs = (P("coef", "arc", None), P("coef", None, None))
    return jax.shard_map(
        per_device, mesh=mesh, in_specs=in_specs, out_specs=out_specs, check_vma=False
    )
```

```python
import functools

import jax
import jax.numpy as jnp
from jax import lax
from jax.experimental import pallas as pl
from jax.experimental.pallas import tpu as pltpu
from jax.sharding import PartitionSpec as P

OB = 512
KB = 256
P_SIZE = 128
STRIDE = OB // P_SIZE
WIDTH = OB + KB
PAIR = 2
TOP_LEVEL = 12.0
HEAD = 8
INNER = (((1,), (1,)), ((), ()))
AXES = ("arc", "coef")

LANES = 128
BLOCK = 8
GROUP = 2
FACTOR_GROUP = 4
FIRST = 4
TILE = 128
ROWS = (((1,), (0,)), ((), ()))
COLS = (((0,), (0,)), ((), ()))


def mm(a, b, dims=ROWS):
    return lax.dot_general(a, b, dims, preferred_element_type=jnp.float32)


def split3(value):
    high = value.astype(jnp.bfloat16)
    rest = value - high.astype(jnp.float32)
    middle = rest.astype(jnp.bfloat16)
    low = (rest - middle.astype(jnp.float32)).astype(jnp.bfloat16)
    return high, middle, low


def row_of(value, i):
    return jnp.broadcast_to(value[i : i + 1, :], (BLOCK, LANES))


def eliminate_group(rows, base, extra):
    sub = lax.broadcasted_iota(jnp.int32, (BLOCK, LANES), 0)
    lane = lax.broadcasted_iota(jnp.int32, (BLOCK, LANES), 1)
    count = len(rows)
    rows = rows + extra
    for q in range(count):
        half, at = divmod(base + BLOCK * q, LANES)
        factors = [
            [
                jnp.broadcast_to(row[half][:, at + j : at + j + 1], (BLOCK, LANES))
                for j in range(BLOCK)
            ]
            for row in rows
        ]
        inside = (lane >= at) & (lane < at + BLOCK)
        unit = (lane - at == sub).astype(jnp.float32)
        for r in range(len(rows)):
            rows[r][half] = jnp.where(inside, unit if r == q else 0.0, rows[r][half])
        columns, own = list(factors[q]), rows[q]
        a, b, d = row_of(columns[0], 0), row_of(columns[1], 0), row_of(columns[1], 1)
        for i in range(0, BLOCK, 2):
            scale = pl.reciprocal(a * d - b * b, approx=True)

            def step(value, i=i, a=a, b=b, d=d, scale=scale):
                first, second = row_of(value, i), row_of(value, i + 1)
                upper, lower = d * first - b * second, a * second - b * first
                new = value - (columns[i] * upper + columns[i + 1] * lower) * scale
                kept = jnp.where(sub == i + 1, lower * scale, new)
                return new, jnp.where(sub == i, upper * scale, kept)

            pairs = {j: step(columns[j]) for j in range(i + 2, BLOCK)}
            for h in range(len(own)):
                own[h] = step(own[h])[1]
            if i + 2 < BLOCK:
                one, two = pairs[i + 2][0], pairs[i + 3][0]
                a, b, d = row_of(one, i + 2), row_of(two, i + 2), row_of(two, i + 3)
            for j, pair in pairs.items():
                columns[j] = pair[1]
        for r in range(len(rows)):
            if r != q:
                for h in range(len(own)):
                    t = [factors[r][j] * row_of(own[h], j) for j in range(BLOCK)]
                    rows[r][h] = rows[r][h] - (
                        ((t[0] + t[1]) + (t[2] + t[3])) + ((t[4] + t[5]) + (t[6] + t[7]))
                    )
    return rows


def sweep_group(a_ref, base):
    n = a_ref.shape[0]
    depth = BLOCK * GROUP
    before = a_ref[base : base + depth, :]

    def blocks(start):
        return [
            [
                a_ref[start + BLOCK * r : start + BLOCK * (r + 1), LANES * h : LANES * (h + 1)]
                for h in range(n // LANES)
            ]
            for r in range(GROUP)
        ]

    def joined(rows):
        return jnp.concatenate([jnp.concatenate(row, axis=1) for row in rows], axis=0)

    after = base + depth
    ahead = after < n
    rows = eliminate_group(blocks(base), base, blocks(after) if ahead else [])
    following, after_rows = joined(rows[GROUP:]) if ahead else None, joined(rows[:GROUP])
    column = lax.broadcasted_iota(jnp.int32, (depth, n), 1)
    row = lax.broadcasted_iota(jnp.int32, (depth, n), 0)
    inside = (column >= base) & (column < base + depth)
    if following is not None:
        a_ref[after : after + depth, :] = jnp.where(inside, -following, following)
    before = jnp.where(inside, jnp.where(column - base == row, -1.0, 0.0), before)
    after_rows = jnp.where(inside, -after_rows, after_rows)
    u0, u1, u2 = split3(before)
    w0, w1, w2 = split3(after_rows)
    left = jnp.concatenate([u0, u0, u0, u1, u1, u2], axis=0).T
    right = jnp.concatenate([w0, w1, w2, w0, w1, w0], axis=0)

    def update(low, high):
        row = lax.broadcasted_iota(jnp.int32, (high - low, n), 0) + low
        column = lax.broadcasted_iota(jnp.int32, (high - low, n), 1)
        outside = ((row < base) | (row >= base + depth)) & (
            (column < base) | (column >= base + depth)
        )
        a_ref[low:high, :] = jnp.where(outside, a_ref[low:high, :], 0.0) - mm(left[low:high], right)

    for low, high in ((after + depth, n), (0, after)):
        if low < high:
            update(low, high)


def place_of():
    arc, coef = lax.axis_index("arc"), lax.axis_index("coef")
    return lax.div(arc, PAIR), lax.rem(arc, PAIR), lax.div(coef, PAIR), lax.rem(coef, PAIR)


def solve_rows(tile, gain_ref, local_rows):
    solved = (mm(tile, gain_ref[1], INNER) + mm(tile, gain_ref[0], INNER)).astype(jnp.bfloat16)
    return (tile.astype(jnp.float32) - mm(solved, local_rows)).astype(jnp.bfloat16)


def normal_kernel(count_ref, local_ref, rows_ref, normal_ref):
    n, m = local_ref.shape
    used = lax.broadcasted_iota(jnp.int32, (n, m), 1) < count_ref[0]
    rows_ref[...] = jnp.where(used, local_ref[...].astype(jnp.float32), 0.0).astype(jnp.bfloat16)
    normal_ref[...] = mm(rows_ref[...], rows_ref[...], INNER)


def sweep_kernel(prior_ref, normal_ref, work_ref):
    n = normal_ref.shape[0]
    row = lax.broadcasted_iota(jnp.int32, (n, n), 0)
    column = lax.broadcasted_iota(jnp.int32, (n, n), 1)
    prior = jnp.broadcast_to(prior_ref[...], (n, n))
    work_ref[...] = normal_ref[...] + jnp.where(row == column, prior, 0.0)
    for p in range(FIRST):
        sweep_group(work_ref, p * BLOCK * GROUP)


def local_kernel(
    n_y, count_ref, band_ref, owner_ref, rows_ref, begun_ref, global_ref,
    send_ref, own_ref, gain_ref, work_ref,
):
    n, m = rows_ref.shape
    owned = n_y * PAIR * OB
    mine = n_y * OB
    count = count_ref[0]
    _, _, y, core = place_of()
    work_ref[...] = begun_ref[...]
    lane = lax.broadcasted_iota(jnp.int32, (TILE, LANES), 1).astype(jnp.int16)
    used = lax.broadcasted_iota(jnp.int32, (TILE, m), 1) < count

    def gather_rows(t):
        position, part = divmod(t * TILE, OB)
        core_away, y_away = divmod(position, n_y)
        owner = (y ^ y_away) * PAIR + (core ^ core_away)
        wanted = []
        for r in range(TILE // LANES):
            at = part // LANES + r
            ids = owner_ref[owner, at : at + 1, :].astype(jnp.float32)
            ids = jnp.broadcast_to(ids, (LANES, LANES)).T
            wanted.append(ids.astype(jnp.int32).astype(jnp.int16))
        wanted = jnp.concatenate(wanted, axis=0)
        hot, nothing = [], jnp.zeros((TILE, LANES), jnp.bfloat16)
        for k in range(owned // LANES):
            sensed = band_ref[0, k * LANES // OB].astype(jnp.float32).astype(jnp.bfloat16)
            sensed = jnp.full((TILE, LANES), sensed)
            hot.append(jnp.where(wanted == lane + jnp.int16(k * LANES), sensed, nothing))
        got = mm(jnp.concatenate(hot, axis=1), global_ref[0:owned, :])
        got = jnp.where(used, got, 0.0).astype(jnp.bfloat16)
        if t * TILE < mine:
            own_ref[t * TILE : (t + 1) * TILE, :] = got
        else:
            send_ref[t * TILE - mine : (t + 1) * TILE - mine, :] = got

    steps = n // (BLOCK * GROUP) - FIRST
    tiles, fill = owned // TILE, steps - 2
    for p in range(steps):
        sweep_group(work_ref, (FIRST + p) * BLOCK * GROUP)
        for t in range(p * tiles // fill, min(tiles, (p + 1) * tiles // fill)):
            gather_rows(t)
    used = lax.broadcasted_iota(jnp.int32, (KB, m), 1) < count
    border = global_ref[owned:, :].astype(jnp.float32)
    send_ref[mine:, :] = jnp.where(used, border, 0.0).astype(jnp.bfloat16)

    local_rows = rows_ref[...]
    i0, i1, i2 = split3(-work_ref[...])
    gain = mm(i2, local_rows) + mm(i1, local_rows) + mm(i0, local_rows)
    for i, part in enumerate(split3(gain)[:2]):
        gain_ref[i] = part
    send_ref[...] = solve_rows(send_ref[...], gain_ref, local_rows)


def begin_normal(count, prior, local_rows):
    n, m = local_rows.shape
    array = pl.BlockSpec(memory_space=pltpu.VMEM)
    rows, normal = pl.pallas_call(
        normal_kernel,
        out_shape=(
            jax.ShapeDtypeStruct((n, m), jnp.bfloat16),
            jax.ShapeDtypeStruct((n, n), jnp.float32),
        ),
        in_specs=[pl.BlockSpec(memory_space=pltpu.SMEM), array],
        out_specs=(array, array),
        compiler_params=pltpu.CompilerParams(vmem_limit_bytes=16 * 1024 * 1024),
        cost_estimate=pl.CostEstimate(flops=10**9, bytes_accessed=0, transcendentals=0),
        name="normal",
    )(count, local_rows)
    begun = pl.pallas_call(
        sweep_kernel,
        out_shape=jax.ShapeDtypeStruct((n, n), jnp.float32),
        in_specs=[array, array],
        out_specs=array,
        compiler_params=pltpu.CompilerParams(vmem_limit_bytes=16 * 1024 * 1024),
        cost_estimate=pl.CostEstimate(flops=4 * 10**9, bytes_accessed=0, transcendentals=0),
        name="first_sweeps",
    )(prior, normal)
    return rows, begun


def reduce_rows(count, band, owners, rows, begun, global_rows, n_y):
    n, m = rows.shape
    scalar = pl.BlockSpec(memory_space=pltpu.SMEM)
    array = pl.BlockSpec(memory_space=pltpu.VMEM)
    shapes = ((n_y * OB + KB, m), (n_y * OB, m), (2, n, m))
    return pl.pallas_call(
        functools.partial(local_kernel, n_y),
        out_shape=tuple(jax.ShapeDtypeStruct(shape, jnp.bfloat16) for shape in shapes),
        in_specs=[scalar, scalar, array, array, array, array],
        out_specs=tuple(array for _ in shapes),
        scratch_shapes=[pltpu.VMEM((n, n), jnp.float32)],
        compiler_params=pltpu.CompilerParams(vmem_limit_bytes=24 * 1024 * 1024),
        name="reduce_rows",
    )(count, band, owners, rows, begun, global_rows)


def own_product_kernel(
    n_y, n_z, own_ref, send_ref, gain_ref, rows_ref, mine_ref, square_ref, side_ref, left
):
    z, x, _, _ = place_of()
    border = send_ref[n_y * OB :, :]
    local_rows = rows_ref[...]
    for t in range(n_y):
        tile = own_ref[t * OB : (t + 1) * OB, :]
        mine_ref[t * OB : (t + 1) * OB, :] = solve_rows(tile, gain_ref, local_rows)
    for y in range(n_y):
        for g in range(OB // LANES):
            low, high = g * LANES, (g + 1) * LANES
            rows = mine_ref[y * OB + low : y * OB + high, :]
            square_ref[y, low:high, :high] = mm(rows, mine_ref[y * OB : y * OB + high, :], INNER)
        order_rows(n_z, z, x, mine_ref, y, left)
        side_ref[y] = mm(left[...], border, INNER)


def order_rows(n_z, z, x, rows_ref, y, left):
    rows = OB // (n_z * PAIR)
    for i in range(PAIR):
        for j in range(n_z):
            at = (i * n_z + j) * rows
            source = pl.multiple_of(y * OB + ((z ^ j) * PAIR + (x ^ i)) * rows, rows)
            left[at : at + rows, :] = rows_ref[pl.ds(source, rows), :]


def lower_blocks():
    return [(g, t) for g in range(OB // LANES) for t in range(g + 1)]


def product_kernel(
    n_y, n_z, other_ref, square_ref, side_ref,
    keep_y_ref, send_y_ref, keep_x_ref, send_x_ref, level_ref, left, square, side,
):
    z, x, _, _ = place_of()
    half = OB // PAIR
    border = other_ref[n_y * OB :, :]
    top = jnp.zeros((BLOCK, LANES), jnp.float32)

    def raised(top, value):
        count = value.shape[0]
        value = jnp.abs(value).reshape(count // BLOCK, BLOCK, LANES)
        return jnp.maximum(top, jnp.max(value, axis=0))

    for y in range(n_y):
        for g in range(OB // LANES):
            low, high = g * LANES, (g + 1) * LANES
            rows = other_ref[y * OB + low : y * OB + high, :]
            square[y, low:high, :high] = square_ref[y, low:high, :high] + mm(
                rows, other_ref[y * OB : y * OB + high, :], INNER
            )
            for t in range(g + 1):
                top = raised(top, square[y, low:high, t * LANES : (t + 1) * LANES])
        order_rows(n_z, z, x, other_ref, y, left)
        side[y] = side_ref[y] + mm(left[...], border, INNER)
        for h in range(KB // LANES):
            top = raised(top, side[y, :, h * LANES : (h + 1) * LANES])
    top = jnp.max(jnp.max(top, axis=0, keepdims=True), axis=1, keepdims=True)
    level = jnp.floor(jnp.log2(jnp.maximum(jnp.broadcast_to(top, (BLOCK, OB)), 1e-30)))
    level_ref[...] = level
    scale = jnp.exp2(TOP_LEVEL - level[:1, :KB])
    for j in range(1, n_y):
        send_y_ref[j - 1, :HEAD, :] = jnp.broadcast_to(level[:1, :LANES], (HEAD, LANES))
    for i, (g, t) in enumerate(lower_blocks()):
        rows, columns = slice(g * LANES, (g + 1) * LANES), slice(t * LANES, (t + 1) * LANES)
        keep_y_ref[i * LANES : (i + 1) * LANES, :] = square[0, rows, columns]
        for j in range(1, n_y):
            at = HEAD + i * LANES
            send_y_ref[j - 1, at : at + LANES, :] = square[j, rows, columns] * scale[:, :LANES]
    send_x_ref[:HEAD, :] = jnp.broadcast_to(level[:1, :KB], (HEAD, KB))
    for y in range(n_y):
        keep_x_ref[y] = side[y, :half, :]
        at = HEAD + y * half
        send_x_ref[at : at + half, :] = side[y, half:, :] * scale


def expand_kernel(n_z, packed_ref, out_ref):
    z, x, _, _ = place_of()
    rows = OB // (n_z * PAIR)
    place = {pair: i for i, pair in enumerate(lower_blocks())}
    for g in range(OB // LANES):
        for t in range(OB // LANES):
            at = place[max(g, t), min(g, t)] * LANES
            block = packed_ref[at : at + LANES, :]
            block = block if t <= g else block.T
            for b in range(LANES // rows):
                arc = g * (LANES // rows) + b
                to = (((arc % PAIR) ^ x) * n_z + ((arc // PAIR) ^ z)) * rows
                to = pl.multiple_of(to, rows)
                out_ref[pl.ds(to, rows), t * LANES : (t + 1) * LANES] = block[
                    b * rows : (b + 1) * rows, :
                ]


def panel_kernel(n_y, mine_ref, other_ref, level_ref, out_ref):
    pick = lax.broadcasted_iota(jnp.int32, (P_SIZE, OB), 1) == STRIDE * lax.broadcasted_iota(
        jnp.int32, (P_SIZE, OB), 0
    )
    pick = pick.astype(jnp.float32).astype(jnp.bfloat16)
    level = level_ref[:1, :P_SIZE]
    scale = jnp.exp2(TOP_LEVEL - level)
    half = P_SIZE // 2
    row = lax.broadcasted_iota(jnp.int32, (half, P_SIZE), 0)
    column = lax.broadcasted_iota(jnp.int32, (half, P_SIZE), 1) - half
    for y in range(n_y):
        panel = jnp.zeros((P_SIZE, P_SIZE), jnp.float32)
        for ref in (mine_ref, other_ref):
            strip = mm(pick, ref[y * OB : (y + 1) * OB, :]).astype(jnp.bfloat16)
            panel = panel + mm(strip, strip, INNER)
        upper, lower = panel[:half], panel[half:]
        corner = jnp.where(row >= column, pltpu.roll(upper, half, 1), lower)
        spare = jnp.sum(jnp.where(row == column, lower, 0.0), axis=0, keepdims=True)
        out_ref[y, :HEAD, :] = jnp.broadcast_to(level, (HEAD, P_SIZE))
        out_ref[y, HEAD : HEAD + half, :] = jnp.where(column < 0, lower, corner) * scale
        out_ref[y, HEAD + half :, :] = jnp.broadcast_to(spare * scale, (BLOCK, P_SIZE))


def own_products(own, send, gain, rows, n_y, n_z):
    array = pl.BlockSpec(memory_space=pltpu.VMEM)
    m = own.shape[1]
    return pl.pallas_call(
        functools.partial(own_product_kernel, n_y, n_z),
        out_shape=(
            jax.ShapeDtypeStruct(own.shape, jnp.bfloat16),
            jax.ShapeDtypeStruct((n_y, OB, OB), jnp.float32),
            jax.ShapeDtypeStruct((n_y, OB, KB), jnp.float32),
        ),
        in_specs=[array, array, array, array],
        out_specs=(array, array, array),
        scratch_shapes=[pltpu.VMEM((OB, m), jnp.bfloat16)],
        compiler_params=pltpu.CompilerParams(vmem_limit_bytes=24 * 1024 * 1024),
        cost_estimate=pl.CostEstimate(
            flops=4 * n_y * OB * WIDTH * m, bytes_accessed=0, transcendentals=0
        ),
        name="own_products",
    )(own, send, gain, rows)


def products(other, square, side, n_y, n_z):
    array = pl.BlockSpec(memory_space=pltpu.VMEM)
    m = other.shape[1]
    half, packed = OB // PAIR, len(lower_blocks()) * LANES
    shapes = (
        (packed, LANES),
        (n_y - 1, HEAD + packed, LANES),
        (n_y, half, KB),
        (HEAD + n_y * half, KB),
        (BLOCK, OB),
    )
    return pl.pallas_call(
        functools.partial(product_kernel, n_y, n_z),
        out_shape=tuple(jax.ShapeDtypeStruct(shape, jnp.float32) for shape in shapes),
        in_specs=[array, array, array],
        out_specs=tuple(array for _ in shapes),
        scratch_shapes=[
            pltpu.VMEM((OB, m), jnp.bfloat16),
            pltpu.VMEM((n_y, OB, OB), jnp.float32),
            pltpu.VMEM((n_y, OB, KB), jnp.float32),
        ],
        compiler_params=pltpu.CompilerParams(vmem_limit_bytes=24 * 1024 * 1024),
        name="products",
    )(other, square, side)


def expand(packed, n_z):
    array = pl.BlockSpec(memory_space=pltpu.VMEM)
    return pl.pallas_call(
        functools.partial(expand_kernel, n_z),
        out_shape=jax.ShapeDtypeStruct((OB, OB), jnp.float32),
        in_specs=[array],
        out_specs=array,
        compiler_params=pltpu.CompilerParams(vmem_limit_bytes=8 * 1024 * 1024),
        name="expand",
    )(packed)


def panel_products(mine, other, level, n_y):
    array = pl.BlockSpec(memory_space=pltpu.VMEM)
    return pl.pallas_call(
        functools.partial(panel_kernel, n_y),
        out_shape=jax.ShapeDtypeStruct((n_y, HEAD + P_SIZE // 2 + BLOCK, P_SIZE), jnp.float32),
        in_specs=[array, array, array],
        out_specs=array,
        cost_estimate=pl.CostEstimate(
            flops=4 * n_y * P_SIZE * OB * mine.shape[1], bytes_accessed=0, transcendentals=0
        ),
        compiler_params=pltpu.CompilerParams(vmem_limit_bytes=8 * 1024 * 1024),
        name="panel_products",
    )(mine, other, level)


def factor_group(rows, base):
    sub = lax.broadcasted_iota(jnp.int32, (BLOCK, LANES), 0)
    count = len(rows)
    for q in range(count):
        at = base + BLOCK * q
        factors = [
            [
                jnp.broadcast_to(rows[r][:, at + j : at + j + 1], (BLOCK, LANES))
                for j in range(BLOCK)
            ]
            for r in range(q, count)
        ]
        columns, own = factors[0], rows[q]
        scales, entries = [], []
        for i in range(BLOCK):
            pivot = row_of(columns[i], i)
            scale = lax.rsqrt(pivot)
            scale = scale * (1.5 - 0.5 * pivot * scale * scale)
            scales.append(scale)
            scaled = row_of(own, i) * scale
            step = columns[i] * scale
            own = jnp.where(sub == i, scaled, jnp.where(sub > i, own - step * scaled, own))
            entries.append([row_of(columns[j], i) * scale for j in range(BLOCK)])
            for j in range(i + 1, BLOCK):
                columns[j] = columns[j] - step * entries[i][j]
        rows[q] = own
        for r in range(q + 1, count):
            value = rows[r]
            below = list(factors[r - q])
            for i in range(BLOCK):
                step = below[i] * scales[i]
                value = value - step * row_of(own, i)
                for j in range(i + 1, BLOCK):
                    below[j] = below[j] - step * entries[i][j]
            rows[r] = value
    return rows


def factor_kernel(panel_ref, prior_ref, out_ref, work_ref):
    n = work_ref.shape[0]
    depth = BLOCK * FACTOR_GROUP
    row = lax.broadcasted_iota(jnp.int32, (n, n), 0)
    column = lax.broadcasted_iota(jnp.int32, (n, n), 1)
    prior = jnp.broadcast_to(prior_ref[...], (n, n))
    half = n // 2
    packed, spare = panel_ref[:half, :], panel_ref[half : half + 1, :]
    diagonal = column[:half] - half == row[:half]
    whole = jnp.concatenate(
        [pltpu.roll(packed, half, 1), jnp.where(diagonal, spare, packed)], axis=0
    )
    known = ((row < half) & (column < half) & (row >= column)) | (
        (row >= half) & ((column < half) | (row <= column))
    )
    whole = jnp.where(known, whole, whole.T)
    work_ref[...] = whole + jnp.where(row == column, prior, 0.0)
    for p in range(n // depth):
        base = p * depth
        rows = [
            work_ref[base + BLOCK * r : base + BLOCK * (r + 1), :] for r in range(FACTOR_GROUP)
        ]
        done = jnp.concatenate(factor_group(rows, base), axis=0)
        work_ref[base : base + depth, :] = done
        if base + depth < n:
            d0, d1, d2 = split3(done)
            update = mm(
                jnp.concatenate([d0, d0, d0, d1, d1, d2], axis=0),
                jnp.concatenate([d0, d1, d2, d0, d1, d0], axis=0),
                COLS,
            )
            work_ref[base + depth :, :] = work_ref[base + depth :, :] - update[base + depth :, :]
    out_ref[...] = jnp.where(row <= column, work_ref[...], 0.0).T


def factor_panel(panel, prior):
    n = panel.shape[1]
    return pl.pallas_call(
        factor_kernel,
        out_shape=jax.ShapeDtypeStruct((n, n), jnp.float32),
        scratch_shapes=[pltpu.VMEM((n, n), jnp.float32)],
        cost_estimate=pl.CostEstimate(flops=n**3, bytes_accessed=12 * n * n, transcendentals=n),
        compiler_params=pltpu.CompilerParams(vmem_limit_bytes=8 * 1024 * 1024),
        name="factor_panel",
    )(panel, prior)


def level_of(message):
    return message[:1].astype(jnp.float32)


def values_of(message):
    return message[HEAD:].astype(jnp.float32) * jnp.exp2(level_of(message) - TOP_LEVEL)


def message_of(values, level):
    head = jnp.broadcast_to(level, (HEAD, values.shape[1]))
    return jnp.concatenate([head, values * jnp.exp2(TOP_LEVEL - level)]).astype(jnp.float16)


def pairwise(terms):
    while len(terms) > 1:
        terms = [terms[2 * i] + terms[2 * i + 1] for i in range(len(terms) // 2)]
    return terms[0]


def per_device(
    local_design, global_design, local_prior, obs_count, band_mask, owner_columns, kaula_prior
):
    n_arc, n_coef = lax.axis_size("arc"), lax.axis_size("coef")
    n_z, n_y = n_arc // PAIR, n_coef // PAIR
    rows = OB // n_arc
    def swap(values, dz=0, dx=0, dy=0, dk=0):
        pairs = []
        for a in range(n_arc):
            for c in range(n_coef):
                to_a = ((a // PAIR) ^ dz) * PAIR + ((a % PAIR) ^ dx)
                to_c = ((c // PAIR) ^ dy) * PAIR + ((c % PAIR) ^ dk)
                pairs.append((a * n_coef + c, to_a * n_coef + to_c))
        return lax.ppermute(values, AXES, pairs)

    local_rows, begun = begin_normal(obs_count, local_prior, local_design[0])
    send, own, gain = reduce_rows(
        obs_count,
        band_mask,
        owner_columns.reshape(n_coef, OB // LANES, LANES),
        local_rows,
        begun,
        global_design[0],
        n_y,
    )
    other = swap(send, dk=1)
    mine, square, side = own_products(own, send, gain, local_rows, n_y, n_z)
    keep_y, send_y, keep_x, send_x, level = products(other, square, side, n_y, n_z)
    half = OB // PAIR
    grown = float(n_y.bit_length() - 1)

    from_y = [swap(send_y[j - 1].astype(jnp.float16), dy=j) for j in range(1, n_y)]
    from_x = swap(send_x.astype(jnp.float16), dx=1)
    panels = panel_products(mine, other, level, n_y).astype(jnp.float16)
    panel_z = [panels] + [swap(panels, dz=j) for j in range(1, n_z)]

    from_y, from_x = lax.optimization_barrier((from_y, from_x))
    packed = functools.reduce(jnp.add, [values_of(message) for message in from_y], keep_y)
    left_level = functools.reduce(
        jnp.maximum, [level_of(message) for message in from_y], level[:1, :LANES]
    ) + grown
    left_level = jnp.concatenate([left_level] * (OB // LANES), axis=1)
    left = expand(packed, n_z)
    right = keep_x + values_of(from_x).reshape(n_y, half, KB)
    right_level = jnp.maximum(level[:1, :KB], level_of(from_x)) + 1.0

    over_x = message_of(left[half:], left_level)
    over_y = [message_of(right[j], right_level) for j in range(1, n_y)]
    over_x, over_y = lax.optimization_barrier((over_x, over_y))
    panel_z, _ = lax.optimization_barrier((panel_z, (over_x, over_y)))
    from_x = swap(over_x, dx=1)
    from_y = [swap(over_y[j - 1], dy=j) for j in range(1, n_y)]
    from_x, from_y = lax.optimization_barrier((from_x, from_y))
    panel_level = functools.reduce(jnp.maximum, [level_of(p[0]) for p in panel_z])
    panel_level = panel_level + float(n_z.bit_length() - 1)
    panels = [
        message_of(pairwise([values_of(message[j]) for message in panel_z]), panel_level)
        for j in range(n_y)
    ]
    panel_y = [panels[0]] + [swap(panels[j], dy=j) for j in range(1, n_y)]
    panel_x = [swap(panels[j], dx=1, dy=j) for j in range(n_y)]
    left = left[:half] + values_of(from_x)
    left_level = jnp.maximum(left_level, level_of(from_x)) + 1.0
    right = functools.reduce(jnp.add, [values_of(message) for message in from_y], right[0])
    right_level = functools.reduce(
        jnp.maximum, [level_of(message) for message in from_y], right_level
    ) + grown

    total = jnp.concatenate([left, right], axis=1)
    level = jnp.concatenate([left_level, right_level], axis=1)
    over_z = [message_of(total[j * rows : (j + 1) * rows], level) for j in range(1, n_z)]
    over_z = lax.optimization_barrier(over_z)
    from_z = [swap(over_z[j - 1], dz=j) for j in range(1, n_z)]
    *from_z, from_near = from_z[1:] + from_z[:1]
    panel_x, panel_y, _ = lax.optimization_barrier((panel_x, panel_y, over_z))
    panel = functools.reduce(jnp.add, [values_of(message) for message in panel_y])
    panel = panel + functools.reduce(jnp.add, [values_of(message) for message in panel_x])
    panel_factor = factor_panel(panel, kaula_prior)
    from_z, panel_factor = lax.optimization_barrier((from_z + [from_near], panel_factor))
    normal_rows = functools.reduce(
        jnp.add, [values_of(message) for message in from_z], total[:rows]
    )
    return normal_rows[None], panel_factor[None]


def solution(mesh):
    in_specs = (
        P(AXES, None, None),
        P(AXES, None, None),
        P(AXES, None),
        P(AXES),
        P(AXES, None),
        P(),
        P("coef", None),
    )
    out_specs = (P("coef", "arc", None), P("coef", None, None))
    return jax.shard_map(
        per_device, mesh=mesh, in_specs=in_specs, out_specs=out_specs, check_vma=False
    )
```

```python
import functools

import jax
import jax.numpy as jnp
from jax import lax
from jax.experimental import pallas as pl
from jax.experimental.pallas import tpu as pltpu
from jax.sharding import PartitionSpec as P

OB = 512
KB = 256
P_SIZE = 128
STRIDE = OB // P_SIZE
WIDTH = OB + KB
PAIR = 2
TOP_LEVEL = 12.0
HEAD = 8
INNER = (((1,), (1,)), ((), ()))
AXES = ("arc", "coef")

LANES = 128
BLOCK = 8
GROUP = 2
FACTOR_GROUP = 4
FIRST = 4
TILE = 128
ROWS = (((1,), (0,)), ((), ()))
COLS = (((0,), (0,)), ((), ()))


def mm(a, b, dims=ROWS):
    return lax.dot_general(a, b, dims, preferred_element_type=jnp.float32)


def split3(value):
    high = value.astype(jnp.bfloat16)
    rest = value - high.astype(jnp.float32)
    middle = rest.astype(jnp.bfloat16)
    low = (rest - middle.astype(jnp.float32)).astype(jnp.bfloat16)
    return high, middle, low


def row_of(value, i):
    return jnp.broadcast_to(value[i : i + 1, :], (BLOCK, LANES))


def eliminate_group(rows, base, extra):
    sub = lax.broadcasted_iota(jnp.int32, (BLOCK, LANES), 0)
    lane = lax.broadcasted_iota(jnp.int32, (BLOCK, LANES), 1)
    count = len(rows)
    rows = rows + extra
    for q in range(count):
        half, at = divmod(base + BLOCK * q, LANES)
        factors = [
            [
                jnp.broadcast_to(row[half][:, at + j : at + j + 1], (BLOCK, LANES))
                for j in range(BLOCK)
            ]
            for row in rows
        ]
        inside = (lane >= at) & (lane < at + BLOCK)
        unit = (lane - at == sub).astype(jnp.float32)
        for r in range(len(rows)):
            rows[r][half] = jnp.where(inside, unit if r == q else 0.0, rows[r][half])
        columns, own = list(factors[q]), rows[q]
        a, b, d = row_of(columns[0], 0), row_of(columns[1], 0), row_of(columns[1], 1)
        for i in range(0, BLOCK, 2):
            scale = pl.reciprocal(a * d - b * b, approx=True)

            def step(value, i=i, a=a, b=b, d=d, scale=scale):
                first, second = row_of(value, i), row_of(value, i + 1)
                upper, lower = d * first - b * second, a * second - b * first
                new = value - (columns[i] * upper + columns[i + 1] * lower) * scale
                kept = jnp.where(sub == i + 1, lower * scale, new)
                return new, jnp.where(sub == i, upper * scale, kept)

            pairs = {j: step(columns[j]) for j in range(i + 2, BLOCK)}
            for h in range(len(own)):
                own[h] = step(own[h])[1]
            if i + 2 < BLOCK:
                one, two = pairs[i + 2][0], pairs[i + 3][0]
                a, b, d = row_of(one, i + 2), row_of(two, i + 2), row_of(two, i + 3)
            for j, pair in pairs.items():
                columns[j] = pair[1]
        for r in range(len(rows)):
            if r != q:
                for h in range(len(own)):
                    t = [factors[r][j] * row_of(own[h], j) for j in range(BLOCK)]
                    rows[r][h] = rows[r][h] - (
                        ((t[0] + t[1]) + (t[2] + t[3])) + ((t[4] + t[5]) + (t[6] + t[7]))
                    )
    return rows


def sweep_group(a_ref, base):
    n = a_ref.shape[0]
    depth = BLOCK * GROUP
    before = a_ref[base : base + depth, :]

    def blocks(start):
        return [
            [
                a_ref[start + BLOCK * r : start + BLOCK * (r + 1), LANES * h : LANES * (h + 1)]
                for h in range(n // LANES)
            ]
            for r in range(GROUP)
        ]

    def joined(rows):
        return jnp.concatenate([jnp.concatenate(row, axis=1) for row in rows], axis=0)

    after = base + depth
    ahead = after < n
    rows = eliminate_group(blocks(base), base, blocks(after) if ahead else [])
    following, after_rows = joined(rows[GROUP:]) if ahead else None, joined(rows[:GROUP])
    column = lax.broadcasted_iota(jnp.int32, (depth, n), 1)
    row = lax.broadcasted_iota(jnp.int32, (depth, n), 0)
    inside = (column >= base) & (column < base + depth)
    if following is not None:
        a_ref[after : after + depth, :] = jnp.where(inside, -following, following)
    before = jnp.where(inside, jnp.where(column - base == row, -1.0, 0.0), before)
    after_rows = jnp.where(inside, -after_rows, after_rows)
    u0, u1, u2 = split3(before)
    w0, w1, w2 = split3(after_rows)
    left = jnp.concatenate([u0, u0, u0, u1, u1, u2], axis=0).T
    right = jnp.concatenate([w0, w1, w2, w0, w1, w0], axis=0)

    def update(low, high):
        row = lax.broadcasted_iota(jnp.int32, (high - low, n), 0) + low
        column = lax.broadcasted_iota(jnp.int32, (high - low, n), 1)
        outside = ((row < base) | (row >= base + depth)) & (
            (column < base) | (column >= base + depth)
        )
        a_ref[low:high, :] = jnp.where(outside, a_ref[low:high, :], 0.0) - mm(left[low:high], right)

    for low, high in ((after + depth, n), (0, after)):
        if low < high:
            update(low, high)


def place_of():
    arc, coef = lax.axis_index("arc"), lax.axis_index("coef")
    return lax.div(arc, PAIR), lax.rem(arc, PAIR), lax.div(coef, PAIR), lax.rem(coef, PAIR)


def solve_rows(tile, gain_ref, local_rows):
    solved = (mm(tile, gain_ref[1], INNER) + mm(tile, gain_ref[0], INNER)).astype(jnp.bfloat16)
    return (tile.astype(jnp.float32) - mm(solved, local_rows)).astype(jnp.bfloat16)


def normal_kernel(count_ref, local_ref, rows_ref, normal_ref):
    n, m = local_ref.shape
    used = lax.broadcasted_iota(jnp.int32, (n, m), 1) < count_ref[0]
    rows_ref[...] = jnp.where(used, local_ref[...].astype(jnp.float32), 0.0).astype(jnp.bfloat16)
    normal_ref[...] = mm(rows_ref[...], rows_ref[...], INNER)


def sweep_kernel(prior_ref, normal_ref, work_ref):
    n = normal_ref.shape[0]
    row = lax.broadcasted_iota(jnp.int32, (n, n), 0)
    column = lax.broadcasted_iota(jnp.int32, (n, n), 1)
    prior = jnp.broadcast_to(prior_ref[...], (n, n))
    work_ref[...] = normal_ref[...] + jnp.where(row == column, prior, 0.0)
    for p in range(FIRST):
        sweep_group(work_ref, p * BLOCK * GROUP)


def local_kernel(
    n_y, count_ref, band_ref, owner_ref, rows_ref, begun_ref, global_ref,
    send_ref, own_ref, gain_ref, work_ref,
):
    n, m = rows_ref.shape
    owned = n_y * PAIR * OB
    mine = n_y * OB
    count = count_ref[0]
    _, _, y, core = place_of()
    work_ref[...] = begun_ref[...]
    lane = lax.broadcasted_iota(jnp.int32, (TILE, LANES), 1).astype(jnp.int16)
    used = lax.broadcasted_iota(jnp.int32, (TILE, m), 1) < count

    def gather_rows(t):
        position, part = divmod(t * TILE, OB)
        core_away, y_away = divmod(position, n_y)
        owner = (y ^ y_away) * PAIR + (core ^ core_away)
        wanted = []
        for r in range(TILE // LANES):
            at = part // LANES + r
            ids = owner_ref[owner, at : at + 1, :].astype(jnp.float32)
            ids = jnp.broadcast_to(ids, (LANES, LANES)).T
            wanted.append(ids.astype(jnp.int32).astype(jnp.int16))
        wanted = jnp.concatenate(wanted, axis=0)
        hot, nothing = [], jnp.zeros((TILE, LANES), jnp.bfloat16)
        for k in range(owned // LANES):
            sensed = band_ref[0, k * LANES // OB].astype(jnp.float32).astype(jnp.bfloat16)
            sensed = jnp.full((TILE, LANES), sensed)
            hot.append(jnp.where(wanted == lane + jnp.int16(k * LANES), sensed, nothing))
        got = mm(jnp.concatenate(hot, axis=1), global_ref[0:owned, :])
        got = jnp.where(used, got, 0.0).astype(jnp.bfloat16)
        if t * TILE < mine:
            own_ref[t * TILE : (t + 1) * TILE, :] = got
        else:
            send_ref[t * TILE - mine : (t + 1) * TILE - mine, :] = got

    steps = n // (BLOCK * GROUP) - FIRST
    tiles, fill = owned // TILE, steps - 2
    for p in range(steps):
        sweep_group(work_ref, (FIRST + p) * BLOCK * GROUP)
        for t in range(p * tiles // fill, min(tiles, (p + 1) * tiles // fill)):
            gather_rows(t)
    used = lax.broadcasted_iota(jnp.int32, (KB, m), 1) < count
    border = global_ref[owned:, :].astype(jnp.float32)
    send_ref[mine:, :] = jnp.where(used, border, 0.0).astype(jnp.bfloat16)

    local_rows = rows_ref[...]
    i0, i1, i2 = split3(-work_ref[...])
    gain = mm(i2, local_rows) + mm(i1, local_rows) + mm(i0, local_rows)
    for i, part in enumerate(split3(gain)[:2]):
        gain_ref[i] = part
    send_ref[...] = solve_rows(send_ref[...], gain_ref, local_rows)


def begin_normal(count, prior, local_rows):
    n, m = local_rows.shape
    array = pl.BlockSpec(memory_space=pltpu.VMEM)
    rows, normal = pl.pallas_call(
        normal_kernel,
        out_shape=(
            jax.ShapeDtypeStruct((n, m), jnp.bfloat16),
            jax.ShapeDtypeStruct((n, n), jnp.float32),
        ),
        in_specs=[pl.BlockSpec(memory_space=pltpu.SMEM), array],
        out_specs=(array, array),
        compiler_params=pltpu.CompilerParams(vmem_limit_bytes=16 * 1024 * 1024),
        cost_estimate=pl.CostEstimate(flops=10**9, bytes_accessed=0, transcendentals=0),
        name="normal",
    )(count, local_rows)
    begun = pl.pallas_call(
        sweep_kernel,
        out_shape=jax.ShapeDtypeStruct((n, n), jnp.float32),
        in_specs=[array, array],
        out_specs=array,
        compiler_params=pltpu.CompilerParams(vmem_limit_bytes=16 * 1024 * 1024),
        cost_estimate=pl.CostEstimate(flops=4 * 10**9, bytes_accessed=0, transcendentals=0),
        name="first_sweeps",
    )(prior, normal)
    return rows, begun


def reduce_rows(count, band, owners, rows, begun, global_rows, n_y):
    n, m = rows.shape
    scalar = pl.BlockSpec(memory_space=pltpu.SMEM)
    array = pl.BlockSpec(memory_space=pltpu.VMEM)
    shapes = ((n_y * OB + KB, m), (n_y * OB, m), (2, n, m))
    return pl.pallas_call(
        functools.partial(local_kernel, n_y),
        out_shape=tuple(jax.ShapeDtypeStruct(shape, jnp.bfloat16) for shape in shapes),
        in_specs=[scalar, scalar, array, array, array, array],
        out_specs=tuple(array for _ in shapes),
        scratch_shapes=[pltpu.VMEM((n, n), jnp.float32)],
        compiler_params=pltpu.CompilerParams(vmem_limit_bytes=24 * 1024 * 1024),
        name="reduce_rows",
    )(count, band, owners, rows, begun, global_rows)


def own_product_kernel(
    n_y, n_z, own_ref, send_ref, gain_ref, rows_ref, mine_ref, square_ref, side_ref, left
):
    z, x, _, _ = place_of()
    border = send_ref[n_y * OB :, :]
    local_rows = rows_ref[...]
    for t in range(n_y):
        tile = own_ref[t * OB : (t + 1) * OB, :]
        mine_ref[t * OB : (t + 1) * OB, :] = solve_rows(tile, gain_ref, local_rows)
    for y in range(n_y):
        for g in range(OB // LANES):
            low, high = g * LANES, (g + 1) * LANES
            rows = mine_ref[y * OB + low : y * OB + high, :]
            square_ref[y, low:high, :high] = mm(rows, mine_ref[y * OB : y * OB + high, :], INNER)
        order_rows(n_z, z, x, mine_ref, y, left)
        side_ref[y] = mm(left[...], border, INNER)


def order_rows(n_z, z, x, rows_ref, y, left):
    rows = OB // (n_z * PAIR)
    for i in range(PAIR):
        for j in range(n_z):
            at = (i * n_z + j) * rows
            source = pl.multiple_of(y * OB + ((z ^ j) * PAIR + (x ^ i)) * rows, rows)
            left[at : at + rows, :] = rows_ref[pl.ds(source, rows), :]


def lower_blocks():
    return [(g, t) for g in range(OB // LANES) for t in range(g + 1)]


def product_kernel(
    n_y, n_z, other_ref, square_ref, side_ref,
    keep_y_ref, send_y_ref, keep_x_ref, send_x_ref, level_ref, left, square, side,
):
    z, x, _, _ = place_of()
    half = OB // PAIR
    border = other_ref[n_y * OB :, :]
    top = jnp.zeros((BLOCK, LANES), jnp.float32)

    def raised(top, value):
        count = value.shape[0]
        value = jnp.abs(value).reshape(count // BLOCK, BLOCK, LANES)
        return jnp.maximum(top, jnp.max(value, axis=0))

    for y in range(n_y):
        for g in range(OB // LANES):
            low, high = g * LANES, (g + 1) * LANES
            rows = other_ref[y * OB + low : y * OB + high, :]
            square[y, low:high, :high] = square_ref[y, low:high, :high] + mm(
                rows, other_ref[y * OB : y * OB + high, :], INNER
            )
            for t in range(g + 1):
                top = raised(top, square[y, low:high, t * LANES : (t + 1) * LANES])
        order_rows(n_z, z, x, other_ref, y, left)
        side[y] = side_ref[y] + mm(left[...], border, INNER)
        for h in range(KB // LANES):
            top = raised(top, side[y, :, h * LANES : (h + 1) * LANES])
    top = jnp.max(jnp.max(top, axis=0, keepdims=True), axis=1, keepdims=True)
    level = jnp.floor(jnp.log2(jnp.maximum(jnp.broadcast_to(top, (BLOCK, OB)), 1e-30)))
    level_ref[...] = level
    scale = jnp.exp2(TOP_LEVEL - level[:1, :KB])
    for j in range(1, n_y):
        send_y_ref[j - 1, :HEAD, :] = jnp.broadcast_to(level[:1, :LANES], (HEAD, LANES))
    for i, (g, t) in enumerate(lower_blocks()):
        rows, columns = slice(g * LANES, (g + 1) * LANES), slice(t * LANES, (t + 1) * LANES)
        keep_y_ref[i * LANES : (i + 1) * LANES, :] = square[0, rows, columns]
        for j in range(1, n_y):
            at = HEAD + i * LANES
            send_y_ref[j - 1, at : at + LANES, :] = square[j, rows, columns] * scale[:, :LANES]
    send_x_ref[:HEAD, :] = jnp.broadcast_to(level[:1, :KB], (HEAD, KB))
    for y in range(n_y):
        keep_x_ref[y] = side[y, :half, :]
        at = HEAD + y * half
        send_x_ref[at : at + half, :] = side[y, half:, :] * scale


def expand_kernel(n_z, packed_ref, level_ref, out_ref, send_ref):
    z, x, _, _ = place_of()
    rows = OB // (n_z * PAIR)
    place = {pair: i for i, pair in enumerate(lower_blocks())}
    for g in range(OB // LANES):
        for t in range(OB // LANES):
            at = place[max(g, t), min(g, t)] * LANES
            block = packed_ref[at : at + LANES, :]
            block = block if t <= g else block.T
            for b in range(LANES // rows):
                arc = g * (LANES // rows) + b
                to = (((arc % PAIR) ^ x) * n_z + ((arc // PAIR) ^ z)) * rows
                to = pl.multiple_of(to, rows)
                out_ref[pl.ds(to, rows), t * LANES : (t + 1) * LANES] = block[
                    b * rows : (b + 1) * rows, :
                ]
    level = level_ref[:1, :]
    send_ref[:HEAD, :] = jnp.broadcast_to(level, (HEAD, OB))
    send_ref[HEAD:, :] = out_ref[OB // PAIR :, :] * jnp.exp2(TOP_LEVEL - level)


def panel_kernel(n_y, mine_ref, other_ref, level_ref, out_ref):
    pick = lax.broadcasted_iota(jnp.int32, (P_SIZE, OB), 1) == STRIDE * lax.broadcasted_iota(
        jnp.int32, (P_SIZE, OB), 0
    )
    pick = pick.astype(jnp.float32).astype(jnp.bfloat16)
    level = level_ref[:1, :P_SIZE]
    scale = jnp.exp2(TOP_LEVEL - level)
    half = P_SIZE // 2
    row = lax.broadcasted_iota(jnp.int32, (half, P_SIZE), 0)
    column = lax.broadcasted_iota(jnp.int32, (half, P_SIZE), 1) - half
    for y in range(n_y):
        panel = jnp.zeros((P_SIZE, P_SIZE), jnp.float32)
        for ref in (mine_ref, other_ref):
            strip = mm(pick, ref[y * OB : (y + 1) * OB, :]).astype(jnp.bfloat16)
            panel = panel + mm(strip, strip, INNER)
        upper, lower = panel[:half], panel[half:]
        corner = jnp.where(row >= column, pltpu.roll(upper, half, 1), lower)
        spare = jnp.sum(jnp.where(row == column, lower, 0.0), axis=0, keepdims=True)
        out_ref[y, :HEAD, :] = jnp.broadcast_to(level, (HEAD, P_SIZE))
        out_ref[y, HEAD : HEAD + half, :] = jnp.where(column < 0, lower, corner) * scale
        out_ref[y, HEAD + half :, :] = jnp.broadcast_to(spare * scale, (BLOCK, P_SIZE))


def own_products(own, send, gain, rows, n_y, n_z):
    array = pl.BlockSpec(memory_space=pltpu.VMEM)
    m = own.shape[1]
    return pl.pallas_call(
        functools.partial(own_product_kernel, n_y, n_z),
        out_shape=(
            jax.ShapeDtypeStruct(own.shape, jnp.bfloat16),
            jax.ShapeDtypeStruct((n_y, OB, OB), jnp.float32),
            jax.ShapeDtypeStruct((n_y, OB, KB), jnp.float32),
        ),
        in_specs=[array, array, array, array],
        out_specs=(array, array, array),
        scratch_shapes=[pltpu.VMEM((OB, m), jnp.bfloat16)],
        compiler_params=pltpu.CompilerParams(vmem_limit_bytes=24 * 1024 * 1024),
        cost_estimate=pl.CostEstimate(
            flops=4 * n_y * OB * WIDTH * m, bytes_accessed=0, transcendentals=0
        ),
        name="own_products",
    )(own, send, gain, rows)


def products(other, square, side, n_y, n_z):
    array = pl.BlockSpec(memory_space=pltpu.VMEM)
    m = other.shape[1]
    half, packed = OB // PAIR, len(lower_blocks()) * LANES
    shapes = (
        (packed, LANES),
        (n_y - 1, HEAD + packed, LANES),
        (n_y, half, KB),
        (HEAD + n_y * half, KB),
        (BLOCK, OB),
    )
    return pl.pallas_call(
        functools.partial(product_kernel, n_y, n_z),
        out_shape=tuple(jax.ShapeDtypeStruct(shape, jnp.float32) for shape in shapes),
        in_specs=[array, array, array],
        out_specs=tuple(array for _ in shapes),
        scratch_shapes=[
            pltpu.VMEM((OB, m), jnp.bfloat16),
            pltpu.VMEM((n_y, OB, OB), jnp.float32),
            pltpu.VMEM((n_y, OB, KB), jnp.float32),
        ],
        compiler_params=pltpu.CompilerParams(vmem_limit_bytes=24 * 1024 * 1024),
        name="products",
    )(other, square, side)


def expand(packed, level, n_z):
    array = pl.BlockSpec(memory_space=pltpu.VMEM)
    return pl.pallas_call(
        functools.partial(expand_kernel, n_z),
        out_shape=(
            jax.ShapeDtypeStruct((OB, OB), jnp.float32),
            jax.ShapeDtypeStruct((HEAD + OB // PAIR, OB), jnp.float32),
        ),
        in_specs=[array, array],
        out_specs=(array, array),
        compiler_params=pltpu.CompilerParams(vmem_limit_bytes=8 * 1024 * 1024),
        name="expand",
    )(packed, level)


def panel_products(mine, other, level, n_y):
    array = pl.BlockSpec(memory_space=pltpu.VMEM)
    return pl.pallas_call(
        functools.partial(panel_kernel, n_y),
        out_shape=jax.ShapeDtypeStruct((n_y, HEAD + P_SIZE // 2 + BLOCK, P_SIZE), jnp.float32),
        in_specs=[array, array, array],
        out_specs=array,
        cost_estimate=pl.CostEstimate(
            flops=4 * n_y * P_SIZE * OB * mine.shape[1], bytes_accessed=0, transcendentals=0
        ),
        compiler_params=pltpu.CompilerParams(vmem_limit_bytes=8 * 1024 * 1024),
        name="panel_products",
    )(mine, other, level)


def factor_group(rows, base):
    sub = lax.broadcasted_iota(jnp.int32, (BLOCK, LANES), 0)
    count = len(rows)
    for q in range(count):
        at = base + BLOCK * q
        factors = [
            [
                jnp.broadcast_to(rows[r][:, at + j : at + j + 1], (BLOCK, LANES))
                for j in range(BLOCK)
            ]
            for r in range(q, count)
        ]
        columns, own = factors[0], rows[q]
        scales, entries = [], []
        for i in range(BLOCK):
            pivot = row_of(columns[i], i)
            scale = lax.rsqrt(pivot)
            scale = scale * (1.5 - 0.5 * pivot * scale * scale)
            scales.append(scale)
            scaled = row_of(own, i) * scale
            step = columns[i] * scale
            own = jnp.where(sub == i, scaled, jnp.where(sub > i, own - step * scaled, own))
            entries.append([row_of(columns[j], i) * scale for j in range(BLOCK)])
            for j in range(i + 1, BLOCK):
                columns[j] = columns[j] - step * entries[i][j]
        rows[q] = own
        for r in range(q + 1, count):
            value = rows[r]
            below = list(factors[r - q])
            for i in range(BLOCK):
                step = below[i] * scales[i]
                value = value - step * row_of(own, i)
                for j in range(i + 1, BLOCK):
                    below[j] = below[j] - step * entries[i][j]
            rows[r] = value
    return rows


def factor_kernel(panel_ref, prior_ref, out_ref, work_ref):
    n = work_ref.shape[0]
    depth = BLOCK * FACTOR_GROUP
    row = lax.broadcasted_iota(jnp.int32, (n, n), 0)
    column = lax.broadcasted_iota(jnp.int32, (n, n), 1)
    prior = jnp.broadcast_to(prior_ref[...], (n, n))
    half = n // 2
    packed, spare = panel_ref[:half, :], panel_ref[half : half + 1, :]
    diagonal = column[:half] - half == row[:half]
    whole = jnp.concatenate(
        [pltpu.roll(packed, half, 1), jnp.where(diagonal, spare, packed)], axis=0
    )
    known = ((row < half) & (column < half) & (row >= column)) | (
        (row >= half) & ((column < half) | (row <= column))
    )
    whole = jnp.where(known, whole, whole.T)
    work_ref[...] = whole + jnp.where(row == column, prior, 0.0)
    for p in range(n // depth):
        base = p * depth
        rows = [
            work_ref[base + BLOCK * r : base + BLOCK * (r + 1), :] for r in range(FACTOR_GROUP)
        ]
        done = jnp.concatenate(factor_group(rows, base), axis=0)
        work_ref[base : base + depth, :] = done
        if base + depth < n:
            d0, d1, d2 = split3(done)
            update = mm(
                jnp.concatenate([d0, d0, d0, d1, d1, d2], axis=0),
                jnp.concatenate([d0, d1, d2, d0, d1, d0], axis=0),
                COLS,
            )
            work_ref[base + depth :, :] = work_ref[base + depth :, :] - update[base + depth :, :]
    out_ref[...] = jnp.where(row <= column, work_ref[...], 0.0).T


def factor_panel(panel, prior):
    n = panel.shape[1]
    return pl.pallas_call(
        factor_kernel,
        out_shape=jax.ShapeDtypeStruct((n, n), jnp.float32),
        scratch_shapes=[pltpu.VMEM((n, n), jnp.float32)],
        cost_estimate=pl.CostEstimate(flops=n**3, bytes_accessed=12 * n * n, transcendentals=n),
        compiler_params=pltpu.CompilerParams(vmem_limit_bytes=8 * 1024 * 1024),
        name="factor_panel",
    )(panel, prior)


def level_of(message):
    return message[:1].astype(jnp.float32)


def values_of(message):
    return message[HEAD:].astype(jnp.float32) * jnp.exp2(level_of(message) - TOP_LEVEL)


def message_of(values, level):
    head = jnp.broadcast_to(level, (HEAD, values.shape[1]))
    return jnp.concatenate([head, values * jnp.exp2(TOP_LEVEL - level)]).astype(jnp.float16)


def pairwise(terms):
    while len(terms) > 1:
        terms = [terms[2 * i] + terms[2 * i + 1] for i in range(len(terms) // 2)]
    return terms[0]


def per_device(
    local_design, global_design, local_prior, obs_count, band_mask, owner_columns, kaula_prior
):
    n_arc, n_coef = lax.axis_size("arc"), lax.axis_size("coef")
    n_z, n_y = n_arc // PAIR, n_coef // PAIR
    rows = OB // n_arc
    def swap(values, dz=0, dx=0, dy=0, dk=0):
        pairs = []
        for a in range(n_arc):
            for c in range(n_coef):
                to_a = ((a // PAIR) ^ dz) * PAIR + ((a % PAIR) ^ dx)
                to_c = ((c // PAIR) ^ dy) * PAIR + ((c % PAIR) ^ dk)
                pairs.append((a * n_coef + c, to_a * n_coef + to_c))
        return lax.ppermute(values, AXES, pairs)

    local_rows, begun = begin_normal(obs_count, local_prior, local_design[0])
    send, own, gain = reduce_rows(
        obs_count,
        band_mask,
        owner_columns.reshape(n_coef, OB // LANES, LANES),
        local_rows,
        begun,
        global_design[0],
        n_y,
    )
    other = swap(send, dk=1)
    mine, square, side = own_products(own, send, gain, local_rows, n_y, n_z)
    keep_y, send_y, keep_x, send_x, level = products(other, square, side, n_y, n_z)
    half = OB // PAIR
    grown = float(n_y.bit_length() - 1)

    from_y = [swap(send_y[j - 1].astype(jnp.float16), dy=j) for j in range(1, n_y)]
    from_x = swap(send_x.astype(jnp.float16), dx=1)
    panels = panel_products(mine, other, level, n_y).astype(jnp.float16)
    panel_z = [panels] + [swap(panels, dz=j) for j in range(1, n_z)]

    from_y, from_x = lax.optimization_barrier((from_y, from_x))
    packed = functools.reduce(jnp.add, [values_of(message) for message in from_y], keep_y)
    left_level = functools.reduce(
        jnp.maximum, [level_of(message) for message in from_y], level[:1, :LANES]
    ) + grown
    left_level = jnp.concatenate([left_level] * (OB // LANES), axis=1)
    left, over_x = expand(packed, left_level, n_z)
    right = keep_x + values_of(from_x).reshape(n_y, half, KB)
    right_level = jnp.maximum(level[:1, :KB], level_of(from_x)) + 1.0

    over_x = over_x.astype(jnp.float16)
    over_y = [message_of(right[j], right_level) for j in range(1, n_y)]
    over_x, over_y = lax.optimization_barrier((over_x, over_y))
    panel_z, _ = lax.optimization_barrier((panel_z, (over_x, over_y)))
    from_x = swap(over_x, dx=1)
    from_y = [swap(over_y[j - 1], dy=j) for j in range(1, n_y)]
    from_x, from_y = lax.optimization_barrier((from_x, from_y))
    panel_level = functools.reduce(jnp.maximum, [level_of(p[0]) for p in panel_z])
    panel_level = panel_level + float(n_z.bit_length() - 1)
    panels = [
        message_of(pairwise([values_of(message[j]) for message in panel_z]), panel_level)
        for j in range(n_y)
    ]
    panel_y = [panels[0]] + [swap(panels[j], dy=j) for j in range(1, n_y)]
    panel_x = [swap(panels[j], dx=1, dy=j) for j in range(n_y)]
    left = left[:half] + values_of(from_x)
    left_level = jnp.maximum(left_level, level_of(from_x)) + 1.0
    right = functools.reduce(jnp.add, [values_of(message) for message in from_y], right[0])
    right_level = functools.reduce(
        jnp.maximum, [level_of(message) for message in from_y], right_level
    ) + grown

    total = jnp.concatenate([left, right], axis=1)
    level = jnp.concatenate([left_level, right_level], axis=1)
    over_z = [message_of(total[j * rows : (j + 1) * rows], level) for j in range(1, n_z)]
    over_z = lax.optimization_barrier(over_z)
    from_z = [swap(over_z[j - 1], dz=j) for j in range(1, n_z)]
    *from_z, from_near = from_z[1:] + from_z[:1]
    panel_x, panel_y, _ = lax.optimization_barrier((panel_x, panel_y, over_z))
    panel = functools.reduce(jnp.add, [values_of(message) for message in panel_y])
    panel = panel + functools.reduce(jnp.add, [values_of(message) for message in panel_x])
    panel_factor = factor_panel(panel, kaula_prior)
    from_z, panel_factor = lax.optimization_barrier((from_z + [from_near], panel_factor))
    normal_rows = functools.reduce(
        jnp.add, [values_of(message) for message in from_z], total[:rows]
    )
    return normal_rows[None], panel_factor[None]


def solution(mesh):
    in_specs = (
        P(AXES, None, None),
        P(AXES, None, None),
        P(AXES, None),
        P(AXES),
        P(AXES, None),
        P(),
        P("coef", None),
    )
    out_specs = (P("coef", "arc", None), P("coef", None, None))
    return jax.shard_map(
        per_device, mesh=mesh, in_specs=in_specs, out_specs=out_specs, check_vma=False
    )
```

```python
import functools

import jax
import jax.numpy as jnp
from jax import lax
from jax.experimental import pallas as pl
from jax.experimental.pallas import tpu as pltpu
from jax.sharding import PartitionSpec as P

OB = 512
KB = 256
P_SIZE = 128
STRIDE = OB // P_SIZE
WIDTH = OB + KB
PAIR = 2
TOP_LEVEL = 12.0
HEAD = 8
INNER = (((1,), (1,)), ((), ()))
AXES = ("arc", "coef")

LANES = 128
BLOCK = 8
GROUP = 2
FACTOR_GROUP = 4
FIRST = 3
TILE = 128
ROWS = (((1,), (0,)), ((), ()))
COLS = (((0,), (0,)), ((), ()))


def mm(a, b, dims=ROWS):
    return lax.dot_general(a, b, dims, preferred_element_type=jnp.float32)


def split3(value):
    high = value.astype(jnp.bfloat16)
    rest = value - high.astype(jnp.float32)
    middle = rest.astype(jnp.bfloat16)
    low = (rest - middle.astype(jnp.float32)).astype(jnp.bfloat16)
    return high, middle, low


def row_of(value, i):
    return jnp.broadcast_to(value[i : i + 1, :], (BLOCK, LANES))


def eliminate_group(rows, base, extra):
    sub = lax.broadcasted_iota(jnp.int32, (BLOCK, LANES), 0)
    lane = lax.broadcasted_iota(jnp.int32, (BLOCK, LANES), 1)
    count = len(rows)
    rows = rows + extra
    for q in range(count):
        half, at = divmod(base + BLOCK * q, LANES)
        factors = [
            [
                jnp.broadcast_to(row[half][:, at + j : at + j + 1], (BLOCK, LANES))
                for j in range(BLOCK)
            ]
            for row in rows
        ]
        inside = (lane >= at) & (lane < at + BLOCK)
        unit = (lane - at == sub).astype(jnp.float32)
        for r in range(len(rows)):
            rows[r][half] = jnp.where(inside, unit if r == q else 0.0, rows[r][half])
        columns, own = list(factors[q]), rows[q]
        a, b, d = row_of(columns[0], 0), row_of(columns[1], 0), row_of(columns[1], 1)
        for i in range(0, BLOCK, 2):
            scale = pl.reciprocal(a * d - b * b, approx=True)

            def step(value, i=i, a=a, b=b, d=d, scale=scale):
                first, second = row_of(value, i), row_of(value, i + 1)
                upper, lower = d * first - b * second, a * second - b * first
                new = value - (columns[i] * upper + columns[i + 1] * lower) * scale
                kept = jnp.where(sub == i + 1, lower * scale, new)
                return new, jnp.where(sub == i, upper * scale, kept)

            pairs = {j: step(columns[j]) for j in range(i + 2, BLOCK)}
            for h in range(len(own)):
                own[h] = step(own[h])[1]
            if i + 2 < BLOCK:
                one, two = pairs[i + 2][0], pairs[i + 3][0]
                a, b, d = row_of(one, i + 2), row_of(two, i + 2), row_of(two, i + 3)
            for j, pair in pairs.items():
                columns[j] = pair[1]
        for r in range(len(rows)):
            if r != q:
                for h in range(len(own)):
                    t = [factors[r][j] * row_of(own[h], j) for j in range(BLOCK)]
                    rows[r][h] = rows[r][h] - (
                        ((t[0] + t[1]) + (t[2] + t[3])) + ((t[4] + t[5]) + (t[6] + t[7]))
                    )
    return rows


def sweep_group(a_ref, base):
    n = a_ref.shape[0]
    depth = BLOCK * GROUP
    before = a_ref[base : base + depth, :]

    def blocks(start):
        return [
            [
                a_ref[start + BLOCK * r : start + BLOCK * (r + 1), LANES * h : LANES * (h + 1)]
                for h in range(n // LANES)
            ]
            for r in range(GROUP)
        ]

    def joined(rows):
        return jnp.concatenate([jnp.concatenate(row, axis=1) for row in rows], axis=0)

    after = base + depth
    ahead = after < n
    rows = eliminate_group(blocks(base), base, blocks(after) if ahead else [])
    following, after_rows = joined(rows[GROUP:]) if ahead else None, joined(rows[:GROUP])
    column = lax.broadcasted_iota(jnp.int32, (depth, n), 1)
    row = lax.broadcasted_iota(jnp.int32, (depth, n), 0)
    inside = (column >= base) & (column < base + depth)
    if following is not None:
        a_ref[after : after + depth, :] = jnp.where(inside, -following, following)
    before = jnp.where(inside, jnp.where(column - base == row, -1.0, 0.0), before)
    after_rows = jnp.where(inside, -after_rows, after_rows)
    u0, u1, u2 = split3(before)
    w0, w1, w2 = split3(after_rows)
    left = jnp.concatenate([u0, u0, u0, u1, u1, u2], axis=0).T
    right = jnp.concatenate([w0, w1, w2, w0, w1, w0], axis=0)

    def update(low, high):
        row = lax.broadcasted_iota(jnp.int32, (high - low, n), 0) + low
        column = lax.broadcasted_iota(jnp.int32, (high - low, n), 1)
        outside = ((row < base) | (row >= base + depth)) & (
            (column < base) | (column >= base + depth)
        )
        a_ref[low:high, :] = jnp.where(outside, a_ref[low:high, :], 0.0) - mm(left[low:high], right)

    for low, high in ((after + depth, n), (0, after)):
        if low < high:
            update(low, high)


def place_of():
    arc, coef = lax.axis_index("arc"), lax.axis_index("coef")
    return lax.div(arc, PAIR), lax.rem(arc, PAIR), lax.div(coef, PAIR), lax.rem(coef, PAIR)


def solve_rows(tile, gain_ref, local_rows):
    solved = (mm(tile, gain_ref[1], INNER) + mm(tile, gain_ref[0], INNER)).astype(jnp.bfloat16)
    return (tile.astype(jnp.float32) - mm(solved, local_rows)).astype(jnp.bfloat16)


def normal_kernel(count_ref, local_ref, rows_ref, normal_ref):
    n, m = local_ref.shape
    used = lax.broadcasted_iota(jnp.int32, (n, m), 1) < count_ref[0]
    rows_ref[...] = jnp.where(used, local_ref[...].astype(jnp.float32), 0.0).astype(jnp.bfloat16)
    normal_ref[...] = mm(rows_ref[...], rows_ref[...], INNER)


def sweep_kernel(prior_ref, normal_ref, work_ref):
    n = normal_ref.shape[0]
    row = lax.broadcasted_iota(jnp.int32, (n, n), 0)
    column = lax.broadcasted_iota(jnp.int32, (n, n), 1)
    prior = jnp.broadcast_to(prior_ref[...], (n, n))
    work_ref[...] = normal_ref[...] + jnp.where(row == column, prior, 0.0)
    for p in range(FIRST):
        sweep_group(work_ref, p * BLOCK * GROUP)


def local_kernel(
    n_y, count_ref, band_ref, owner_ref, rows_ref, begun_ref, global_ref,
    send_ref, own_ref, gain_ref, work_ref,
):
    n, m = rows_ref.shape
    owned = n_y * PAIR * OB
    mine = n_y * OB
    count = count_ref[0]
    _, _, y, core = place_of()
    work_ref[...] = begun_ref[...]
    lane = lax.broadcasted_iota(jnp.int32, (TILE, LANES), 1).astype(jnp.int16)
    used = lax.broadcasted_iota(jnp.int32, (TILE, m), 1) < count

    def gather_rows(t):
        position, part = divmod(t * TILE, OB)
        core_away, y_away = divmod(position, n_y)
        owner = (y ^ y_away) * PAIR + (core ^ core_away)
        wanted = []
        for r in range(TILE // LANES):
            at = part // LANES + r
            ids = owner_ref[owner, at : at + 1, :].astype(jnp.float32)
            ids = jnp.broadcast_to(ids, (LANES, LANES)).T
            wanted.append(ids.astype(jnp.int32).astype(jnp.int16))
        wanted = jnp.concatenate(wanted, axis=0)
        hot, nothing = [], jnp.zeros((TILE, LANES), jnp.bfloat16)
        for k in range(owned // LANES):
            sensed = band_ref[0, k * LANES // OB].astype(jnp.float32).astype(jnp.bfloat16)
            sensed = jnp.full((TILE, LANES), sensed)
            hot.append(jnp.where(wanted == lane + jnp.int16(k * LANES), sensed, nothing))
        got = mm(jnp.concatenate(hot, axis=1), global_ref[0:owned, :])
        got = jnp.where(used, got, 0.0).astype(jnp.bfloat16)
        if t * TILE < mine:
            own_ref[t * TILE : (t + 1) * TILE, :] = got
        else:
            send_ref[t * TILE - mine : (t + 1) * TILE - mine, :] = got

    steps = n // (BLOCK * GROUP) - FIRST
    tiles, fill = owned // TILE, steps - 2
    for p in range(steps):
        sweep_group(work_ref, (FIRST + p) * BLOCK * GROUP)
        for t in range(p * tiles // fill, min(tiles, (p + 1) * tiles // fill)):
            gather_rows(t)
    used = lax.broadcasted_iota(jnp.int32, (KB, m), 1) < count
    border = global_ref[owned:, :].astype(jnp.float32)
    send_ref[mine:, :] = jnp.where(used, border, 0.0).astype(jnp.bfloat16)

    local_rows = rows_ref[...]
    i0, i1, i2 = split3(-work_ref[...])
    gain = mm(i2, local_rows) + mm(i1, local_rows) + mm(i0, local_rows)
    for i, part in enumerate(split3(gain)[:2]):
        gain_ref[i] = part
    send_ref[...] = solve_rows(send_ref[...], gain_ref, local_rows)


def begin_normal(count, prior, local_rows):
    n, m = local_rows.shape
    array = pl.BlockSpec(memory_space=pltpu.VMEM)
    rows, normal = pl.pallas_call(
        normal_kernel,
        out_shape=(
            jax.ShapeDtypeStruct((n, m), jnp.bfloat16),
            jax.ShapeDtypeStruct((n, n), jnp.float32),
        ),
        in_specs=[pl.BlockSpec(memory_space=pltpu.SMEM), array],
        out_specs=(array, array),
        compiler_params=pltpu.CompilerParams(vmem_limit_bytes=16 * 1024 * 1024),
        cost_estimate=pl.CostEstimate(flops=10**9, bytes_accessed=0, transcendentals=0),
        name="normal",
    )(count, local_rows)
    begun = pl.pallas_call(
        sweep_kernel,
        out_shape=jax.ShapeDtypeStruct((n, n), jnp.float32),
        in_specs=[array, array],
        out_specs=array,
        compiler_params=pltpu.CompilerParams(vmem_limit_bytes=16 * 1024 * 1024),
        cost_estimate=pl.CostEstimate(flops=4 * 10**9, bytes_accessed=0, transcendentals=0),
        name="first_sweeps",
    )(prior, normal)
    return rows, begun


def reduce_rows(count, band, owners, rows, begun, global_rows, n_y):
    n, m = rows.shape
    scalar = pl.BlockSpec(memory_space=pltpu.SMEM)
    array = pl.BlockSpec(memory_space=pltpu.VMEM)
    shapes = ((n_y * OB + KB, m), (n_y * OB, m), (2, n, m))
    return pl.pallas_call(
        functools.partial(local_kernel, n_y),
        out_shape=tuple(jax.ShapeDtypeStruct(shape, jnp.bfloat16) for shape in shapes),
        in_specs=[scalar, scalar, array, array, array, array],
        out_specs=tuple(array for _ in shapes),
        scratch_shapes=[pltpu.VMEM((n, n), jnp.float32)],
        compiler_params=pltpu.CompilerParams(vmem_limit_bytes=24 * 1024 * 1024),
        name="reduce_rows",
    )(count, band, owners, rows, begun, global_rows)


def own_product_kernel(
    n_y, n_z, own_ref, send_ref, gain_ref, rows_ref, mine_ref, square_ref, side_ref, left
):
    z, x, _, _ = place_of()
    border = send_ref[n_y * OB :, :]
    local_rows = rows_ref[...]
    for t in range(n_y):
        tile = own_ref[t * OB : (t + 1) * OB, :]
        mine_ref[t * OB : (t + 1) * OB, :] = solve_rows(tile, gain_ref, local_rows)
    for y in range(n_y):
        for g in range(OB // LANES):
            low, high = g * LANES, (g + 1) * LANES
            rows = mine_ref[y * OB + low : y * OB + high, :]
            square_ref[y, low:high, :high] = mm(rows, mine_ref[y * OB : y * OB + high, :], INNER)
        order_rows(n_z, z, x, mine_ref, y, left)
        side_ref[y] = mm(left[...], border, INNER)


def order_rows(n_z, z, x, rows_ref, y, left):
    rows = OB // (n_z * PAIR)
    for i in range(PAIR):
        for j in range(n_z):
            at = (i * n_z + j) * rows
            source = pl.multiple_of(y * OB + ((z ^ j) * PAIR + (x ^ i)) * rows, rows)
            left[at : at + rows, :] = rows_ref[pl.ds(source, rows), :]


def lower_blocks():
    return [(g, t) for g in range(OB // LANES) for t in range(g + 1)]


def product_kernel(
    n_y, n_z, other_ref, square_ref, side_ref,
    keep_y_ref, send_y_ref, keep_x_ref, send_x_ref, level_ref, left, square, side,
):
    z, x, _, _ = place_of()
    half = OB // PAIR
    border = other_ref[n_y * OB :, :]
    top = jnp.zeros((BLOCK, LANES), jnp.float32)

    def raised(top, value):
        count = value.shape[0]
        value = jnp.abs(value).reshape(count // BLOCK, BLOCK, LANES)
        return jnp.maximum(top, jnp.max(value, axis=0))

    for y in range(n_y):
        for g in range(OB // LANES):
            low, high = g * LANES, (g + 1) * LANES
            rows = other_ref[y * OB + low : y * OB + high, :]
            square[y, low:high, :high] = square_ref[y, low:high, :high] + mm(
                rows, other_ref[y * OB : y * OB + high, :], INNER
            )
            for t in range(g + 1):
                top = raised(top, square[y, low:high, t * LANES : (t + 1) * LANES])
        order_rows(n_z, z, x, other_ref, y, left)
        side[y] = side_ref[y] + mm(left[...], border, INNER)
        for h in range(KB // LANES):
            top = raised(top, side[y, :, h * LANES : (h + 1) * LANES])
    top = jnp.max(jnp.max(top, axis=0, keepdims=True), axis=1, keepdims=True)
    level = jnp.floor(jnp.log2(jnp.maximum(jnp.broadcast_to(top, (BLOCK, OB)), 1e-30)))
    level_ref[...] = level
    scale = jnp.exp2(TOP_LEVEL - level[:1, :KB])
    for j in range(1, n_y):
        send_y_ref[j - 1, :HEAD, :] = jnp.broadcast_to(level[:1, :LANES], (HEAD, LANES))
    for i, (g, t) in enumerate(lower_blocks()):
        rows, columns = slice(g * LANES, (g + 1) * LANES), slice(t * LANES, (t + 1) * LANES)
        keep_y_ref[i * LANES : (i + 1) * LANES, :] = square[0, rows, columns]
        for j in range(1, n_y):
            at = HEAD + i * LANES
            send_y_ref[j - 1, at : at + LANES, :] = square[j, rows, columns] * scale[:, :LANES]
    send_x_ref[:HEAD, :] = jnp.broadcast_to(level[:1, :KB], (HEAD, KB))
    for y in range(n_y):
        keep_x_ref[y] = side[y, :half, :]
        at = HEAD + y * half
        send_x_ref[at : at + half, :] = side[y, half:, :] * scale


def expand_kernel(n_z, packed_ref, level_ref, out_ref, send_ref):
    z, x, _, _ = place_of()
    rows = OB // (n_z * PAIR)
    place = {pair: i for i, pair in enumerate(lower_blocks())}
    for g in range(OB // LANES):
        for t in range(OB // LANES):
            at = place[max(g, t), min(g, t)] * LANES
            block = packed_ref[at : at + LANES, :]
            block = block if t <= g else block.T
            for b in range(LANES // rows):
                arc = g * (LANES // rows) + b
                to = (((arc % PAIR) ^ x) * n_z + ((arc // PAIR) ^ z)) * rows
                to = pl.multiple_of(to, rows)
                out_ref[pl.ds(to, rows), t * LANES : (t + 1) * LANES] = block[
                    b * rows : (b + 1) * rows, :
                ]
    level = level_ref[:1, :]
    send_ref[:HEAD, :] = jnp.broadcast_to(level, (HEAD, OB))
    send_ref[HEAD:, :] = out_ref[OB // PAIR :, :] * jnp.exp2(TOP_LEVEL - level)


def panel_kernel(n_y, mine_ref, other_ref, level_ref, out_ref):
    pick = lax.broadcasted_iota(jnp.int32, (P_SIZE, OB), 1) == STRIDE * lax.broadcasted_iota(
        jnp.int32, (P_SIZE, OB), 0
    )
    pick = pick.astype(jnp.float32).astype(jnp.bfloat16)
    level = level_ref[:1, :P_SIZE]
    scale = jnp.exp2(TOP_LEVEL - level)
    half = P_SIZE // 2
    row = lax.broadcasted_iota(jnp.int32, (half, P_SIZE), 0)
    column = lax.broadcasted_iota(jnp.int32, (half, P_SIZE), 1) - half
    for y in range(n_y):
        panel = jnp.zeros((P_SIZE, P_SIZE), jnp.float32)
        for ref in (mine_ref, other_ref):
            strip = mm(pick, ref[y * OB : (y + 1) * OB, :]).astype(jnp.bfloat16)
            panel = panel + mm(strip, strip, INNER)
        upper, lower = panel[:half], panel[half:]
        corner = jnp.where(row >= column, pltpu.roll(upper, half, 1), lower)
        spare = jnp.sum(jnp.where(row == column, lower, 0.0), axis=0, keepdims=True)
        out_ref[y, :HEAD, :] = jnp.broadcast_to(level, (HEAD, P_SIZE))
        out_ref[y, HEAD : HEAD + half, :] = jnp.where(column < 0, lower, corner) * scale
        out_ref[y, HEAD + half :, :] = jnp.broadcast_to(spare * scale, (BLOCK, P_SIZE))


def own_products(own, send, gain, rows, n_y, n_z):
    array = pl.BlockSpec(memory_space=pltpu.VMEM)
    m = own.shape[1]
    return pl.pallas_call(
        functools.partial(own_product_kernel, n_y, n_z),
        out_shape=(
            jax.ShapeDtypeStruct(own.shape, jnp.bfloat16),
            jax.ShapeDtypeStruct((n_y, OB, OB), jnp.float32),
            jax.ShapeDtypeStruct((n_y, OB, KB), jnp.float32),
        ),
        in_specs=[array, array, array, array],
        out_specs=(array, array, array),
        scratch_shapes=[pltpu.VMEM((OB, m), jnp.bfloat16)],
        compiler_params=pltpu.CompilerParams(vmem_limit_bytes=24 * 1024 * 1024),
        cost_estimate=pl.CostEstimate(
            flops=4 * n_y * OB * WIDTH * m, bytes_accessed=0, transcendentals=0
        ),
        name="own_products",
    )(own, send, gain, rows)


def products(other, square, side, n_y, n_z):
    array = pl.BlockSpec(memory_space=pltpu.VMEM)
    m = other.shape[1]
    half, packed = OB // PAIR, len(lower_blocks()) * LANES
    shapes = (
        (packed, LANES),
        (n_y - 1, HEAD + packed, LANES),
        (n_y, half, KB),
        (HEAD + n_y * half, KB),
        (BLOCK, OB),
    )
    return pl.pallas_call(
        functools.partial(product_kernel, n_y, n_z),
        out_shape=tuple(jax.ShapeDtypeStruct(shape, jnp.float32) for shape in shapes),
        in_specs=[array, array, array],
        out_specs=tuple(array for _ in shapes),
        scratch_shapes=[
            pltpu.VMEM((OB, m), jnp.bfloat16),
            pltpu.VMEM((n_y, OB, OB), jnp.float32),
            pltpu.VMEM((n_y, OB, KB), jnp.float32),
        ],
        compiler_params=pltpu.CompilerParams(vmem_limit_bytes=24 * 1024 * 1024),
        name="products",
    )(other, square, side)


def expand(packed, level, n_z):
    array = pl.BlockSpec(memory_space=pltpu.VMEM)
    return pl.pallas_call(
        functools.partial(expand_kernel, n_z),
        out_shape=(
            jax.ShapeDtypeStruct((OB, OB), jnp.float32),
            jax.ShapeDtypeStruct((HEAD + OB // PAIR, OB), jnp.float32),
        ),
        in_specs=[array, array],
        out_specs=(array, array),
        compiler_params=pltpu.CompilerParams(vmem_limit_bytes=8 * 1024 * 1024),
        name="expand",
    )(packed, level)


def panel_products(mine, other, level, n_y):
    array = pl.BlockSpec(memory_space=pltpu.VMEM)
    return pl.pallas_call(
        functools.partial(panel_kernel, n_y),
        out_shape=jax.ShapeDtypeStruct((n_y, HEAD + P_SIZE // 2 + BLOCK, P_SIZE), jnp.float32),
        in_specs=[array, array, array],
        out_specs=array,
        cost_estimate=pl.CostEstimate(
            flops=4 * n_y * P_SIZE * OB * mine.shape[1], bytes_accessed=0, transcendentals=0
        ),
        compiler_params=pltpu.CompilerParams(vmem_limit_bytes=8 * 1024 * 1024),
        name="panel_products",
    )(mine, other, level)


def factor_group(rows, base):
    sub = lax.broadcasted_iota(jnp.int32, (BLOCK, LANES), 0)
    count = len(rows)
    for q in range(count):
        at = base + BLOCK * q
        factors = [
            [
                jnp.broadcast_to(rows[r][:, at + j : at + j + 1], (BLOCK, LANES))
                for j in range(BLOCK)
            ]
            for r in range(q, count)
        ]
        columns, own = factors[0], rows[q]
        scales, entries = [], []
        for i in range(BLOCK):
            pivot = row_of(columns[i], i)
            scale = lax.rsqrt(pivot)
            scale = scale * (1.5 - 0.5 * pivot * scale * scale)
            scales.append(scale)
            scaled = row_of(own, i) * scale
            step = columns[i] * scale
            own = jnp.where(sub == i, scaled, jnp.where(sub > i, own - step * scaled, own))
            entries.append([row_of(columns[j], i) * scale for j in range(BLOCK)])
            for j in range(i + 1, BLOCK):
                columns[j] = columns[j] - step * entries[i][j]
        rows[q] = own
        for r in range(q + 1, count):
            value = rows[r]
            below = list(factors[r - q])
            for i in range(BLOCK):
                step = below[i] * scales[i]
                value = value - step * row_of(own, i)
                for j in range(i + 1, BLOCK):
                    below[j] = below[j] - step * entries[i][j]
            rows[r] = value
    return rows


def factor_kernel(panel_ref, prior_ref, out_ref, work_ref):
    n = work_ref.shape[0]
    depth = BLOCK * FACTOR_GROUP
    row = lax.broadcasted_iota(jnp.int32, (n, n), 0)
    column = lax.broadcasted_iota(jnp.int32, (n, n), 1)
    prior = jnp.broadcast_to(prior_ref[...], (n, n))
    half = n // 2
    packed, spare = panel_ref[:half, :], panel_ref[half : half + 1, :]
    diagonal = column[:half] - half == row[:half]
    whole = jnp.concatenate(
        [pltpu.roll(packed, half, 1), jnp.where(diagonal, spare, packed)], axis=0
    )
    known = ((row < half) & (column < half) & (row >= column)) | (
        (row >= half) & ((column < half) | (row <= column))
    )
    whole = jnp.where(known, whole, whole.T)
    work_ref[...] = whole + jnp.where(row == column, prior, 0.0)
    for p in range(n // depth):
        base = p * depth
        rows = [
            work_ref[base + BLOCK * r : base + BLOCK * (r + 1), :] for r in range(FACTOR_GROUP)
        ]
        done = jnp.concatenate(factor_group(rows, base), axis=0)
        work_ref[base : base + depth, :] = done
        if base + depth < n:
            d0, d1, d2 = split3(done)
            update = mm(
                jnp.concatenate([d0, d0, d0, d1, d1, d2], axis=0),
                jnp.concatenate([d0, d1, d2, d0, d1, d0], axis=0),
                COLS,
            )
            work_ref[base + depth :, :] = work_ref[base + depth :, :] - update[base + depth :, :]
    out_ref[...] = jnp.where(row <= column, work_ref[...], 0.0).T


def factor_panel(panel, prior):
    n = panel.shape[1]
    return pl.pallas_call(
        factor_kernel,
        out_shape=jax.ShapeDtypeStruct((n, n), jnp.float32),
        scratch_shapes=[pltpu.VMEM((n, n), jnp.float32)],
        cost_estimate=pl.CostEstimate(flops=n**3, bytes_accessed=12 * n * n, transcendentals=n),
        compiler_params=pltpu.CompilerParams(vmem_limit_bytes=8 * 1024 * 1024),
        name="factor_panel",
    )(panel, prior)


def level_of(message):
    return message[:1].astype(jnp.float32)


def values_of(message):
    return message[HEAD:].astype(jnp.float32) * jnp.exp2(level_of(message) - TOP_LEVEL)


def message_of(values, level):
    head = jnp.broadcast_to(level, (HEAD, values.shape[1]))
    return jnp.concatenate([head, values * jnp.exp2(TOP_LEVEL - level)]).astype(jnp.float16)


def pairwise(terms):
    while len(terms) > 1:
        terms = [terms[2 * i] + terms[2 * i + 1] for i in range(len(terms) // 2)]
    return terms[0]


def per_device(
    local_design, global_design, local_prior, obs_count, band_mask, owner_columns, kaula_prior
):
    n_arc, n_coef = lax.axis_size("arc"), lax.axis_size("coef")
    n_z, n_y = n_arc // PAIR, n_coef // PAIR
    rows = OB // n_arc
    def swap(values, dz=0, dx=0, dy=0, dk=0):
        pairs = []
        for a in range(n_arc):
            for c in range(n_coef):
                to_a = ((a // PAIR) ^ dz) * PAIR + ((a % PAIR) ^ dx)
                to_c = ((c // PAIR) ^ dy) * PAIR + ((c % PAIR) ^ dk)
                pairs.append((a * n_coef + c, to_a * n_coef + to_c))
        return lax.ppermute(values, AXES, pairs)

    local_rows, begun = begin_normal(obs_count, local_prior, local_design[0])
    send, own, gain = reduce_rows(
        obs_count,
        band_mask,
        owner_columns.reshape(n_coef, OB // LANES, LANES),
        local_rows,
        begun,
        global_design[0],
        n_y,
    )
    other = swap(send, dk=1)
    mine, square, side = own_products(own, send, gain, local_rows, n_y, n_z)
    keep_y, send_y, keep_x, send_x, level = products(other, square, side, n_y, n_z)
    half = OB // PAIR
    grown = float(n_y.bit_length() - 1)

    from_y = [swap(send_y[j - 1].astype(jnp.float16), dy=j) for j in range(1, n_y)]
    from_x = swap(send_x.astype(jnp.float16), dx=1)
    panels = panel_products(mine, other, level, n_y).astype(jnp.float16)
    panel_z = [panels] + [swap(panels, dz=j) for j in range(1, n_z)]

    from_y, from_x = lax.optimization_barrier((from_y, from_x))
    packed = functools.reduce(jnp.add, [values_of(message) for message in from_y], keep_y)
    left_level = functools.reduce(
        jnp.maximum, [level_of(message) for message in from_y], level[:1, :LANES]
    ) + grown
    left_level = jnp.concatenate([left_level] * (OB // LANES), axis=1)
    left, over_x = expand(packed, left_level, n_z)
    right = keep_x + values_of(from_x).reshape(n_y, half, KB)
    right_level = jnp.maximum(level[:1, :KB], level_of(from_x)) + 1.0

    over_x = over_x.astype(jnp.float16)
    over_y = [message_of(right[j], right_level) for j in range(1, n_y)]
    over_x, over_y = lax.optimization_barrier((over_x, over_y))
    panel_z, _ = lax.optimization_barrier((panel_z, (over_x, over_y)))
    from_x = swap(over_x, dx=1)
    from_y = [swap(over_y[j - 1], dy=j) for j in range(1, n_y)]
    from_x, from_y = lax.optimization_barrier((from_x, from_y))
    panel_level = functools.reduce(jnp.maximum, [level_of(p[0]) for p in panel_z])
    panel_level = panel_level + float(n_z.bit_length() - 1)
    panels = [
        message_of(pairwise([values_of(message[j]) for message in panel_z]), panel_level)
        for j in range(n_y)
    ]
    panel_y = [panels[0]] + [swap(panels[j], dy=j) for j in range(1, n_y)]
    panel_x = [swap(panels[j], dx=1, dy=j) for j in range(n_y)]
    left = left[:half] + values_of(from_x)
    left_level = jnp.maximum(left_level, level_of(from_x)) + 1.0
    right = functools.reduce(jnp.add, [values_of(message) for message in from_y], right[0])
    right_level = functools.reduce(
        jnp.maximum, [level_of(message) for message in from_y], right_level
    ) + grown

    total = jnp.concatenate([left, right], axis=1)
    level = jnp.concatenate([left_level, right_level], axis=1)
    over_z = [message_of(total[j * rows : (j + 1) * rows], level) for j in range(1, n_z)]
    over_z = lax.optimization_barrier(over_z)
    from_z = [swap(over_z[j - 1], dz=j) for j in range(1, n_z)]
    *from_z, from_near = from_z[1:] + from_z[:1]
    panel_x, panel_y, _ = lax.optimization_barrier((panel_x, panel_y, over_z))
    panel = functools.reduce(jnp.add, [values_of(message) for message in panel_y])
    panel = panel + functools.reduce(jnp.add, [values_of(message) for message in panel_x])
    panel_factor = factor_panel(panel, kaula_prior)
    from_z, panel_factor = lax.optimization_barrier((from_z + [from_near], panel_factor))
    normal_rows = functools.reduce(
        jnp.add, [values_of(message) for message in from_z], total[:rows]
    )
    return normal_rows[None], panel_factor[None]


def solution(mesh):
    in_specs = (
        P(AXES, None, None),
        P(AXES, None, None),
        P(AXES, None),
        P(AXES),
        P(AXES, None),
        P(),
        P("coef", None),
    )
    out_specs = (P("coef", "arc", None), P("coef", None, None))
    return jax.shard_map(
        per_device, mesh=mesh, in_specs=in_specs, out_specs=out_specs, check_vma=False
    )
```
